256 devices in a mesh: group: 32 (over z, y), tensor: 8 (over x, core).
Axes of the slice: x: 4, y: 4, z: 8, core: 2. Of those that a mesh axis runs over, the one named last changes fastest.
Arguments:
- hidden: bfloat16 [256, 8192], P(None, 'group'), may hold values from -6 to 6
- vision: bfloat16 [20480, 8192], P('group', 'tensor'), may hold values from -6 to 6
- attn_gain: float32 [8192], P('group'), may hold values from 0.1 to 1.9
- q_weight: bfloat16 [8192, 8192], P('group', 'tensor'), may hold values from -0.0625 to 0.0625
- k_weight: bfloat16 [8192, 1024], P('tensor'), may hold values from -0.0625 to 0.0625
- v_weight: bfloat16 [8192, 1024], P('tensor'), may hold values from -0.0625 to 0.0625
- q_gain: float32 [128], replicated, may hold values from 0.5 to 2
- k_gain: float32 [128], replicated, may hold values from 0.5 to 2
- o_weight: bfloat16 [8192, 8192], P('tensor', 'group'), may hold values from -0.0625 to 0.0625
- gate_logits: float32 [2], replicated, may hold values from 0.5 to 2
- mlp_gain: float32 [8192], P('group'), may hold values from 0.1 to 1.9
- gate_weight: bfloat16 [8192, 28672], P('group', 'tensor'), may hold values from -0.0625 to 0.0625
- up_weight: bfloat16 [8192, 28672], P('group', 'tensor'), may hold values from -0.0625 to 0.0625
- down_weight: bfloat16 [28672, 8192], P('tensor', 'group'), may hold values from -0.03125 to 0.03125
- image_tiles: int32 [32, 4], replicated, may hold values from 1 to 4, 10 in all within a row
- image_groups: int32 [128, 8], replicated, may hold values from 0 to 31, as said below
- image_requests: int32 [128, 8], replicated, may hold values from 0 to 3, as said below
Outputs:
- output: bfloat16 [256, 8192], P(None, 'group')
The draws below stay inside these ranges and needn't reach their ends.
Inputs may be any that keep to these rules, and one draw needn't show every extreme that they name: `image_tiles`: row e lists the tiles of the 4 images of encoder group e in order; each row sums to 10 and holds an image of 4 tiles. `image_groups`: row i names 8 different decoder groups that receive image i. Among the rows of one encoder group (rows e * 4 to e * 4 + 3) no decoder group is named more than 2 times, and some decoder group is named exactly 2 times by some encoder group; every decoder group is named by some image. image_requests[i, c] is the request, numbered within decoder group image_groups[i, c], that sees image i; a request may see no image at all.
All inputs are finite; a program needn't handle non-finite values.
Results may differ from the reference program's by a relative error of at most 0.008.
Values may be sent and summed in bfloat16 or wider, within the bound.
No kernel may reach another device: no remote copies, remote signals or barrier semaphores. Data moves between devices by JAX's collectives and lax.ppermute only.
A program may use at most 128 MiB of HBM per device.

```python
import math
import jax
import jax.numpy as jnp
import numpy as np
from jax import lax

D = 8192
HQ = 64
KVH = 8
HEAD = 128
FF = 28672
REQ_DEV = 4
STEPS = 2
TILE_TOK = 64
MAXT = 4
IMG_DEV = 4
TILE_DEV = 10
COPIES = 8
VROWS = 640
ROWS_ALL = 256
REQUESTS = 128
N_GROUP = 32


def route_table(key):
    block_keys = jax.random.split(jax.random.fold_in(key, 101), N_GROUP)
    shuffled = jax.vmap(lambda block_key: jax.random.permutation(block_key, N_GROUP))(block_keys).astype(jnp.int32)
    hot_pair = jax.random.randint(jax.random.fold_in(key, 102), (2,), 0, N_GROUP, dtype=jnp.int32)
    hot_pick = jax.random.randint(jax.random.fold_in(key, 103), (N_GROUP,), 0, 2, dtype=jnp.int32)
    hot_each = hot_pair[hot_pick]
    hot_column = ((IMG_DEV - 1) * COPIES - 1) % N_GROUP
    column_index = jnp.arange(N_GROUP, dtype=jnp.int32)
    hot_place = jnp.argmax((shuffled == hot_each[:, None]).astype(jnp.int32), axis=1).astype(jnp.int32)
    displaced = shuffled[:, hot_column]
    swapped = jnp.where(column_index[None, :] == hot_column, hot_each[:, None], jnp.where(column_index[None, :] == hot_place[:, None], displaced[:, None], shuffled))
    intersection = max(0, 1 - (IMG_DEV * COPIES - N_GROUP))
    encoder_block = jnp.arange(N_GROUP, dtype=jnp.int32)[:, None, None]
    image_slot = jnp.arange(IMG_DEV, dtype=jnp.int32)[None, :, None]
    copy_slot = jnp.arange(COPIES, dtype=jnp.int32)[None, None, :]
    later_block = (encoder_block > 0).astype(jnp.int32)
    last_image = (image_slot == IMG_DEV - 1).astype(jnp.int32)
    first_slot = image_slot * COPIES - intersection * later_block * last_image
    position = (first_slot + copy_slot) % N_GROUP
    routed = jnp.take_along_axis(swapped, position.reshape(N_GROUP, IMG_DEV * COPIES), axis=1)
    return routed.reshape(N_GROUP * IMG_DEV, COPIES).astype(jnp.int32)


def draw_image_groups(key, part):
    return route_table(key)


def draw_image_requests(key, part):
    routed = route_table(key)
    key = jax.random.fold_in(key, 5)
    dark_count = max(2, N_GROUP // 10)
    group_order = jax.random.permutation(jax.random.fold_in(key, 1), N_GROUP).astype(jnp.int32)
    group_range = jnp.arange(N_GROUP, dtype=jnp.int32)
    is_dark = jnp.any(group_order[:dark_count][None, :] == group_range[:, None], axis=1).astype(jnp.int32)
    dark_request = jax.random.randint(jax.random.fold_in(key, 2), (N_GROUP,), 0, REQ_DEV, dtype=jnp.int32)
    dark_flag = is_dark[routed]
    skipped_request = dark_request[routed]
    drawn = jax.random.randint(jax.random.fold_in(key, 3), routed.shape, 0, REQ_DEV - dark_flag, dtype=jnp.int32)
    return (drawn + dark_flag * (drawn >= skipped_request).astype(jnp.int32)).astype(jnp.int32)


def shard_levels(rng, dims, pieces, least, largest):
    def one(axis_at, parts):
        steps = jax.random.uniform(jax.random.fold_in(jax.random.fold_in(rng, 6), axis_at), (parts,), jnp.float32, least / len(pieces), largest / len(pieces))
        return jnp.repeat(jnp.exp(steps), dims[axis_at] // parts).reshape((-1,) + (1,) * (len(dims) - axis_at - 1))

    level = one(*pieces[0])
    for cut in pieces[1:]:
        level = level * one(*cut)
    return level


def profile(amount, total, bound, slope):
    weights = [(1 << 20) // math.isqrt(grade ** slope) + 1 for grade in range(2, amount + 1)]
    surplus, counts = total - bound - (amount - 1), [1] * (amount - 1)
    while surplus > 0:
        free = [i for i in range(amount - 1) if counts[i] < bound]
        whole, budget = sum([weights[i] for i in free]), surplus
        for i in free:
            more = min(bound - counts[i], max(1, budget * weights[i] // whole), surplus)
            counts[i] = counts[i] + more
            surplus = surplus - more
    return np.array([bound] + counts)


def uneven(rng, number_of, total, limit, slope):
    if number_of == 2:
        one = jax.random.randint(rng, (), max(1, total - limit), min(limit, total - 1) + 1)
        return jnp.stack([one, total - one])
    tallies = jnp.asarray(profile(number_of, total, limit, slope), jnp.int32)
    twos = (number_of - 1) // 2
    giver, receiver = tallies[1:1 + 2 * twos:2], tallies[2:2 + 2 * twos:2]
    slack = jnp.minimum(giver - 1, limit - receiver)
    moved = jax.random.randint(jax.random.fold_in(rng, 1), (twos,), 0, 1 << 20) % (slack + 1)
    tallies = tallies.at[1:1 + 2 * twos:2].set(giver - moved).at[2:2 + 2 * twos:2].set(receiver + moved)
    return tallies[jax.random.permutation(jax.random.fold_in(rng, 2), number_of)]


def centred(own_key, shape, spread, bound, shards=(), kind=jnp.bfloat16):
    level = shard_levels(own_key, shape, shards, -0.22, 0.18) if shards else 1.0
    result = jax.random.normal(own_key, shape, jnp.float32) * spread * level
    return jnp.minimum(jnp.maximum(result, -bound), bound).astype(kind)


def setup_inputs(seed: int = 0) -> dict:
    keys = jax.random.split(jax.random.key(seed), 18)
    return {
        "hidden": centred(keys[0], (ROWS_ALL, D), 1.0, 6.0, ((1, 32),)),
        "vision": centred(keys[1], (N_GROUP * VROWS, D), 1.0, 6.0, ((0, 32), (1, 8))),
        "attn_gain": jnp.clip(1.0 + 0.18 * jax.random.normal(keys[2], (D,), jnp.float32), 0.1, 1.9),
        "q_weight": centred(keys[3], (D, HQ * HEAD), D ** -0.5, 0.0625, ((0, 32), (1, 8))),
        "k_weight": centred(keys[4], (D, KVH * HEAD), D ** -0.5, 0.0625, ((0, 8),)),
        "v_weight": centred(keys[5], (D, KVH * HEAD), D ** -0.5, 0.0625, ((0, 8),)),
        "q_gain": jnp.clip(jnp.exp(jax.random.uniform(keys[6], (HEAD,), jnp.float32, math.log(0.5), math.log(2.0))), 0.5, 2.0),
        "k_gain": jnp.clip(jnp.exp(jax.random.uniform(keys[7], (HEAD,), jnp.float32, math.log(0.5), math.log(2.0))), 0.5, 2.0),
        "o_weight": centred(keys[8], (HQ * HEAD, D), (HQ * HEAD) ** -0.5, 0.0625, ((0, 8), (1, 32))),
        "gate_logits": jnp.clip(jax.random.uniform(keys[9], (2,), jnp.float32, 0.5, 2.0), 0.5, 2.0),
        "mlp_gain": jnp.clip(1.0 + 0.18 * jax.random.normal(keys[10], (D,), jnp.float32), 0.1, 1.9),
        "gate_weight": centred(keys[11], (D, FF), D ** -0.5, 0.0625, ((0, 32), (1, 8))),
        "up_weight": centred(keys[12], (D, FF), D ** -0.5, 0.0625, ((0, 32), (1, 8))),
        "down_weight": centred(keys[13], (FF, D), FF ** -0.5, 0.03125, ((0, 8), (1, 32))),
        "image_tiles": jax.vmap(lambda own: uneven(own, IMG_DEV, TILE_DEV, MAXT, 1))(jax.random.split(keys[14], N_GROUP)).reshape((N_GROUP, IMG_DEV)).astype(jnp.int32),
        "image_groups": draw_image_groups(jax.random.fold_in(keys[17], 71), 0),
        "image_requests": draw_image_requests(jax.random.fold_in(keys[17], 71), 0),
    }


def rms_norm(values, gain):
    mean_square = lax.optimization_barrier(jnp.mean(values * values, axis=-1, keepdims=True))
    return values * lax.rsqrt(mean_square + 1e-05) * gain

def reference(hidden, vision, attn_gain, q_weight, k_weight, v_weight, q_gain, k_gain, o_weight, gate_logits, mlp_gain, gate_weight, up_weight, down_weight, image_tiles, image_groups, image_requests):
    all_rows = hidden.shape[0]
    group_share = HQ // KVH
    score_scale = 1.0 / math.sqrt(HEAD)
    hidden_f = hidden.astype(jnp.float32)
    normed = (hidden_f * attn_gain).astype(jnp.bfloat16)
    queries = jnp.dot(normed, q_weight, preferred_element_type=jnp.float32).reshape(all_rows, HQ, HEAD)
    queries = lax.optimization_barrier(rms_norm(queries, q_gain).astype(jnp.bfloat16))
    key_proj = jnp.dot(vision, k_weight, preferred_element_type=jnp.float32).reshape(-1, KVH, HEAD)
    key_proj = lax.optimization_barrier(rms_norm(key_proj, k_gain).astype(jnp.bfloat16))
    value_proj = jnp.dot(vision, v_weight, preferred_element_type=jnp.float32).astype(jnp.bfloat16)
    value_proj = lax.optimization_barrier(value_proj).reshape(-1, KVH, HEAD)
    tile_ends = jnp.cumsum(image_tiles, axis=1).astype(jnp.int32)
    tile_number = jnp.arange(TILE_DEV, dtype=jnp.int32)
    owner_local = lax.optimization_barrier(jnp.sum((tile_number[None, :, None] >= tile_ends[:, None, :]).astype(jnp.int32), axis=2))
    owner_image = owner_local + jnp.arange(N_GROUP, dtype=jnp.int32)[:, None] * IMG_DEV
    key_image = jnp.repeat(owner_image.reshape(-1), TILE_TOK, total_repeat_length=N_GROUP * VROWS)
    request_ids = image_groups * REQ_DEV + image_requests
    request_range = jnp.arange(REQUESTS, dtype=jnp.int32)
    links = jnp.any(request_ids[:, :, None] == request_range[None, None, :], axis=1)
    row_request = jnp.arange(all_rows, dtype=jnp.int32) // STEPS
    allowed = links[key_image][:, row_request].T
    has_image = jnp.any(links, axis=0)[row_request]

    def one_head(kv_index):
        query_block = lax.dynamic_slice_in_dim(queries, kv_index * group_share, group_share, 1).astype(jnp.float32)
        key_block = lax.dynamic_index_in_dim(key_proj, kv_index, 1, keepdims=False).astype(jnp.float32)
        value_block = lax.dynamic_index_in_dim(value_proj, kv_index, 1, keepdims=False).astype(jnp.float32)
        scores = jnp.einsum('rsh,nh->srn', query_block, key_block) * score_scale
        permitted = allowed[None]
        highest = lax.optimization_barrier(jnp.max(jnp.where(permitted, scores, -1e+30), axis=-1, keepdims=True))
        weights = jnp.where(permitted, jnp.exp(scores - highest), 0.0)
        denominator = jnp.maximum(lax.optimization_barrier(jnp.sum(weights, axis=-1, keepdims=True)), 1.0)
        attn_probs = lax.optimization_barrier((weights / denominator).astype(jnp.bfloat16)).astype(jnp.float32)
        return jnp.einsum('srn,nh->rsh', attn_probs, value_block)
    heads_out = lax.map(one_head, jnp.arange(KVH, dtype=jnp.int32))
    attended = jnp.transpose(heads_out, (1, 0, 2, 3)).reshape(all_rows, HQ * HEAD).astype(jnp.bfloat16)
    attn_sum = jnp.dot(attended, o_weight, preferred_element_type=jnp.float32)
    middle = (hidden_f + jnp.tanh(gate_logits[0]) * attn_sum).astype(jnp.bfloat16)
    middle_f = lax.optimization_barrier(middle).astype(jnp.float32)
    mlp_normed = rms_norm(middle_f, mlp_gain).astype(jnp.bfloat16)
    gate_sum = jnp.dot(mlp_normed, gate_weight, preferred_element_type=jnp.float32)
    up_sum = jnp.dot(mlp_normed, up_weight, preferred_element_type=jnp.float32)
    active = (jax.nn.silu(gate_sum) * up_sum).astype(jnp.bfloat16)
    down_sum = jnp.dot(active, down_weight, preferred_element_type=jnp.float32)
    image_mask = has_image.astype(jnp.float32)
    return (middle_f + jnp.tanh(gate_logits[1]) * image_mask[:, None] * down_sum).astype(jnp.bfloat16)
```

```python
import math

import jax
import jax.numpy as jnp
from jax import lax
from jax.experimental import pallas as pl
from jax.experimental.pallas import tpu as pltpu
from jax.sharding import Mesh
from jax.sharding import PartitionSpec as P

GROUP = ("z", "y")
TENSOR = ("x", "c")
HEAD = 128
SLOTS = 2
STEPS = 2
EPS = 1e-05
VMEM_BYTES = 40 * 1024 * 1024
BF = jnp.bfloat16
F32 = jnp.float32


def params():
    return pltpu.CompilerParams(vmem_limit_bytes=VMEM_BYTES)


def dot(a, b):
    return jnp.dot(a, b, preferred_element_type=F32)


def vmem():
    return pl.BlockSpec(memory_space=pltpu.VMEM)


def smem():
    return pl.BlockSpec(memory_space=pltpu.SMEM)


def route_kernel(me_ref, routes_ref, requests_ref, sel_ref, image_ref):
    me = me_ref[0]
    groups, links = routes_ref.shape
    rows = groups * SLOTS * STEPS
    row = lax.broadcasted_iota(jnp.int32, (rows, links), 0)
    lane = lax.broadcasted_iota(jnp.int32, (rows, links), 1)
    group_of_row = row >> 2
    slot = (row >> 1) & 1
    step = row & 1
    spread = (group_of_row == lane).astype(F32)
    link = lax.broadcasted_iota(jnp.int32, (groups, links), 1)
    code = (link * 4 + requests_ref[...]).astype(F32)
    route_rows = dot(spread, routes_ref[...].astype(F32))
    code_rows = dot(spread, code)
    hit = route_rows == me.astype(F32)
    first = jnp.min(jnp.where(hit, code_rows, 1e4), axis=1, keepdims=True)
    last = jnp.max(jnp.where(hit, code_rows, -1.0), axis=1, keepdims=True)
    slot1, step1 = slot[:, :1], step[:, :1]
    chosen = jnp.where(slot1 == 0, first, last).astype(jnp.int32)
    found_first = jnp.where(first < 1e3, 1, 0)
    found_last = jnp.where(last > first, 1, 0)
    found = jnp.where(slot1 == 0, found_first, found_last)
    wanted = jnp.where(found == 1, (chosen & 3) * STEPS + step1, -1)
    sel_ref[...] = jnp.where(lane[:, :8] == wanted, 1.0, 0.0).astype(BF)
    mine = routes_ref[pl.ds(me, 1), :]
    here = mine == group_of_row
    first_link = jnp.min(jnp.where(here, lane, 1000), axis=1, keepdims=True)
    last_link = jnp.max(jnp.where(here, lane, -1), axis=1, keepdims=True)
    first_image = jnp.where(first_link < 1000, first_link >> 3, -1)
    last_image = jnp.where(last_link > first_link, last_link >> 3, -1)
    image_ref[...] = jnp.where(slot1 == 0, first_image, last_image)


def kv_kernel(place_ref, vision_ref, k_ref, v_ref, out_ref):
    weight = jnp.concatenate((k_ref[...], v_ref[...]), axis=1)
    out_ref[0] = dot(vision_ref[...], weight).astype(BF)


def kv_project(place, vision, k_weight, v_weight, other):
    rows, depth = vision.shape
    chips = 4

    def head(d, place_ref):
        core = place_ref[1]
        return 0, lax.rem(place_ref[0] + d, chips) * 2 + (1 - core if other else core)

    return pl.pallas_call(
        kv_kernel,
        grid_spec=pltpu.PrefetchScalarGridSpec(
            num_scalar_prefetch=1,
            grid=(chips,),
            in_specs=[
                pl.BlockSpec((rows, depth), lambda d, p: (0, 0)),
                pl.BlockSpec((depth, HEAD), head),
                pl.BlockSpec((depth, HEAD), head),
            ],
            out_specs=pl.BlockSpec((1, rows, 2 * HEAD), lambda d, p: (d, 0, 0)),
        ),
        out_shape=jax.ShapeDtypeStruct((chips, rows, 2 * HEAD), BF),
        compiler_params=params(),
        cost_estimate=pl.CostEstimate(
            flops=2 * chips * rows * depth * 2 * HEAD,
            bytes_accessed=2 * (rows * depth + chips * 2 * HEAD * (depth + rows)),
            transcendentals=0,
        ),
    )(place, vision, k_weight, v_weight)


def query_kernel(parts_ref, sel_ref, gain_ref, out_ref):
    total = jnp.sum(parts_ref[...].astype(F32), axis=0)
    gain = gain_ref[...]
    sel = sel_ref[...]
    for h in range(total.shape[1] // HEAD):
        span = slice(h * HEAD, (h + 1) * HEAD)
        v = total[:, span]
        scale = lax.rsqrt(jnp.mean(v * v, axis=1, keepdims=True) + EPS)
        q = (v * scale * gain).astype(BF)
        out_ref[:, span] = dot(sel, q).astype(BF)


def attention_kernel(me_ref, tiles_ref, own_ref, left_ref, right_ref, gain_ref, q_ref, image_ref, out_ref):
    me = me_ref[0]
    total = own_ref[...].astype(F32) + left_ref[...].astype(F32) + right_ref[...].astype(F32)
    k = total[:, :HEAD]
    scale = lax.rsqrt(jnp.mean(k * k, axis=1, keepdims=True) + EPS)
    k = (k * scale * gain_ref[...]).astype(BF)
    v = total[:, HEAD:].astype(BF)
    rows, keys = q_ref.shape[0], k.shape[0]
    tile = lax.broadcasted_iota(jnp.int32, (1, keys), 1) >> 6
    owner = jnp.zeros((1, keys), jnp.int32)
    end = jnp.int32(0)
    for j in range(4):
        end = end + tiles_ref[me, j]
        owner = owner + (tile >= end).astype(jnp.int32)
    allowed = owner == image_ref[...]
    lane = lax.broadcasted_iota(jnp.int32, (rows, HEAD), 1)
    sums = jnp.zeros((rows, HEAD), F32)
    heads = q_ref.shape[1] // HEAD
    for h in range(heads):
        span = slice(h * HEAD, (h + 1) * HEAD)
        score = lax.dot_general(
            q_ref[:, span], k, (((1,), (1,)), ((), ())), preferred_element_type=F32
        )
        weight = jnp.where(allowed, jnp.exp(score * (1.0 / math.sqrt(HEAD))), 0.0)
        den = jnp.sum(weight, axis=1, keepdims=True)
        high = den.astype(BF).astype(F32)
        sums = sums + jnp.where(lane == h, high, 0.0) + jnp.where(lane == heads + h, den - high, 0.0)
        out_ref[:, span] = dot(weight.astype(BF), v).astype(BF)
    out_ref[:, heads * HEAD :] = sums.astype(BF)


def combine_kernel(parts_ref, sel_ref, out_ref):
    total = lax.dot_general(
        sel_ref[...], parts_ref[...], (((0,), (0,)), ((), ())), preferred_element_type=F32
    )
    heads = out_ref.shape[2] // HEAD
    sums = total[:, heads * HEAD :]
    for h in range(heads):
        span = slice(h * HEAD, (h + 1) * HEAD)
        den = sums[:, h : h + 1] + sums[:, heads + h : heads + h + 1]
        mixed = (total[:, span] / jnp.where(den > 0.0, den, 1.0)).astype(BF)
        out_ref[:, :, span] = jnp.broadcast_to(mixed[None], (out_ref.shape[0],) + mixed.shape)


def shift(value, axis, by):
    n = lax.axis_size(axis)
    return lax.ppermute(value, axis, [(i, (i + by) % n) for i in range(n)])


def exchange(value, axis):
    n = lax.axis_size(axis)
    out = lax.all_to_all(value, axis, 0, 0, tiled=True)
    return out.reshape((n, value.shape[0] // n) + value.shape[1:])


def gather(value, axis):
    n = lax.axis_size(axis)
    wide = jnp.broadcast_to(value[None], (n,) + value.shape)
    out = lax.all_to_all(wide, axis, 0, 0, tiled=True)
    return out.reshape((n * value.shape[0],) + value.shape[1:])


def tensor_sum(part):
    part = part.astype(BF)
    pair = (part.astype(F32) + shift(part, "c", 1).astype(F32)).astype(BF)
    ahead, behind, across = shift(pair, "x", 1), shift(pair, "x", -1), shift(pair, "x", 2)
    return (pair.astype(F32) + across.astype(F32)) + (ahead.astype(F32) + behind.astype(F32))


def shards(
    hidden,
    vision,
    attn_gain,
    q_weight,
    k_weight,
    v_weight,
    q_gain,
    k_gain,
    o_weight,
    gate_logits,
    mlp_gain,
    gate_weight,
    up_weight,
    down_weight,
    image_tiles,
    image_groups,
    image_requests,
):
    groups = lax.axis_size("z") * lax.axis_size("y")
    me = (lax.axis_index("z") * lax.axis_size("y") + lax.axis_index("y")).astype(jnp.int32).reshape(1)
    place = jnp.stack((lax.axis_index("x"), lax.axis_index("c"))).astype(jnp.int32)
    all_rows, width_part = hidden.shape
    own_rows = all_rows // groups
    full_width = width_part * groups
    local_heads = q_weight.shape[1]
    hidden_part = gate_weight.shape[1]
    slot_rows = groups * SLOTS * STEPS
    key_rows = vision.shape[0]

    sel, row_image = pl.pallas_call(
        route_kernel,
        in_specs=[smem(), vmem(), vmem()],
        out_specs=[vmem(), vmem()],
        out_shape=[
            jax.ShapeDtypeStruct((slot_rows, own_rows), BF),
            jax.ShapeDtypeStruct((slot_rows, 1), jnp.int32),
        ],
        compiler_params=params(),
    )(me, image_groups.reshape(groups, -1), image_requests.reshape(groups, -1))

    hidden_f = hidden.astype(F32)
    normed = (hidden_f * attn_gain).astype(BF)
    q_parts = exchange(dot(normed, q_weight).astype(BF), GROUP)

    there = kv_project(place, vision, k_weight, v_weight, True)
    from_core = shift(there, "c", 1)
    here = kv_project(place, vision, k_weight, v_weight, False)
    pieces = (here.astype(F32) + from_core.astype(F32)).astype(BF)
    half = key_rows // 2
    low = shift(pieces[2, :half], "x", 1)
    high = shift(pieces[2, half:], "x", -1)
    forward = jnp.concatenate(
        ((pieces[1, :half].astype(F32) + low.astype(F32)).astype(BF), pieces[1, half:]), axis=0
    )
    backward = jnp.concatenate(
        (pieces[3, :half], (pieces[3, half:].astype(F32) + high.astype(F32)).astype(BF)), axis=0
    )
    kv_left = shift(forward, "x", 1)
    kv_right = shift(backward, "x", -1)

    queries = pl.pallas_call(
        query_kernel,
        in_specs=[vmem()] * 3,
        out_specs=vmem(),
        out_shape=jax.ShapeDtypeStruct((slot_rows, local_heads), BF),
        compiler_params=params(),
    )(q_parts, sel, q_gain.reshape(1, HEAD))
    queries = lax.all_to_all(queries, GROUP, 0, 0, tiled=True)

    mixed = pl.pallas_call(
        attention_kernel,
        in_specs=[smem(), smem()] + [vmem()] * 6,
        out_specs=vmem(),
        out_shape=jax.ShapeDtypeStruct((slot_rows, local_heads + HEAD), BF),
        compiler_params=params(),
    )(me, image_tiles, pieces[0], kv_left, kv_right, k_gain.reshape(1, HEAD), queries, row_image)
    mixed = lax.all_to_all(mixed, GROUP, 0, 0, tiled=True)

    attended = pl.pallas_call(
        combine_kernel,
        in_specs=[vmem()] * 2,
        out_specs=vmem(),
        out_shape=jax.ShapeDtypeStruct((groups, own_rows, local_heads), BF),
        compiler_params=params(),
    )(mixed, sel)
    attended = lax.all_to_all(attended, GROUP, 0, 0, tiled=True).reshape(all_rows, local_heads)

    attn_sum = tensor_sum(dot(attended, o_weight))
    middle = (hidden_f + jnp.tanh(gate_logits[0]) * attn_sum).astype(BF)
    middle_f = middle.astype(F32)
    scaled = (middle_f * mlp_gain).astype(BF)
    square = jnp.sum(middle_f * middle_f, axis=1, keepdims=True)
    square_high = square.astype(BF)
    square_low = (square - square_high.astype(F32)).astype(BF)
    lane = lax.broadcasted_iota(jnp.int32, (all_rows, HEAD), 1)
    extra = jnp.where(lane == 0, square_high, jnp.where(lane == 1, square_low, jnp.zeros((), BF)))
    gate_up = jnp.concatenate(
        (dot(scaled, gate_weight).astype(BF), dot(scaled, up_weight).astype(BF), extra), axis=1
    )
    by_y = jnp.sum(exchange(gate_up, "y").astype(F32), axis=0).astype(BF)
    summed = jnp.sum(exchange(by_y, "z").astype(F32), axis=0)
    square = summed[:, 2 * hidden_part : 2 * hidden_part + 1] + summed[:, 2 * hidden_part + 1 : 2 * hidden_part + 2]
    row_scale = lax.rsqrt(square / full_width + EPS)
    gate = summed[:, :hidden_part] * row_scale
    up = summed[:, hidden_part : 2 * hidden_part] * row_scale
    active = (jax.nn.silu(gate) * up).astype(BF)
    active = gather(gather(active, "z"), "y")
    down_sum = tensor_sum(dot(active, down_weight))
    row_request = jnp.arange(all_rows, dtype=jnp.int32) // STEPS
    request_ids = (image_groups * (own_rows // STEPS) + image_requests).reshape(-1)
    has_image = jnp.any(row_request[:, None] == request_ids[None, :], axis=1).astype(F32)
    return (middle_f + jnp.tanh(gate_logits[1]) * has_image[:, None] * down_sum).astype(BF)


def solution(mesh):
    fine = Mesh(mesh.devices.reshape(8, 4, 4, 2), GROUP + TENSOR)
    in_specs = (
        P(None, GROUP),
        P(GROUP, TENSOR),
        P(GROUP),
        P(GROUP, TENSOR),
        P(TENSOR, None),
        P(TENSOR, None),
        P(),
        P(),
        P(TENSOR, GROUP),
        P(),
        P(GROUP),
        P(GROUP, TENSOR),
        P(GROUP, TENSOR),
        P(TENSOR, GROUP),
        P(),
        P(),
        P(),
    )
    return jax.shard_map(shards, mesh=fine, in_specs=in_specs, out_specs=P(None, GROUP), check_vma=False)
```

```python
import functools
import math

import jax
import jax.numpy as jnp
from jax import lax
from jax.experimental import pallas as pl
from jax.experimental.pallas import tpu as pltpu
from jax.sharding import Mesh
from jax.sharding import PartitionSpec as P

GROUP = ("z", "y")
TENSOR = ("x", "c")
HEAD = 128
SLOTS = 2
STEPS = 2
EPS = 1e-05
VMEM_BYTES = 40 * 1024 * 1024
BF = jnp.bfloat16
F32 = jnp.float32


def params():
    return pltpu.CompilerParams(vmem_limit_bytes=VMEM_BYTES)


def dot(a, b):
    return jnp.dot(a, b, preferred_element_type=F32)


def vmem():
    return pl.BlockSpec(memory_space=pltpu.VMEM)


def smem():
    return pl.BlockSpec(memory_space=pltpu.SMEM)


def route_kernel(me_ref, routes_ref, requests_ref, sel_ref, image_ref):
    me = me_ref[0]
    groups, links = routes_ref.shape
    rows = groups * SLOTS * STEPS
    row = lax.broadcasted_iota(jnp.int32, (rows, links), 0)
    lane = lax.broadcasted_iota(jnp.int32, (rows, links), 1)
    group_of_row = row >> 2
    slot = (row >> 1) & 1
    step = row & 1
    spread = (group_of_row == lane).astype(F32)
    link = lax.broadcasted_iota(jnp.int32, (groups, links), 1)
    code = (link * 4 + requests_ref[...]).astype(F32)
    route_rows = dot(spread, routes_ref[...].astype(F32))
    code_rows = dot(spread, code)
    hit = route_rows == me.astype(F32)
    first = jnp.min(jnp.where(hit, code_rows, 1e4), axis=1, keepdims=True)
    last = jnp.max(jnp.where(hit, code_rows, -1.0), axis=1, keepdims=True)
    slot1, step1 = slot[:, :1], step[:, :1]
    chosen = jnp.where(slot1 == 0, first, last).astype(jnp.int32)
    found_first = jnp.where(first < 1e3, 1, 0)
    found_last = jnp.where(last > first, 1, 0)
    found = jnp.where(slot1 == 0, found_first, found_last)
    wanted = jnp.where(found == 1, (chosen & 3) * STEPS + step1, -1)
    sel_ref[...] = jnp.where(lane[:, :8] == wanted, 1.0, 0.0).astype(BF)
    mine = routes_ref[pl.ds(me, 1), :]
    here = mine == group_of_row
    first_link = jnp.min(jnp.where(here, lane, 1000), axis=1, keepdims=True)
    last_link = jnp.max(jnp.where(here, lane, -1), axis=1, keepdims=True)
    first_image = jnp.where(first_link < 1000, first_link >> 3, -1)
    last_image = jnp.where(last_link > first_link, last_link >> 3, -1)
    image_ref[...] = jnp.where(slot1 == 0, first_image, last_image)


def kv_there_kernel(place_ref, vision_ref, k_ref, v_ref, out_ref):
    weight = jnp.concatenate((k_ref[...], v_ref[...]), axis=1)
    out_ref[0] = dot(vision_ref[...], weight).astype(BF)


def kv_here_kernel(place_ref, vision_ref, k_ref, v_ref, core_ref, low_ref, high_ref, ahead_ref, behind_ref, own_ref):
    weight = jnp.concatenate((k_ref[...], v_ref[...]), axis=1)
    total = (dot(vision_ref[...], weight) + core_ref[0].astype(F32)).astype(BF)
    half = low_ref.shape[0]
    step = pl.program_id(0)

    @pl.when(step == 0)
    def _():
        low_ref[...] = total[:half]
        high_ref[...] = total[half:]

    @pl.when(step == 1)
    def _():
        ahead_ref[...] = total

    @pl.when(step == 2)
    def _():
        behind_ref[...] = total

    @pl.when(step == 3)
    def _():
        own_ref[...] = total


def kv_project(place, vision, k_weight, v_weight, from_core=None):
    rows, depth = vision.shape
    chips = 4
    other = from_core is None

    def head(d, place_ref):
        core = place_ref[1]
        ahead = jnp.where(d == 0, 2, jnp.where(d == 1, 1, jnp.where(d == 2, 3, 0)))
        return 0, lax.rem(place_ref[0] + ahead, chips) * 2 + (1 - core if other else core)

    one = pl.BlockSpec((1, rows, 2 * HEAD), lambda d, p: (d, 0, 0))
    sizes = [rows // 2, rows // 2, rows, rows, rows]
    whole = [pl.BlockSpec((n, 2 * HEAD), lambda d, p: (0, 0)) for n in sizes]
    return pl.pallas_call(
        kv_there_kernel if other else kv_here_kernel,
        grid_spec=pltpu.PrefetchScalarGridSpec(
            num_scalar_prefetch=1,
            grid=(chips,),
            in_specs=[
                pl.BlockSpec((rows, depth), lambda d, p: (0, 0)),
                pl.BlockSpec((depth, HEAD), head),
                pl.BlockSpec((depth, HEAD), head),
            ]
            + ([] if other else [one]),
            out_specs=one if other else whole,
        ),
        out_shape=jax.ShapeDtypeStruct((chips, rows, 2 * HEAD), BF)
        if other
        else [jax.ShapeDtypeStruct((n, 2 * HEAD), BF) for n in sizes],
        compiler_params=params(),
        cost_estimate=pl.CostEstimate(
            flops=2 * chips * rows * depth * 2 * HEAD,
            bytes_accessed=2 * (rows * depth + chips * 2 * HEAD * (depth + rows)),
            transcendentals=0,
        ),
    )(place, vision, k_weight, v_weight, *(() if other else (from_core,)))


def kv_merge_kernel(ahead_ref, behind_ref, low_ref, high_ref, forward_ref, backward_ref):
    half = low_ref.shape[0]
    forward_ref[:half] = (ahead_ref[:half].astype(F32) + low_ref[...].astype(F32)).astype(BF)
    forward_ref[half:] = ahead_ref[half:]
    backward_ref[:half] = behind_ref[:half]
    backward_ref[half:] = (behind_ref[half:].astype(F32) + high_ref[...].astype(F32)).astype(BF)


def query_kernel(parts_ref, sel_ref, gain_ref, out_ref):
    total = jnp.sum(parts_ref[...].astype(F32), axis=0)
    gain = gain_ref[...]
    sel = sel_ref[...]
    for h in range(total.shape[1] // HEAD):
        span = slice(h * HEAD, (h + 1) * HEAD)
        v = total[:, span]
        scale = lax.rsqrt(jnp.mean(v * v, axis=1, keepdims=True) + EPS)
        q = (v * scale * gain).astype(BF)
        out_ref[:, span] = dot(sel, q).astype(BF)


def attention_kernel(me_ref, tiles_ref, own_ref, left_ref, right_ref, gain_ref, q_ref, image_ref, out_ref):
    me = me_ref[0]
    total = own_ref[...].astype(F32) + left_ref[...].astype(F32) + right_ref[...].astype(F32)
    k = total[:, :HEAD]
    scale = lax.rsqrt(jnp.mean(k * k, axis=1, keepdims=True) + EPS)
    k = (k * scale * gain_ref[...]).astype(BF)
    v = total[:, HEAD:].astype(BF)
    rows, keys = q_ref.shape[0], k.shape[0]
    tile = lax.broadcasted_iota(jnp.int32, (1, keys), 1) >> 6
    owner = jnp.zeros((1, keys), jnp.int32)
    end = jnp.int32(0)
    for j in range(4):
        end = end + tiles_ref[me, j]
        owner = owner + (tile >= end).astype(jnp.int32)
    allowed = owner == image_ref[...]
    lane = lax.broadcasted_iota(jnp.int32, (rows, HEAD), 1)
    sums = jnp.zeros((rows, HEAD), F32)
    heads = q_ref.shape[1] // HEAD
    for h in range(heads):
        span = slice(h * HEAD, (h + 1) * HEAD)
        score = lax.dot_general(
            q_ref[:, span], k, (((1,), (1,)), ((), ())), preferred_element_type=F32
        )
        weight = jnp.where(allowed, jnp.exp(score * (1.0 / math.sqrt(HEAD))), 0.0)
        den = jnp.sum(weight, axis=1, keepdims=True)
        high = den.astype(BF).astype(F32)
        sums = sums + jnp.where(lane == h, high, 0.0) + jnp.where(lane == heads + h, den - high, 0.0)
        out_ref[:, span] = dot(weight.astype(BF), v).astype(BF)
    out_ref[:, heads * HEAD :] = sums.astype(BF)


def combine_kernel(parts_ref, sel_ref, out_ref):
    total = lax.dot_general(
        sel_ref[...], parts_ref[...], (((0,), (0,)), ((), ())), preferred_element_type=F32
    )
    heads = out_ref.shape[2] // HEAD
    sums = total[:, heads * HEAD :]
    for h in range(heads):
        span = slice(h * HEAD, (h + 1) * HEAD)
        den = sums[:, h : h + 1] + sums[:, heads + h : heads + h + 1]
        mixed = (total[:, span] / jnp.where(den > 0.0, den, 1.0)).astype(BF)
        out_ref[:, :, span] = jnp.broadcast_to(mixed[None], (out_ref.shape[0],) + mixed.shape)


def gate_up_kernel(m0, m1, m2, m3, w0, w1, gate2, up2, w3, out_ref):
    blocks = (m0, m1, m2, m3)
    units = gate2.shape[1]
    columns = 2 * units
    for start in range(0, columns, HEAD):
        span = slice(start, start + HEAD)
        part = slice(start % units, start % units + HEAD)
        w2 = gate2 if start < units else up2
        total = dot(m0[...], w0[:, span]) + dot(m1[...], w1[:, span])
        total = total + dot(m2[...], w2[:, part]) + dot(m3[...], w3[:, span])
        out_ref[:, span] = total.astype(BF)
    square = jnp.zeros((m0.shape[0], 1), F32)
    for m in blocks:
        value = m[...].astype(F32)
        square = square + jnp.sum(value * value, axis=1, keepdims=True)
    high = square.astype(BF).astype(F32)
    lane = lax.broadcasted_iota(jnp.int32, (m0.shape[0], HEAD), 1)
    extra = jnp.where(lane == 0, high, jnp.where(lane == 1, square - high, 0.0))
    out_ref[:, columns:] = extra.astype(BF)


def active_kernel(full_width, parts_ref, out_ref):
    total = jnp.sum(parts_ref[...].astype(F32), axis=0)
    units = out_ref.shape[2]
    square = total[:, 2 * units : 2 * units + 1] + total[:, 2 * units + 1 : 2 * units + 2]
    scale = lax.rsqrt(square * (1.0 / full_width) + EPS)
    gate = total[:, :units] * scale
    up = total[:, units : 2 * units] * scale
    active = (gate / (1.0 + jnp.exp(-gate)) * up).astype(BF)
    out_ref[...] = jnp.broadcast_to(active[None], out_ref.shape)


def shift(value, axis, by):
    n = lax.axis_size(axis)
    return lax.ppermute(value, axis, [(i, (i + by) % n) for i in range(n)])


def after(value, *others):
    return lax.optimization_barrier((value,) + others)[0]


def exchange(value, axis):
    n = lax.axis_size(axis)
    out = lax.all_to_all(value, axis, 0, 0, tiled=True)
    return out.reshape((n, value.shape[0] // n) + value.shape[1:])


def tensor_sum(part):
    part = part.astype(BF)
    pair = (part.astype(F32) + shift(part, "c", 1).astype(F32)).astype(BF)
    ahead, behind, across = shift(pair, "x", 1), shift(pair, "x", -1), shift(pair, "x", 2)
    return (pair.astype(F32) + across.astype(F32)) + (ahead.astype(F32) + behind.astype(F32))


def shards(
    hidden,
    vision,
    attn_gain,
    q_weight,
    k_weight,
    v_weight,
    q_gain,
    k_gain,
    o_weight,
    gate_logits,
    mlp_gain,
    gate_weight,
    up_weight,
    down_weight,
    image_tiles,
    image_groups,
    image_requests,
):
    groups = lax.axis_size("z") * lax.axis_size("y")
    me = (lax.axis_index("z") * lax.axis_size("y") + lax.axis_index("y")).astype(jnp.int32).reshape(1)
    place = jnp.stack((lax.axis_index("x"), lax.axis_index("c"))).astype(jnp.int32)
    all_rows, width_part = hidden.shape
    own_rows = all_rows // groups
    full_width = width_part * groups
    local_heads = q_weight.shape[1]
    hidden_part = gate_weight.shape[1]
    slot_rows = groups * SLOTS * STEPS
    key_rows = vision.shape[0]

    sel, row_image = pl.pallas_call(
        route_kernel,
        in_specs=[smem(), vmem(), vmem()],
        out_specs=[vmem(), vmem()],
        out_shape=[
            jax.ShapeDtypeStruct((slot_rows, own_rows), BF),
            jax.ShapeDtypeStruct((slot_rows, 1), jnp.int32),
        ],
        compiler_params=params(),
    )(me, image_groups.reshape(groups, -1), image_requests.reshape(groups, -1))

    hidden_f = hidden.astype(F32)
    normed = (hidden_f * attn_gain).astype(BF)
    q_part = dot(normed, q_weight).astype(BF)
    q_part, vision = lax.optimization_barrier((q_part, vision))
    q_parts = exchange(q_part, GROUP)

    there = kv_project(place, vision, k_weight, v_weight)
    low, high, ahead, behind, own = kv_project(place, vision, k_weight, v_weight, shift(there, "c", 1))
    q_parts = after(q_parts, own)
    forward, backward = pl.pallas_call(
        kv_merge_kernel,
        in_specs=[vmem()] * 4,
        out_specs=[vmem()] * 2,
        out_shape=[jax.ShapeDtypeStruct(ahead.shape, BF)] * 2,
        compiler_params=params(),
    )(ahead, behind, shift(low, "x", 1), shift(high, "x", -1))
    kv_left = shift(forward, "x", 1)
    kv_right = shift(backward, "x", -1)

    chips_y = lax.axis_size("y")
    units = hidden_part // chips_y
    gain = mlp_gain[:, None]

    def columns(weight, d):
        at = lax.rem(lax.axis_index("y") + d, chips_y) * units
        return lax.dynamic_slice_in_dim(weight, at, units, 1).astype(F32)

    def rows(weight, d, start, size):
        at = lax.rem(lax.axis_index("y") + d, chips_y) * units + start
        return lax.dynamic_slice_in_dim(weight, at, size, 0)

    def wide(*parts):
        return (jnp.concatenate(parts, axis=1) * gain).astype(BF)

    wide_0 = wide(columns(gate_weight, 0), columns(up_weight, 0))
    wide_1 = wide(columns(gate_weight, 1), columns(up_weight, 1), columns(gate_weight, 2))
    wide_3 = wide(columns(gate_weight, 3), columns(up_weight, 3), columns(up_weight, 2))
    wide_1 = shift(wide_1, "y", 1)
    wide_3 = shift(wide_3, "y", -1)
    gate_2 = shift(wide_1[:, 2 * units :], "y", 1)
    up_2 = shift(wide_3[:, 2 * units :], "y", -1)
    half = units // 2
    down_0 = rows(down_weight, 0, 0, units)
    down_1 = jnp.concatenate((rows(down_weight, 1, 0, units), rows(down_weight, 2, 0, half)), axis=0)
    down_3 = jnp.concatenate((rows(down_weight, 3, 0, units), rows(down_weight, 2, half, half)), axis=0)

    queries = pl.pallas_call(
        query_kernel,
        in_specs=[vmem()] * 3,
        out_specs=vmem(),
        out_shape=jax.ShapeDtypeStruct((slot_rows, local_heads), BF),
        compiler_params=params(),
    )(q_parts, sel, q_gain.reshape(1, HEAD))
    queries = lax.all_to_all(queries, GROUP, 0, 0, tiled=True)

    queries = after(queries, wide_1, wide_3)
    mixed = pl.pallas_call(
        attention_kernel,
        in_specs=[smem(), smem()] + [vmem()] * 6,
        out_specs=vmem(),
        out_shape=jax.ShapeDtypeStruct((slot_rows, local_heads + HEAD), BF),
        compiler_params=params(),
    )(me, image_tiles, own, kv_left, kv_right, k_gain.reshape(1, HEAD), queries, row_image)
    mixed = lax.all_to_all(mixed, GROUP, 0, 0, tiled=True)

    mixed = after(mixed, gate_2, up_2)
    attended = pl.pallas_call(
        combine_kernel,
        in_specs=[vmem()] * 2,
        out_specs=vmem(),
        out_shape=jax.ShapeDtypeStruct((groups, own_rows, local_heads), BF),
        compiler_params=params(),
    )(mixed, sel)
    down_1 = shift(after(down_1, queries), "y", 1)
    down_3 = shift(after(down_3, queries), "y", -1)
    attended = lax.all_to_all(attended, GROUP, 0, 0, tiled=True).reshape(all_rows, local_heads)

    attended = after(attended, down_1, down_3)
    attn_sum = tensor_sum(dot(attended, o_weight))
    middle = (hidden_f + jnp.tanh(gate_logits[0]) * attn_sum).astype(BF)
    middle_f = middle.astype(F32)
    middles = [middle] + [shift(middle, "y", d) for d in (1, 2, 3)]
    gate_up = pl.pallas_call(
        gate_up_kernel,
        in_specs=[vmem()] * 9,
        out_specs=vmem(),
        out_shape=jax.ShapeDtypeStruct((all_rows, 2 * units + HEAD), BF),
        compiler_params=params(),
    )(*middles, wide_0, wide_1, gate_2, up_2, wide_3)
    down_2 = (shift(down_1[units:], "y", 1), shift(down_3[units:], "y", -1))
    parts = exchange(gate_up, "z")
    active = pl.pallas_call(
        functools.partial(active_kernel, full_width),
        in_specs=[vmem()],
        out_specs=vmem(),
        out_shape=jax.ShapeDtypeStruct(parts.shape[:2] + (units,), BF),
        compiler_params=params(),
    )(parts)
    active = lax.all_to_all(active, "z", 0, 0, tiled=True).reshape(all_rows, units)
    across = dot(active[:, :half], down_2[0]) + dot(active[:, half:], down_2[1])
    across = shift(across.astype(BF), "y", 2)
    behind = shift(dot(active, down_1[:units]).astype(BF), "y", -1)
    ahead = shift(dot(active, down_3[:units]).astype(BF), "y", 1)
    down_part = dot(active, down_0) + across.astype(F32) + behind.astype(F32) + ahead.astype(F32)
    down_sum = tensor_sum(down_part)
    row_request = jnp.arange(all_rows, dtype=jnp.int32) // STEPS
    request_ids = (image_groups * (own_rows // STEPS) + image_requests).reshape(-1)
    has_image = jnp.any(row_request[:, None] == request_ids[None, :], axis=1).astype(F32)
    return (middle_f + jnp.tanh(gate_logits[1]) * has_image[:, None] * down_sum).astype(BF)


def solution(mesh):
    fine = Mesh(mesh.devices.reshape(8, 4, 4, 2), GROUP + TENSOR)
    in_specs = (
        P(None, GROUP),
        P(GROUP, TENSOR),
        P(GROUP),
        P(GROUP, TENSOR),
        P(TENSOR, None),
        P(TENSOR, None),
        P(),
        P(),
        P(TENSOR, GROUP),
        P(),
        P(GROUP),
        P(GROUP, TENSOR),
        P(GROUP, TENSOR),
        P(TENSOR, GROUP),
        P(),
        P(),
        P(),
    )
    return jax.shard_map(shards, mesh=fine, in_specs=in_specs, out_specs=P(None, GROUP), check_vma=False)
```

```python
import functools
import math

import jax
import jax.numpy as jnp
from jax import lax
from jax.experimental import pallas as pl
from jax.experimental.pallas import tpu as pltpu
from jax.sharding import Mesh
from jax.sharding import PartitionSpec as P

GROUP = ("z", "y")
TENSOR = ("x", "c")
HEAD = 128
SLOTS = 2
STEPS = 2
EPS = 1e-05
VMEM_BYTES = 40 * 1024 * 1024
KV_VMEM_BYTES = 58 * 1024 * 1024
BF = jnp.bfloat16
F32 = jnp.float32


def params(limit=VMEM_BYTES):
    return pltpu.CompilerParams(vmem_limit_bytes=limit)


def dot(a, b):
    return jnp.dot(a, b, preferred_element_type=F32)


def vmem():
    return pl.BlockSpec(memory_space=pltpu.VMEM)


def smem():
    return pl.BlockSpec(memory_space=pltpu.SMEM)


def route_kernel(me_ref, routes_ref, requests_ref, sel_ref, image_ref):
    me = me_ref[0]
    groups, links = routes_ref.shape
    rows = groups * 2 * SLOTS * STEPS
    row = lax.broadcasted_iota(jnp.int32, (rows, links), 0)
    lane = lax.broadcasted_iota(jnp.int32, (rows, links), 1)
    group_of_row = row >> 3
    slot = (row >> 1) & 1
    step = row & 1
    spread = (group_of_row == lane).astype(F32)
    link = lax.broadcasted_iota(jnp.int32, (groups, links), 1)
    code = (link * 4 + requests_ref[...]).astype(F32)
    route_rows = dot(spread, routes_ref[...].astype(F32))
    code_rows = dot(spread, code)
    hit = route_rows == me.astype(F32)
    first = jnp.min(jnp.where(hit, code_rows, 1e4), axis=1, keepdims=True)
    last = jnp.max(jnp.where(hit, code_rows, -1.0), axis=1, keepdims=True)
    slot1, step1 = slot[:, :1], step[:, :1]
    chosen = jnp.where(slot1 == 0, first, last).astype(jnp.int32)
    found_first = jnp.where(first < 1e3, 1, 0)
    found_last = jnp.where(last > first, 1, 0)
    found = jnp.where(slot1 == 0, found_first, found_last)
    wanted = jnp.where(found == 1, (chosen & 3) * STEPS + step1, -1)
    sel_ref[...] = jnp.where(lane[:, :8] == wanted, 1.0, 0.0).astype(BF)
    mine = routes_ref[pl.ds(me, 1), :]
    here = mine == group_of_row
    first_link = jnp.min(jnp.where(here, lane, 1000), axis=1, keepdims=True)
    last_link = jnp.max(jnp.where(here, lane, -1), axis=1, keepdims=True)
    first_image = jnp.where(first_link < 1000, first_link >> 3, -1)
    last_image = jnp.where(last_link > first_link, last_link >> 3, -1)
    image_ref[...] = jnp.where(slot1 == 0, first_image, last_image)


def kv_there_kernel(place_ref, vision_ref, k_ref, v_ref, out_ref):
    weight = jnp.concatenate((k_ref[...], v_ref[...]), axis=1)
    out_ref[0] = dot(vision_ref[...], weight).astype(BF)


def kv_here_kernel(place_ref, vision_ref, k_ref, v_ref, core_ref, low_ref, high_ref, ahead_ref, behind_ref, own_ref):
    weight = jnp.concatenate((k_ref[...], v_ref[...]), axis=1)
    total = (dot(vision_ref[...], weight) + core_ref[0].astype(F32)).astype(BF)
    half = low_ref.shape[0]
    step = pl.program_id(0)

    @pl.when(step == 0)
    def _():
        low_ref[...] = total[:half]
        high_ref[...] = total[half:]

    @pl.when(step == 1)
    def _():
        ahead_ref[...] = total

    @pl.when(step == 2)
    def _():
        behind_ref[...] = total

    @pl.when(step == 3)
    def _():
        own_ref[...] = total


def kv_project(place, vision, k_weight, v_weight, from_core=None):
    rows, depth = vision.shape
    chips = 4
    other = from_core is None

    def head(d, place_ref):
        core = place_ref[1]
        ahead = jnp.where(d == 0, 2, jnp.where(d == 1, 1, jnp.where(d == 2, 3, 0)))
        return 0, lax.rem(place_ref[0] + ahead, chips) * 2 + (1 - core if other else core)

    one = pl.BlockSpec((1, rows, 2 * HEAD), lambda d, p: (d, 0, 0))
    sizes = [rows // 2, rows // 2, rows, rows, rows]
    whole = [pl.BlockSpec((n, 2 * HEAD), lambda d, p: (0, 0)) for n in sizes]
    return pl.pallas_call(
        kv_there_kernel if other else kv_here_kernel,
        grid_spec=pltpu.PrefetchScalarGridSpec(
            num_scalar_prefetch=1,
            grid=(chips,),
            in_specs=[
                pl.BlockSpec((rows, depth), lambda d, p: (0, 0)),
                pl.BlockSpec((depth, HEAD), head),
                pl.BlockSpec((depth, HEAD), head),
            ]
            + ([] if other else [one]),
            out_specs=one if other else whole,
        ),
        out_shape=jax.ShapeDtypeStruct((chips, rows, 2 * HEAD), BF)
        if other
        else [jax.ShapeDtypeStruct((n, 2 * HEAD), BF) for n in sizes],
        compiler_params=params(KV_VMEM_BYTES),
    )(place, vision, k_weight, v_weight, *(() if other else (from_core,)))


def kv_merge_kernel(ahead_ref, behind_ref, low_ref, high_ref, forward_ref, backward_ref):
    half = low_ref.shape[0]
    forward_ref[:half] = (ahead_ref[:half].astype(F32) + low_ref[...].astype(F32)).astype(BF)
    forward_ref[half:] = ahead_ref[half:]
    backward_ref[:half] = behind_ref[:half]
    backward_ref[half:] = (behind_ref[half:].astype(F32) + high_ref[...].astype(F32)).astype(BF)


def half_of(shape):
    return (lax.broadcasted_iota(jnp.int32, shape, 0) >> 2) & 1


def query_kernel(parts_ref, sel_ref, gain_ref, out_ref):
    total = jnp.sum(parts_ref[...].astype(F32), axis=0)
    gain = gain_ref[...]
    sel = sel_ref[...]
    heads = total.shape[1] // HEAD // 2
    upper = half_of((sel.shape[0], HEAD)) == 1

    def chosen(h):
        v = total[:, h * HEAD : (h + 1) * HEAD]
        scale = lax.rsqrt(jnp.mean(v * v, axis=1, keepdims=True) + EPS)
        return dot(sel, (v * scale * gain).astype(BF))

    for h in range(heads):
        out_ref[:, h * HEAD : (h + 1) * HEAD] = jnp.where(upper, chosen(heads + h), chosen(h)).astype(BF)


def attention_kernel(me_ref, tiles_ref, own_ref, left_ref, right_ref, gain_ref, q_ref, image_ref, out_ref):
    me = me_ref[0]
    total = own_ref[...].astype(F32) + left_ref[...].astype(F32) + right_ref[...].astype(F32)
    k = total[:, :HEAD]
    scale = lax.rsqrt(jnp.mean(k * k, axis=1, keepdims=True) + EPS)
    k = (k * scale * gain_ref[...]).astype(BF)
    v = total[:, HEAD:].astype(BF)
    rows, keys = q_ref.shape[0], k.shape[0]
    tile = lax.broadcasted_iota(jnp.int32, (1, keys), 1) >> 6
    owner = jnp.zeros((1, keys), jnp.int32)
    end = jnp.int32(0)
    for j in range(4):
        end = end + tiles_ref[me, j]
        owner = owner + (tile >= end).astype(jnp.int32)
    allowed = owner == image_ref[...]
    lane = lax.broadcasted_iota(jnp.int32, (rows, HEAD), 1)
    sums = jnp.zeros((rows, HEAD), F32)
    heads = q_ref.shape[1] // HEAD
    for h in range(heads):
        span = slice(h * HEAD, (h + 1) * HEAD)
        score = lax.dot_general(
            q_ref[:, span], k, (((1,), (1,)), ((), ())), preferred_element_type=F32
        )
        weight = jnp.where(allowed, jnp.exp(score * (1.0 / math.sqrt(HEAD))), 0.0)
        den = jnp.sum(weight, axis=1, keepdims=True)
        high = den.astype(BF).astype(F32)
        sums = sums + jnp.where(lane == h, high, 0.0) + jnp.where(lane == heads + h, den - high, 0.0)
        out_ref[:, span] = dot(weight.astype(BF), v).astype(BF)
    out_ref[:, heads * HEAD :] = sums.astype(BF)


def combine_kernel(parts_ref, sel_ref, out_ref):
    sel = sel_ref[...].astype(F32)
    parts = parts_ref[...]
    heads = out_ref.shape[2] // HEAD // 2
    for part in range(2):
        mine = jnp.where(half_of(sel.shape) == part, sel, 0.0).astype(BF)
        total = lax.dot_general(mine, parts, (((0,), (0,)), ((), ())), preferred_element_type=F32)
        sums = total[:, heads * HEAD :]
        for h in range(heads):
            den = sums[:, h : h + 1] + sums[:, heads + h : heads + h + 1]
            mixed = total[:, h * HEAD : (h + 1) * HEAD] / jnp.where(den > 0.0, den, 1.0)
            mixed = jnp.broadcast_to(mixed.astype(BF)[None], (out_ref.shape[0],) + mixed.shape)
            at = (part * heads + h) * HEAD
            out_ref[:, :, at : at + HEAD] = mixed


def gate_up_kernel(m0, m1, m2, m3, w0, w1, gate2, up2, w3, out_ref):
    blocks = (m0, m1, m2, m3)
    units = gate2.shape[1]
    columns = 2 * units
    for start in range(0, columns, HEAD):
        span = slice(start, start + HEAD)
        part = slice(start % units, start % units + HEAD)
        w2 = gate2 if start < units else up2
        total = dot(m0[...], w0[:, span]) + dot(m1[...], w1[:, span])
        total = total + dot(m2[...], w2[:, part]) + dot(m3[...], w3[:, span])
        out_ref[:, span] = total.astype(BF)
    square = jnp.zeros((m0.shape[0], 1), F32)
    for m in blocks:
        value = m[...].astype(F32)
        square = square + jnp.sum(value * value, axis=1, keepdims=True)
    high = square.astype(BF).astype(F32)
    lane = lax.broadcasted_iota(jnp.int32, (m0.shape[0], HEAD), 1)
    extra = jnp.where(lane == 0, high, jnp.where(lane == 1, square - high, 0.0))
    out_ref[:, columns:] = extra.astype(BF)


def active_kernel(full_width, parts_ref, out_ref):
    total = jnp.sum(parts_ref[...].astype(F32), axis=0)
    units = out_ref.shape[2]
    square = total[:, 2 * units : 2 * units + 1] + total[:, 2 * units + 1 : 2 * units + 2]
    scale = lax.rsqrt(square * (1.0 / full_width) + EPS)
    gate = total[:, :units] * scale
    up = total[:, units : 2 * units] * scale
    active = (gate / (1.0 + jnp.exp(-gate)) * up).astype(BF)
    out_ref[...] = jnp.broadcast_to(active[None], out_ref.shape)


def shift(value, axis, by):
    n = lax.axis_size(axis)
    return lax.ppermute(value, axis, [(i, (i + by) % n) for i in range(n)])


def after(value, *others):
    return lax.optimization_barrier((value,) + others)[0]


def exchange(value, axis):
    n = lax.axis_size(axis)
    out = lax.all_to_all(value, axis, 0, 0, tiled=True)
    return out.reshape((n, value.shape[0] // n) + value.shape[1:])


def tensor_sum(part):
    part = part.astype(BF)
    pair = (part.astype(F32) + shift(part, "c", 1).astype(F32)).astype(BF)
    ahead, behind, across = shift(pair, "x", 1), shift(pair, "x", -1), shift(pair, "x", 2)
    return (pair.astype(F32) + across.astype(F32)) + (ahead.astype(F32) + behind.astype(F32))


def shards(
    hidden,
    vision,
    attn_gain,
    q_weight,
    k_weight,
    v_weight,
    q_gain,
    k_gain,
    o_weight,
    gate_logits,
    mlp_gain,
    gate_weight,
    up_weight,
    down_weight,
    image_tiles,
    image_groups,
    image_requests,
):
    groups = lax.axis_size("z") * lax.axis_size("y")
    me = (lax.axis_index("z") * lax.axis_size("y") + lax.axis_index("y")).astype(jnp.int32).reshape(1)
    place = jnp.stack((lax.axis_index("x"), lax.axis_index("c"))).astype(jnp.int32)
    all_rows, width_part = hidden.shape
    own_rows = all_rows // groups
    full_width = width_part * groups
    local_heads = q_weight.shape[1]
    hidden_part = gate_weight.shape[1]
    slot_rows = groups * 2 * SLOTS * STEPS
    key_rows = vision.shape[0]

    sel, row_image = pl.pallas_call(
        route_kernel,
        in_specs=[smem(), vmem(), vmem()],
        out_specs=[vmem(), vmem()],
        out_shape=[
            jax.ShapeDtypeStruct((slot_rows, own_rows), BF),
            jax.ShapeDtypeStruct((slot_rows, 1), jnp.int32),
        ],
        compiler_params=params(),
    )(me, image_groups.reshape(groups, -1), image_requests.reshape(groups, -1))

    hidden_f = hidden.astype(F32)
    normed = (hidden_f * attn_gain).astype(BF)
    q_part = dot(normed, q_weight).astype(BF)
    q_part, vision = lax.optimization_barrier((q_part, vision))
    q_parts = exchange(q_part, GROUP)

    there = kv_project(place, vision, k_weight, v_weight)
    low, high, ahead, behind, own = kv_project(place, vision, k_weight, v_weight, shift(there, "c", 1))
    q_parts = after(q_parts, own)
    forward, backward = pl.pallas_call(
        kv_merge_kernel,
        in_specs=[vmem()] * 4,
        out_specs=[vmem()] * 2,
        out_shape=[jax.ShapeDtypeStruct(ahead.shape, BF)] * 2,
        compiler_params=params(),
    )(ahead, behind, shift(low, "x", 1), shift(high, "x", -1))
    kv_left = shift(forward, "x", 1)
    kv_right = shift(backward, "x", -1)

    queries = pl.pallas_call(
        query_kernel,
        in_specs=[vmem()] * 3,
        out_specs=vmem(),
        out_shape=jax.ShapeDtypeStruct((slot_rows, local_heads // 2), BF),
        compiler_params=params(),
    )(q_parts, sel, q_gain.reshape(1, HEAD))
    chips_y = lax.axis_size("y")
    units = hidden_part // chips_y
    half = units // 2
    gain = mlp_gain[:, None]
    queries = after(queries, forward, backward)
    gate_weight, up_weight = lax.optimization_barrier((gate_weight, up_weight, queries))[:2]

    def columns(weight, d):
        at = lax.rem(lax.axis_index("y") + d, chips_y) * units
        return lax.dynamic_slice_in_dim(weight, at, units, 1).astype(F32)

    def wide(*parts):
        return (jnp.concatenate(parts, axis=1) * gain).astype(BF)

    wide_0 = wide(columns(gate_weight, 0), columns(up_weight, 0))
    wide_1 = shift(wide(columns(gate_weight, 1), columns(up_weight, 1)), "y", 1)
    wide_3 = shift(wide(columns(gate_weight, 3), columns(up_weight, 3)), "y", -1)
    gate_2 = shift(wide(columns(gate_weight, 2)), "y", 1)
    up_2 = shift(wide(columns(up_weight, 2)), "y", -1)

    queries = lax.all_to_all(queries, GROUP, 0, 0, tiled=True)

    mixed = pl.pallas_call(
        attention_kernel,
        in_specs=[smem(), smem()] + [vmem()] * 6,
        out_specs=vmem(),
        out_shape=jax.ShapeDtypeStruct((slot_rows, local_heads // 2 + HEAD), BF),
        compiler_params=params(),
    )(me, image_tiles, own, kv_left, kv_right, k_gain.reshape(1, HEAD), queries, row_image)
    down_weight = after(down_weight, mixed)

    def rows(d, start, size):
        at = lax.rem(lax.axis_index("y") + d, chips_y) * units + start
        return lax.dynamic_slice_in_dim(down_weight, at, size, 0)

    down_0 = rows(0, 0, units)
    down_1 = shift(rows(1, 0, units), "y", 1)
    down_3 = shift(rows(3, 0, units), "y", -1)
    down_2 = (shift(rows(2, 0, half), "y", 1), shift(rows(2, half, half), "y", -1))
    mixed = lax.all_to_all(mixed, GROUP, 0, 0, tiled=True)
    mixed = after(mixed, wide_1, wide_3, gate_2, up_2)
    gate_2, up_2 = shift(gate_2, "y", 1), shift(up_2, "y", -1)

    attended = pl.pallas_call(
        combine_kernel,
        in_specs=[vmem()] * 2,
        out_specs=vmem(),
        out_shape=jax.ShapeDtypeStruct((groups, own_rows, local_heads), BF),
        compiler_params=params(),
    )(mixed, sel)
    attended = lax.all_to_all(attended, GROUP, 0, 0, tiled=True).reshape(all_rows, local_heads)

    attended = after(attended, gate_2, up_2, *down_2)
    attn_sum = tensor_sum(dot(attended, o_weight))
    middle = (hidden_f + jnp.tanh(gate_logits[0]) * attn_sum).astype(BF)
    middle_f = middle.astype(F32)
    middle = after(middle, down_1, down_3)
    down_2 = (shift(down_2[0], "y", 1), shift(down_2[1], "y", -1))
    middles = [middle] + [shift(middle, "y", d) for d in (1, 2, 3)]
    gate_up = pl.pallas_call(
        gate_up_kernel,
        in_specs=[vmem()] * 9,
        out_specs=vmem(),
        out_shape=jax.ShapeDtypeStruct((all_rows, 2 * units + HEAD), BF),
        compiler_params=params(),
    )(*middles, wide_0, wide_1, gate_2, up_2, wide_3)
    parts = after(exchange(gate_up, "z"), *down_2)
    active = pl.pallas_call(
        functools.partial(active_kernel, full_width),
        in_specs=[vmem()],
        out_specs=vmem(),
        out_shape=jax.ShapeDtypeStruct(parts.shape[:2] + (units,), BF),
        compiler_params=params(),
    )(parts)
    active = lax.all_to_all(active, "z", 0, 0, tiled=True).reshape(all_rows, units)
    across = dot(active[:, :half], down_2[0]) + dot(active[:, half:], down_2[1])
    across = shift(across.astype(BF), "y", 2)
    behind = shift(dot(active, down_1).astype(BF), "y", -1)
    ahead = shift(dot(active, down_3).astype(BF), "y", 1)
    down_part = dot(active, down_0) + across.astype(F32) + behind.astype(F32) + ahead.astype(F32)
    down_sum = tensor_sum(down_part)
    row_request = jnp.arange(all_rows, dtype=jnp.int32) // STEPS
    request_ids = (image_groups * (own_rows // STEPS) + image_requests).reshape(-1)
    has_image = jnp.any(row_request[:, None] == request_ids[None, :], axis=1).astype(F32)
    return (middle_f + jnp.tanh(gate_logits[1]) * has_image[:, None] * down_sum).astype(BF)


def solution(mesh):
    fine = Mesh(mesh.devices.reshape(8, 4, 4, 2), GROUP + TENSOR)
    in_specs = (
        P(None, GROUP),
        P(GROUP, TENSOR),
        P(GROUP),
        P(GROUP, TENSOR),
        P(TENSOR, None),
        P(TENSOR, None),
        P(),
        P(),
        P(TENSOR, GROUP),
        P(),
        P(GROUP),
        P(GROUP, TENSOR),
        P(GROUP, TENSOR),
        P(TENSOR, GROUP),
        P(),
        P(),
        P(),
    )
    return jax.shard_map(shards, mesh=fine, in_specs=in_specs, out_specs=P(None, GROUP), check_vma=False)
```

```python
import functools
import math

import jax
import jax.numpy as jnp
from jax import lax
from jax.experimental import pallas as pl
from jax.experimental.pallas import tpu as pltpu
from jax.sharding import Mesh
from jax.sharding import PartitionSpec as P

GROUP = ("z", "y")
TENSOR = ("x", "c")
HEAD = 128
SLOTS = 2
STEPS = 2
EPS = 1e-05
VMEM_BYTES = 16 * 1024 * 1024
LARGE_VMEM_BYTES = 58 * 1024 * 1024
BF = jnp.bfloat16
F32 = jnp.float32


def params(limit=VMEM_BYTES):
    return pltpu.CompilerParams(vmem_limit_bytes=limit)


def dot(a, b):
    return jnp.dot(a, b, preferred_element_type=F32)


def vmem():
    return pl.BlockSpec(memory_space=pltpu.VMEM)


def smem():
    return pl.BlockSpec(memory_space=pltpu.SMEM)


def route_kernel(me_ref, routes_ref, requests_ref, sel_ref, image_ref):
    me = me_ref[0]
    groups, links = routes_ref.shape
    rows = groups * 2 * SLOTS * STEPS
    row = lax.broadcasted_iota(jnp.int32, (rows, links), 0)
    lane = lax.broadcasted_iota(jnp.int32, (rows, links), 1)
    group_of_row = row >> 3
    slot = (row >> 1) & 1
    step = row & 1
    spread = (group_of_row == lane).astype(F32)
    link = lax.broadcasted_iota(jnp.int32, (groups, links), 1)
    code = (link * 4 + requests_ref[...]).astype(F32)
    route_rows = dot(spread, routes_ref[...].astype(F32))
    code_rows = dot(spread, code)
    hit = route_rows == me.astype(F32)
    first = jnp.min(jnp.where(hit, code_rows, 1e4), axis=1, keepdims=True)
    last = jnp.max(jnp.where(hit, code_rows, -1.0), axis=1, keepdims=True)
    slot1, step1 = slot[:, :1], step[:, :1]
    chosen = jnp.where(slot1 == 0, first, last).astype(jnp.int32)
    found_first = jnp.where(first < 1e3, 1, 0)
    found_last = jnp.where(last > first, 1, 0)
    found = jnp.where(slot1 == 0, found_first, found_last)
    wanted = jnp.where(found == 1, (chosen & 3) * STEPS + step1, -1)
    sel_ref[...] = jnp.where(lane[:, :8] == wanted, 1.0, 0.0).astype(BF)
    mine = routes_ref[pl.ds(me, 1), :]
    here = mine == group_of_row
    first_link = jnp.min(jnp.where(here, lane, 1000), axis=1, keepdims=True)
    last_link = jnp.max(jnp.where(here, lane, -1), axis=1, keepdims=True)
    first_image = jnp.where(first_link < 1000, first_link >> 3, -1)
    last_image = jnp.where(last_link > first_link, last_link >> 3, -1)
    image_ref[...] = jnp.where(slot1 == 0, first_image, last_image)


def kv_there_kernel(place_ref, k_ref, v_ref, out_ref):
    out_ref[0, :, :HEAD] = k_ref[...]
    out_ref[0, :, HEAD:] = v_ref[...]


def kv_here_kernel(place_ref, k_ref, v_ref, core_ref, low_ref, high_ref, ahead_ref, behind_ref, own_ref):
    total = jnp.concatenate((k_ref[...], v_ref[...]), axis=1).astype(F32)
    total = (total + core_ref[0].astype(F32)).astype(BF)
    half = low_ref.shape[0]
    step = pl.program_id(0)

    @pl.when(step == 0)
    def _():
        low_ref[...] = total[:half]
        high_ref[...] = total[half:]

    @pl.when(step == 1)
    def _():
        ahead_ref[...] = total

    @pl.when(step == 2)
    def _():
        behind_ref[...] = total

    @pl.when(step == 3)
    def _():
        own_ref[...] = total


def kv_split(place, k_part, v_part, from_core=None):
    rows = k_part.shape[0]
    chips = 4
    other = from_core is None

    def head(d, place_ref):
        core = place_ref[1]
        ahead = jnp.where(d == 0, 2, jnp.where(d == 1, 1, jnp.where(d == 2, 3, 0)))
        return 0, lax.rem(place_ref[0] + ahead, chips) * 2 + (1 - core if other else core)

    one = pl.BlockSpec((1, rows, 2 * HEAD), lambda d, p: (d, 0, 0))
    sizes = [rows // 2, rows // 2, rows, rows, rows]
    whole = [pl.BlockSpec((n, 2 * HEAD), lambda d, p: (0, 0)) for n in sizes]
    return pl.pallas_call(
        kv_there_kernel if other else kv_here_kernel,
        grid_spec=pltpu.PrefetchScalarGridSpec(
            num_scalar_prefetch=1,
            grid=(chips,),
            in_specs=[pl.BlockSpec((rows, HEAD), head)] * 2 + ([] if other else [one]),
            out_specs=one if other else whole,
        ),
        out_shape=jax.ShapeDtypeStruct((chips, rows, 2 * HEAD), BF)
        if other
        else [jax.ShapeDtypeStruct((n, 2 * HEAD), BF) for n in sizes],
        compiler_params=params(LARGE_VMEM_BYTES),
    )(place, k_part, v_part, *(() if other else (from_core,)))


def kv_merge_kernel(ahead_ref, behind_ref, low_ref, high_ref, forward_ref, backward_ref):
    half = low_ref.shape[0]
    forward_ref[:half] = (ahead_ref[:half].astype(F32) + low_ref[...].astype(F32)).astype(BF)
    forward_ref[half:] = ahead_ref[half:]
    backward_ref[:half] = behind_ref[:half]
    backward_ref[half:] = (behind_ref[half:].astype(F32) + high_ref[...].astype(F32)).astype(BF)


def half_of(shape):
    return (lax.broadcasted_iota(jnp.int32, shape, 0) >> 2) & 1


def query_kernel(parts_ref, sel_ref, gain_ref, out_ref):
    total = jnp.sum(parts_ref[...].astype(F32), axis=0)
    gain = gain_ref[...]
    sel = sel_ref[...]
    heads = total.shape[1] // HEAD // 2
    upper = half_of((sel.shape[0], HEAD)) == 1

    def chosen(h):
        v = total[:, h * HEAD : (h + 1) * HEAD]
        scale = lax.rsqrt(jnp.mean(v * v, axis=1, keepdims=True) + EPS)
        return dot(sel, (v * scale * gain).astype(BF))

    for h in range(heads):
        out_ref[:, h * HEAD : (h + 1) * HEAD] = jnp.where(upper, chosen(heads + h), chosen(h)).astype(BF)


def attention_kernel(me_ref, tiles_ref, own_ref, left_ref, right_ref, gain_ref, q_ref, image_ref, out_ref):
    me = me_ref[0]
    total = own_ref[...].astype(F32) + left_ref[...].astype(F32) + right_ref[...].astype(F32)
    k = total[:, :HEAD]
    scale = lax.rsqrt(jnp.mean(k * k, axis=1, keepdims=True) + EPS)
    k = (k * scale * gain_ref[...]).astype(BF)
    v = total[:, HEAD:].astype(BF)
    rows, keys = q_ref.shape[0], k.shape[0]
    tile = lax.broadcasted_iota(jnp.int32, (1, keys), 1) >> 6
    owner = jnp.zeros((1, keys), jnp.int32)
    end = jnp.int32(0)
    for j in range(4):
        end = end + tiles_ref[me, j]
        owner = owner + (tile >= end).astype(jnp.int32)
    allowed = owner == image_ref[...]
    lane = lax.broadcasted_iota(jnp.int32, (rows, HEAD), 1)
    sums = jnp.zeros((rows, HEAD), F32)
    heads = q_ref.shape[1] // HEAD
    for h in range(heads):
        span = slice(h * HEAD, (h + 1) * HEAD)
        score = lax.dot_general(
            q_ref[:, span], k, (((1,), (1,)), ((), ())), preferred_element_type=F32
        )
        weight = jnp.where(allowed, jnp.exp(score * (1.0 / math.sqrt(HEAD))), 0.0)
        den = jnp.sum(weight, axis=1, keepdims=True)
        high = den.astype(BF).astype(F32)
        sums = sums + jnp.where(lane == h, high, 0.0) + jnp.where(lane == heads + h, den - high, 0.0)
        out_ref[:, span] = dot(weight.astype(BF), v).astype(BF)
    out_ref[:, heads * HEAD :] = sums.astype(BF)


def combine_kernel(parts_ref, sel_ref, out_ref):
    sel = sel_ref[...].astype(F32)
    parts = parts_ref[...]
    heads = out_ref.shape[2] // HEAD // 2
    for part in range(2):
        mine = jnp.where(half_of(sel.shape) == part, sel, 0.0).astype(BF)
        total = lax.dot_general(mine, parts, (((0,), (0,)), ((), ())), preferred_element_type=F32)
        sums = total[:, heads * HEAD :]
        for h in range(heads):
            den = sums[:, h : h + 1] + sums[:, heads + h : heads + h + 1]
            mixed = total[:, h * HEAD : (h + 1) * HEAD] / jnp.where(den > 0.0, den, 1.0)
            mixed = jnp.broadcast_to(mixed.astype(BF)[None], (out_ref.shape[0],) + mixed.shape)
            at = (part * heads + h) * HEAD
            out_ref[:, :, at : at + HEAD] = mixed


def gate_up_kernel(m0, m1, m2, m3, w0, w1, gate2, up2, w3, out_ref):
    blocks = (m0, m1, m2, m3)
    units = gate2.shape[1]
    columns = 2 * units
    for start in range(0, columns, HEAD):
        span = slice(start, start + HEAD)
        part = slice(start % units, start % units + HEAD)
        w2 = gate2 if start < units else up2
        total = dot(m0[...], w0[:, span]) + dot(m1[...], w1[:, span])
        total = total + dot(m2[...], w2[:, part]) + dot(m3[...], w3[:, span])
        out_ref[:, span] = total.astype(BF)
    square = jnp.zeros((m0.shape[0], 1), F32)
    for m in blocks:
        value = m[...].astype(F32)
        square = square + jnp.sum(value * value, axis=1, keepdims=True)
    high = square.astype(BF).astype(F32)
    lane = lax.broadcasted_iota(jnp.int32, (m0.shape[0], HEAD), 1)
    extra = jnp.where(lane == 0, high, jnp.where(lane == 1, square - high, 0.0))
    out_ref[:, columns:] = extra.astype(BF)


def active_kernel(full_width, parts_ref, out_ref):
    total = jnp.sum(parts_ref[...].astype(F32), axis=0)
    units = out_ref.shape[2]
    square = total[:, 2 * units : 2 * units + 1] + total[:, 2 * units + 1 : 2 * units + 2]
    scale = lax.rsqrt(square * (1.0 / full_width) + EPS)
    gate = total[:, :units] * scale
    up = total[:, units : 2 * units] * scale
    active = (gate / (1.0 + jnp.exp(-gate)) * up).astype(BF)
    out_ref[...] = jnp.broadcast_to(active[None], out_ref.shape)


def shift(value, axis, by):
    n = lax.axis_size(axis)
    return lax.ppermute(value, axis, [(i, (i + by) % n) for i in range(n)])


def after(value, *others):
    return lax.optimization_barrier((value,) + others)[0]


def exchange(value, axis):
    n = lax.axis_size(axis)
    out = lax.all_to_all(value, axis, 0, 0, tiled=True)
    return out.reshape((n, value.shape[0] // n) + value.shape[1:])


def tensor_sum(part):
    part = part.astype(BF)
    pair = (part.astype(F32) + shift(part, "c", 1).astype(F32)).astype(BF)
    ahead, behind, across = shift(pair, "x", 1), shift(pair, "x", -1), shift(pair, "x", 2)
    return (pair.astype(F32) + across.astype(F32)) + (ahead.astype(F32) + behind.astype(F32))


def shards(
    hidden,
    vision,
    attn_gain,
    q_weight,
    k_weight,
    v_weight,
    q_gain,
    k_gain,
    o_weight,
    gate_logits,
    mlp_gain,
    gate_weight,
    up_weight,
    down_weight,
    image_tiles,
    image_groups,
    image_requests,
):
    groups = lax.axis_size("z") * lax.axis_size("y")
    me = (lax.axis_index("z") * lax.axis_size("y") + lax.axis_index("y")).astype(jnp.int32).reshape(1)
    place = jnp.stack((lax.axis_index("x"), lax.axis_index("c"))).astype(jnp.int32)
    all_rows, width_part = hidden.shape
    own_rows = all_rows // groups
    full_width = width_part * groups
    local_heads = q_weight.shape[1]
    hidden_part = gate_weight.shape[1]
    slot_rows = groups * 2 * SLOTS * STEPS
    key_rows = vision.shape[0]

    sel, row_image = pl.pallas_call(
        route_kernel,
        in_specs=[smem(), vmem(), vmem()],
        out_specs=[vmem(), vmem()],
        out_shape=[
            jax.ShapeDtypeStruct((slot_rows, own_rows), BF),
            jax.ShapeDtypeStruct((slot_rows, 1), jnp.int32),
        ],
        compiler_params=params(),
    )(me, image_groups.reshape(groups, -1), image_requests.reshape(groups, -1))

    hidden_f = hidden.astype(F32)
    normed = (hidden_f * attn_gain).astype(BF)
    q_part = dot(normed, q_weight).astype(BF)
    q_part, vision = lax.optimization_barrier((q_part, vision))
    q_parts = exchange(q_part, GROUP)

    k_part = dot(vision, k_weight).astype(BF)
    v_part = dot(vision, v_weight).astype(BF)
    there = kv_split(place, k_part, v_part)
    low, high, ahead, behind, own = kv_split(place, k_part, v_part, shift(there, "c", 1))
    q_parts = after(q_parts, own)
    forward, backward = pl.pallas_call(
        kv_merge_kernel,
        in_specs=[vmem()] * 4,
        out_specs=[vmem()] * 2,
        out_shape=[jax.ShapeDtypeStruct(ahead.shape, BF)] * 2,
        compiler_params=params(),
    )(ahead, behind, shift(low, "x", 1), shift(high, "x", -1))
    kv_left = shift(forward, "x", 1)
    kv_right = shift(backward, "x", -1)

    chips_y = lax.axis_size("y")
    units = hidden_part // chips_y
    half = units // 2
    gain = mlp_gain[:, None]

    def columns(weight, d):
        at = lax.rem(lax.axis_index("y") + d, chips_y) * units
        return lax.dynamic_slice_in_dim(weight, at, units, 1).astype(F32)

    def wide(*parts):
        return (jnp.concatenate(parts, axis=1) * gain).astype(BF)

    first_gate, first_up = lax.optimization_barrier((gate_weight, up_weight, own))[:2]
    gate_2 = shift(wide(columns(first_gate, 2)), "y", 1)
    up_2 = shift(wide(columns(first_up, 2)), "y", -1)

    queries = pl.pallas_call(
        query_kernel,
        in_specs=[vmem()] * 3,
        out_specs=vmem(),
        out_shape=jax.ShapeDtypeStruct((slot_rows, local_heads // 2), BF),
        compiler_params=params(),
    )(q_parts, sel, q_gain.reshape(1, HEAD))
    queries = after(queries, forward, backward)
    later_gate, later_up = lax.optimization_barrier((gate_weight, up_weight, queries))[:2]
    wide_0 = wide(columns(later_gate, 0), columns(later_up, 0))
    wide_1 = shift(wide(columns(later_gate, 1), columns(later_up, 1)), "y", 1)
    wide_3 = shift(wide(columns(later_gate, 3), columns(later_up, 3)), "y", -1)
    queries = lax.all_to_all(queries, GROUP, 0, 0, tiled=True)
    queries = after(queries, gate_2, up_2)
    gate_2, up_2 = shift(gate_2, "y", 1), shift(up_2, "y", -1)

    mixed = pl.pallas_call(
        attention_kernel,
        in_specs=[smem(), smem()] + [vmem()] * 6,
        out_specs=vmem(),
        out_shape=jax.ShapeDtypeStruct((slot_rows, local_heads // 2 + HEAD), BF),
        compiler_params=params(),
    )(me, image_tiles, own, kv_left, kv_right, k_gain.reshape(1, HEAD), queries, row_image)
    down_weight = after(down_weight, mixed)

    def rows(d, start, size):
        at = lax.rem(lax.axis_index("y") + d, chips_y) * units + start
        return lax.dynamic_slice_in_dim(down_weight, at, size, 0)

    down_0 = rows(0, 0, units)
    down_1 = shift(rows(1, 0, units), "y", 1)
    down_3 = shift(rows(3, 0, units), "y", -1)
    down_2 = (shift(rows(2, 0, half), "y", 1), shift(rows(2, half, half), "y", -1))
    mixed = lax.all_to_all(mixed, GROUP, 0, 0, tiled=True)
    mixed = after(mixed, wide_1, wide_3)

    attended = pl.pallas_call(
        combine_kernel,
        in_specs=[vmem()] * 2,
        out_specs=vmem(),
        out_shape=jax.ShapeDtypeStruct((groups, own_rows, local_heads), BF),
        compiler_params=params(),
    )(mixed, sel)
    attended = lax.all_to_all(attended, GROUP, 0, 0, tiled=True).reshape(all_rows, local_heads)

    attended = after(attended, gate_2, up_2)
    attn_sum = tensor_sum(dot(attended, o_weight))
    middle = (hidden_f + jnp.tanh(gate_logits[0]) * attn_sum).astype(BF)
    middle_f = middle.astype(F32)
    middle = after(middle, down_1, down_3, *down_2)
    down_2 = (shift(down_2[0], "y", 1), shift(down_2[1], "y", -1))
    middles = [middle] + [shift(middle, "y", d) for d in (1, 2, 3)]
    gate_up = pl.pallas_call(
        gate_up_kernel,
        in_specs=[vmem()] * 9,
        out_specs=vmem(),
        out_shape=jax.ShapeDtypeStruct((all_rows, 2 * units + HEAD), BF),
        compiler_params=params(),
    )(*middles, wide_0, wide_1, gate_2, up_2, wide_3)
    parts = after(exchange(gate_up, "z"), *down_2)
    active = pl.pallas_call(
        functools.partial(active_kernel, full_width),
        in_specs=[vmem()],
        out_specs=vmem(),
        out_shape=jax.ShapeDtypeStruct(parts.shape[:2] + (units,), BF),
        compiler_params=params(),
    )(parts)
    active = lax.all_to_all(active, "z", 0, 0, tiled=True).reshape(all_rows, units)
    across = dot(active[:, :half], down_2[0]) + dot(active[:, half:], down_2[1])
    across = shift(across.astype(BF), "y", 2)
    behind = shift(dot(active, down_1).astype(BF), "y", -1)
    ahead = shift(dot(active, down_3).astype(BF), "y", 1)
    down_part = dot(active, down_0) + across.astype(F32) + behind.astype(F32) + ahead.astype(F32)
    down_sum = tensor_sum(down_part)
    row_request = jnp.arange(all_rows, dtype=jnp.int32) // STEPS
    request_ids = (image_groups * (own_rows // STEPS) + image_requests).reshape(-1)
    has_image = jnp.any(row_request[:, None] == request_ids[None, :], axis=1).astype(F32)
    return (middle_f + jnp.tanh(gate_logits[1]) * has_image[:, None] * down_sum).astype(BF)


def solution(mesh):
    fine = Mesh(mesh.devices.reshape(8, 4, 4, 2), GROUP + TENSOR)
    in_specs = (
        P(None, GROUP),
        P(GROUP, TENSOR),
        P(GROUP),
        P(GROUP, TENSOR),
        P(TENSOR, None),
        P(TENSOR, None),
        P(),
        P(),
        P(TENSOR, GROUP),
        P(),
        P(GROUP),
        P(GROUP, TENSOR),
        P(GROUP, TENSOR),
        P(TENSOR, GROUP),
        P(),
        P(),
        P(),
    )
    return jax.shard_map(shards, mesh=fine, in_specs=in_specs, out_specs=P(None, GROUP), check_vma=False)
```

```python
import functools
import math

import jax
import jax.numpy as jnp
from jax import lax
from jax.experimental import pallas as pl
from jax.experimental.pallas import tpu as pltpu
from jax.sharding import Mesh
from jax.sharding import PartitionSpec as P

GROUP = ("z", "y")
TENSOR = ("x", "c")
HEAD = 128
SLOTS = 2
STEPS = 2
EPS = 1e-05
VMEM_BYTES = 16 * 1024 * 1024
LARGE_VMEM_BYTES = 58 * 1024 * 1024
BF = jnp.bfloat16
F32 = jnp.float32


def params(limit=VMEM_BYTES):
    return pltpu.CompilerParams(vmem_limit_bytes=limit)


def dot(a, b):
    return jnp.dot(a, b, preferred_element_type=F32)


def vmem():
    return pl.BlockSpec(memory_space=pltpu.VMEM)


def smem():
    return pl.BlockSpec(memory_space=pltpu.SMEM)


def route_kernel(me_ref, routes_ref, requests_ref, sel_ref, image_ref):
    me = me_ref[0]
    groups, links = routes_ref.shape
    rows = groups * 2 * SLOTS * STEPS
    row = lax.broadcasted_iota(jnp.int32, (rows, links), 0)
    lane = lax.broadcasted_iota(jnp.int32, (rows, links), 1)
    group_of_row = row >> 3
    slot = (row >> 1) & 1
    step = row & 1
    spread = (group_of_row == lane).astype(F32)
    link = lax.broadcasted_iota(jnp.int32, (groups, links), 1)
    code = (link * 4 + requests_ref[...]).astype(F32)
    route_rows = dot(spread, routes_ref[...].astype(F32))
    code_rows = dot(spread, code)
    hit = route_rows == me.astype(F32)
    first = jnp.min(jnp.where(hit, code_rows, 1e4), axis=1, keepdims=True)
    last = jnp.max(jnp.where(hit, code_rows, -1.0), axis=1, keepdims=True)
    slot1, step1 = slot[:, :1], step[:, :1]
    chosen = jnp.where(slot1 == 0, first, last).astype(jnp.int32)
    found_first = jnp.where(first < 1e3, 1, 0)
    found_last = jnp.where(last > first, 1, 0)
    found = jnp.where(slot1 == 0, found_first, found_last)
    wanted = jnp.where(found == 1, (chosen & 3) * STEPS + step1, -1)
    sel_ref[...] = jnp.where(lane[:, :8] == wanted, 1.0, 0.0).astype(BF)
    mine = routes_ref[pl.ds(me, 1), :]
    here = mine == group_of_row
    first_link = jnp.min(jnp.where(here, lane, 1000), axis=1, keepdims=True)
    last_link = jnp.max(jnp.where(here, lane, -1), axis=1, keepdims=True)
    first_image = jnp.where(first_link < 1000, first_link >> 3, -1)
    last_image = jnp.where(last_link > first_link, last_link >> 3, -1)
    image_ref[...] = jnp.where(slot1 == 0, first_image, last_image)


def kv_kernel(place_ref, x0, x1, k0, v0, k1, v1, low_ref, high_ref, ahead_ref, behind_ref, own_ref):
    total = dot(x0[...], jnp.concatenate((k0[...], v0[...]), axis=1))
    total = total + dot(x1[...], jnp.concatenate((k1[...], v1[...]), axis=1))
    total = total.astype(BF)
    half = low_ref.shape[0]
    step = pl.program_id(0)

    @pl.when(step == 0)
    def _():
        low_ref[...] = total[:half]
        high_ref[...] = total[half:]

    @pl.when(step == 1)
    def _():
        ahead_ref[...] = total

    @pl.when(step == 2)
    def _():
        behind_ref[...] = total

    @pl.when(step == 3)
    def _():
        own_ref[...] = total


def kv_project(place, vision, k_weight, v_weight):
    rows, depth = vision.shape
    chips = 4

    def head(d, place_ref):
        ahead = jnp.where(d == 0, 2, jnp.where(d == 1, 1, jnp.where(d == 2, 3, 0)))
        return 0, lax.rem(place_ref[0] + ahead, chips) * 2 + place_ref[1]

    states = pl.BlockSpec((rows, depth), lambda d, p: (0, 0))
    weights = pl.BlockSpec((depth, HEAD), head)
    sizes = [rows // 2, rows // 2, rows, rows, rows]
    return pl.pallas_call(
        kv_kernel,
        grid_spec=pltpu.PrefetchScalarGridSpec(
            num_scalar_prefetch=1,
            grid=(chips,),
            in_specs=[states] * 2 + [weights] * 4,
            out_specs=[pl.BlockSpec((n, 2 * HEAD), lambda d, p: (0, 0)) for n in sizes],
        ),
        out_shape=[jax.ShapeDtypeStruct((n, 2 * HEAD), BF) for n in sizes],
        compiler_params=params(LARGE_VMEM_BYTES),
    )(
        place,
        vision,
        shift(vision, "c", 1),
        k_weight,
        v_weight,
        shift(k_weight, "c", 1),
        shift(v_weight, "c", 1),
    )


def kv_merge_kernel(ahead_ref, behind_ref, low_ref, high_ref, forward_ref, backward_ref):
    half = low_ref.shape[0]
    forward_ref[:half] = (ahead_ref[:half].astype(F32) + low_ref[...].astype(F32)).astype(BF)
    forward_ref[half:] = ahead_ref[half:]
    backward_ref[:half] = behind_ref[:half]
    backward_ref[half:] = (behind_ref[half:].astype(F32) + high_ref[...].astype(F32)).astype(BF)


def half_of(shape):
    return (lax.broadcasted_iota(jnp.int32, shape, 0) >> 2) & 1


def query_kernel(parts_ref, sel_ref, gain_ref, out_ref):
    total = jnp.sum(parts_ref[...].astype(F32), axis=0)
    gain = gain_ref[...]
    sel = sel_ref[...]
    heads = total.shape[1] // HEAD // 2
    upper = half_of((sel.shape[0], HEAD)) == 1

    def chosen(h):
        v = total[:, h * HEAD : (h + 1) * HEAD]
        scale = lax.rsqrt(jnp.mean(v * v, axis=1, keepdims=True) + EPS)
        return dot(sel, (v * scale * gain).astype(BF))

    for h in range(heads):
        out_ref[:, h * HEAD : (h + 1) * HEAD] = jnp.where(upper, chosen(heads + h), chosen(h)).astype(BF)


def attention_kernel(me_ref, tiles_ref, own_ref, left_ref, right_ref, gain_ref, q_ref, image_ref, out_ref):
    me = me_ref[0]
    total = own_ref[...].astype(F32) + left_ref[...].astype(F32) + right_ref[...].astype(F32)
    k = total[:, :HEAD]
    scale = lax.rsqrt(jnp.mean(k * k, axis=1, keepdims=True) + EPS)
    k = (k * scale * gain_ref[...]).astype(BF)
    v = total[:, HEAD:].astype(BF)
    rows, keys = q_ref.shape[0], k.shape[0]
    tile = lax.broadcasted_iota(jnp.int32, (1, keys), 1) >> 6
    owner = jnp.zeros((1, keys), jnp.int32)
    end = jnp.int32(0)
    for j in range(4):
        end = end + tiles_ref[me, j]
        owner = owner + (tile >= end).astype(jnp.int32)
    allowed = owner == image_ref[...]
    lane = lax.broadcasted_iota(jnp.int32, (rows, HEAD), 1)
    sums = jnp.zeros((rows, HEAD), F32)
    heads = q_ref.shape[1] // HEAD
    for h in range(heads):
        span = slice(h * HEAD, (h + 1) * HEAD)
        score = lax.dot_general(
            q_ref[:, span], k, (((1,), (1,)), ((), ())), preferred_element_type=F32
        )
        weight = jnp.where(allowed, jnp.exp(score * (1.0 / math.sqrt(HEAD))), 0.0)
        den = jnp.sum(weight, axis=1, keepdims=True)
        high = den.astype(BF).astype(F32)
        sums = sums + jnp.where(lane == h, high, 0.0) + jnp.where(lane == heads + h, den - high, 0.0)
        out_ref[:, span] = dot(weight.astype(BF), v).astype(BF)
    out_ref[:, heads * HEAD :] = sums.astype(BF)


def combine_kernel(parts_ref, sel_ref, out_ref):
    sel = sel_ref[...].astype(F32)
    parts = parts_ref[...]
    heads = out_ref.shape[2] // HEAD // 2
    for part in range(2):
        mine = jnp.where(half_of(sel.shape) == part, sel, 0.0).astype(BF)
        total = lax.dot_general(mine, parts, (((0,), (0,)), ((), ())), preferred_element_type=F32)
        sums = total[:, heads * HEAD :]
        for h in range(heads):
            den = sums[:, h : h + 1] + sums[:, heads + h : heads + h + 1]
            mixed = total[:, h * HEAD : (h + 1) * HEAD] / jnp.where(den > 0.0, den, 1.0)
            mixed = jnp.broadcast_to(mixed.astype(BF)[None], (out_ref.shape[0],) + mixed.shape)
            at = (part * heads + h) * HEAD
            out_ref[:, :, at : at + HEAD] = mixed


def gate_up_kernel(m0, m1, m2, m3, w0, w1, gate2, up2, w3, out_ref):
    units = gate2.shape[1]
    step = pl.program_id(0)

    def product(w2):
        total = dot(m0[...], w0[...]) + dot(m1[...], w1[...])
        return (total + dot(m2[...], w2[...]) + dot(m3[...], w3[...])).astype(BF)

    @pl.when(step == 0)
    def _():
        out_ref[:, :units] = product(gate2)

    @pl.when(step == 1)
    def _():
        out_ref[:, units : 2 * units] = product(up2)
        square = jnp.zeros((m0.shape[0], 1), F32)
        for m in (m0, m1, m2, m3):
            value = m[...].astype(F32)
            square = square + jnp.sum(value * value, axis=1, keepdims=True)
        high = square.astype(BF).astype(F32)
        lane = lax.broadcasted_iota(jnp.int32, (m0.shape[0], HEAD), 1)
        extra = jnp.where(lane == 0, high, jnp.where(lane == 1, square - high, 0.0))
        out_ref[:, 2 * units :] = extra.astype(BF)


def down_kernel(a_ref, d0, d1, low2, high2, d3, own_ref, behind_ref, across_ref, ahead_ref):
    active = a_ref[...]
    half = low2.shape[0]
    total = dot(active[:, :half], low2[...]) + dot(active[:, half:], high2[...])
    across_ref[...] = total.astype(BF)
    behind_ref[...] = dot(active, d1[...]).astype(BF)
    ahead_ref[...] = dot(active, d3[...]).astype(BF)
    own_ref[...] = dot(active, d0[...])


def active_kernel(full_width, parts_ref, out_ref):
    total = jnp.sum(parts_ref[...].astype(F32), axis=0)
    units = out_ref.shape[2]
    square = total[:, 2 * units : 2 * units + 1] + total[:, 2 * units + 1 : 2 * units + 2]
    scale = lax.rsqrt(square * (1.0 / full_width) + EPS)
    gate = total[:, :units] * scale
    up = total[:, units : 2 * units] * scale
    active = (gate / (1.0 + jnp.exp(-gate)) * up).astype(BF)
    out_ref[...] = jnp.broadcast_to(active[None], out_ref.shape)


def shift(value, axis, by):
    n = lax.axis_size(axis)
    return lax.ppermute(value, axis, [(i, (i + by) % n) for i in range(n)])


def after(value, *others):
    return lax.optimization_barrier((value,) + others)[0]


def exchange(value, axis):
    n = lax.axis_size(axis)
    out = lax.all_to_all(value, axis, 0, 0, tiled=True)
    return out.reshape((n, value.shape[0] // n) + value.shape[1:])


def tensor_sum(part):
    part = part.astype(BF)
    pair = (part.astype(F32) + shift(part, "c", 1).astype(F32)).astype(BF)
    ahead, behind, across = shift(pair, "x", 1), shift(pair, "x", -1), shift(pair, "x", 2)
    return (pair.astype(F32) + across.astype(F32)) + (ahead.astype(F32) + behind.astype(F32))


def shards(
    hidden,
    vision,
    attn_gain,
    q_weight,
    k_weight,
    v_weight,
    q_gain,
    k_gain,
    o_weight,
    gate_logits,
    mlp_gain,
    gate_weight,
    up_weight,
    down_weight,
    image_tiles,
    image_groups,
    image_requests,
):
    groups = lax.axis_size("z") * lax.axis_size("y")
    me = (lax.axis_index("z") * lax.axis_size("y") + lax.axis_index("y")).astype(jnp.int32).reshape(1)
    place = jnp.stack((lax.axis_index("x"), lax.axis_index("c"))).astype(jnp.int32)
    all_rows, width_part = hidden.shape
    own_rows = all_rows // groups
    full_width = width_part * groups
    local_heads = q_weight.shape[1]
    hidden_part = gate_weight.shape[1]
    slot_rows = groups * 2 * SLOTS * STEPS
    key_rows = vision.shape[0]

    sel, row_image = pl.pallas_call(
        route_kernel,
        in_specs=[smem(), vmem(), vmem()],
        out_specs=[vmem(), vmem()],
        out_shape=[
            jax.ShapeDtypeStruct((slot_rows, own_rows), BF),
            jax.ShapeDtypeStruct((slot_rows, 1), jnp.int32),
        ],
        compiler_params=params(),
    )(me, image_groups.reshape(groups, -1), image_requests.reshape(groups, -1))

    hidden_f = hidden.astype(F32)
    normed = (hidden_f * attn_gain).astype(BF)
    q_part = dot(normed, q_weight).astype(BF)
    q_parts = exchange(q_part, GROUP)

    low, high, ahead, behind, own = kv_project(place, vision, k_weight, v_weight)
    q_parts = after(q_parts, own)
    forward, backward = pl.pallas_call(
        kv_merge_kernel,
        in_specs=[vmem()] * 4,
        out_specs=[vmem()] * 2,
        out_shape=[jax.ShapeDtypeStruct(ahead.shape, BF)] * 2,
        compiler_params=params(),
    )(ahead, behind, shift(low, "x", 1), shift(high, "x", -1))
    kv_left = shift(forward, "x", 1)
    kv_right = shift(backward, "x", -1)

    chips_y = lax.axis_size("y")
    units = hidden_part // chips_y
    half = units // 2
    gain = mlp_gain[:, None]

    def columns(weight, d):
        at = lax.rem(lax.axis_index("y") + d, chips_y) * units
        return lax.dynamic_slice_in_dim(weight, at, units, 1).astype(F32)

    def wide(*parts):
        return (jnp.concatenate(parts, axis=1) * gain).astype(BF)

    first_gate, first_up = lax.optimization_barrier((gate_weight, up_weight, own))[:2]
    gate_2 = shift(wide(columns(first_gate, 2)), "y", 1)
    up_2 = shift(wide(columns(first_up, 2)), "y", -1)

    queries = pl.pallas_call(
        query_kernel,
        in_specs=[vmem()] * 3,
        out_specs=vmem(),
        out_shape=jax.ShapeDtypeStruct((slot_rows, local_heads // 2), BF),
        compiler_params=params(),
    )(q_parts, sel, q_gain.reshape(1, HEAD))
    queries = after(queries, forward, backward)
    later_gate, later_up = lax.optimization_barrier((gate_weight, up_weight, queries))[:2]
    wide_0 = wide(columns(later_gate, 0), columns(later_up, 0))
    wide_1 = shift(wide(columns(later_gate, 1), columns(later_up, 1)), "y", 1)
    wide_3 = shift(wide(columns(later_gate, 3), columns(later_up, 3)), "y", -1)
    queries = lax.all_to_all(queries, GROUP, 0, 0, tiled=True)
    queries = after(queries, gate_2, up_2)
    gate_2, up_2 = shift(gate_2, "y", 1), shift(up_2, "y", -1)

    mixed = pl.pallas_call(
        attention_kernel,
        in_specs=[smem(), smem()] + [vmem()] * 6,
        out_specs=vmem(),
        out_shape=jax.ShapeDtypeStruct((slot_rows, local_heads // 2 + HEAD), BF),
        compiler_params=params(),
    )(me, image_tiles, own, kv_left, kv_right, k_gain.reshape(1, HEAD), queries, row_image)
    down_weight = after(down_weight, mixed)

    def rows(d, start, size):
        at = lax.rem(lax.axis_index("y") + d, chips_y) * units + start
        return lax.dynamic_slice_in_dim(down_weight, at, size, 0)

    down_0, down_1, down_3 = rows(0, 0, units), rows(1, 0, units), rows(3, 0, units)
    down_2 = rows(2, 0, half), rows(2, half, half)
    mixed = lax.all_to_all(mixed, GROUP, 0, 0, tiled=True)
    mixed = after(mixed, wide_1, wide_3, down_1, down_3, *down_2)
    down_1, down_3 = shift(down_1, "y", 1), shift(down_3, "y", -1)
    down_2 = shift(down_2[0], "y", 1), shift(down_2[1], "y", -1)

    attended = pl.pallas_call(
        combine_kernel,
        in_specs=[vmem()] * 2,
        out_specs=vmem(),
        out_shape=jax.ShapeDtypeStruct((groups, own_rows, local_heads), BF),
        compiler_params=params(),
    )(mixed, sel)
    attended = lax.all_to_all(attended, GROUP, 0, 0, tiled=True).reshape(all_rows, local_heads)

    attended = after(attended, gate_2, up_2, *down_2)
    attn_sum = tensor_sum(dot(attended, o_weight))
    middle = (hidden_f + jnp.tanh(gate_logits[0]) * attn_sum).astype(BF)
    middle_f = middle.astype(F32)
    middle = after(middle, down_1, down_3)
    down_2 = (shift(down_2[0], "y", 1), shift(down_2[1], "y", -1))
    middles = [middle] + [shift(middle, "y", d) for d in (1, 2, 3)]
    block = pl.BlockSpec((all_rows, width_part), lambda i: (0, 0))
    direct = pl.BlockSpec((width_part, units), lambda i: (0, i))
    passed = pl.BlockSpec((width_part, units), lambda i: (0, 0))
    gate_up = pl.pallas_call(
        gate_up_kernel,
        grid=(2,),
        in_specs=[block] * 4 + [direct] * 2 + [passed] * 2 + [direct],
        out_specs=pl.BlockSpec((all_rows, 2 * units + HEAD), lambda i: (0, 0)),
        out_shape=jax.ShapeDtypeStruct((all_rows, 2 * units + HEAD), BF),
        compiler_params=params(LARGE_VMEM_BYTES),
    )(*middles, wide_0, wide_1, gate_2, up_2, wide_3)
    parts = after(exchange(gate_up, "z"), *down_2)
    active = pl.pallas_call(
        functools.partial(active_kernel, full_width),
        in_specs=[vmem()],
        out_specs=vmem(),
        out_shape=jax.ShapeDtypeStruct(parts.shape[:2] + (units,), BF),
        compiler_params=params(),
    )(parts)
    active = lax.all_to_all(active, "z", 0, 0, tiled=True).reshape(all_rows, units)
    own_down, behind, across, ahead = pl.pallas_call(
        down_kernel,
        in_specs=[vmem()] * 6,
        out_specs=[vmem()] * 4,
        out_shape=[jax.ShapeDtypeStruct((all_rows, width_part), F32)]
        + [jax.ShapeDtypeStruct((all_rows, width_part), BF)] * 3,
        compiler_params=params(LARGE_VMEM_BYTES),
    )(active, down_0, down_1, *down_2, down_3)
    across, behind, ahead = shift(across, "y", 2), shift(behind, "y", -1), shift(ahead, "y", 1)
    down_part = own_down + across.astype(F32) + behind.astype(F32) + ahead.astype(F32)
    down_sum = tensor_sum(down_part)
    row_request = jnp.arange(all_rows, dtype=jnp.int32) // STEPS
    request_ids = (image_groups * (own_rows // STEPS) + image_requests).reshape(-1)
    has_image = jnp.any(row_request[:, None] == request_ids[None, :], axis=1).astype(F32)
    return (middle_f + jnp.tanh(gate_logits[1]) * has_image[:, None] * down_sum).astype(BF)


def solution(mesh):
    fine = Mesh(mesh.devices.reshape(8, 4, 4, 2), GROUP + TENSOR)
    in_specs = (
        P(None, GROUP),
        P(GROUP, TENSOR),
        P(GROUP),
        P(GROUP, TENSOR),
        P(TENSOR, None),
        P(TENSOR, None),
        P(),
        P(),
        P(TENSOR, GROUP),
        P(),
        P(GROUP),
        P(GROUP, TENSOR),
        P(GROUP, TENSOR),
        P(TENSOR, GROUP),
        P(),
        P(),
        P(),
    )
    return jax.shard_map(shards, mesh=fine, in_specs=in_specs, out_specs=P(None, GROUP), check_vma=False)
```

```python
import functools
import math

import jax
import jax.numpy as jnp
from jax import lax
from jax.experimental import pallas as pl
from jax.experimental.pallas import tpu as pltpu
from jax.sharding import Mesh
from jax.sharding import PartitionSpec as P

GROUP = ("z", "y")
TENSOR = ("x", "c")
HEAD = 128
SLOTS = 2
STEPS = 2
EPS = 1e-05
VMEM_BYTES = 16 * 1024 * 1024
LARGE_VMEM_BYTES = 58 * 1024 * 1024
BF = jnp.bfloat16
F32 = jnp.float32


def params(limit=VMEM_BYTES):
    return pltpu.CompilerParams(vmem_limit_bytes=limit)


def dot(a, b):
    return jnp.dot(a, b, preferred_element_type=F32)


def vmem():
    return pl.BlockSpec(memory_space=pltpu.VMEM)


def smem():
    return pl.BlockSpec(memory_space=pltpu.SMEM)


def route_kernel(me_ref, routes_ref, requests_ref, sel_ref, image_ref):
    me = me_ref[0]
    groups, links = routes_ref.shape
    rows = groups * 2 * SLOTS * STEPS
    row = lax.broadcasted_iota(jnp.int32, (rows, links), 0)
    lane = lax.broadcasted_iota(jnp.int32, (rows, links), 1)
    group_of_row = row >> 3
    slot = (row >> 1) & 1
    step = row & 1
    spread = (group_of_row == lane).astype(F32)
    link = lax.broadcasted_iota(jnp.int32, (groups, links), 1)
    code = (link * 4 + requests_ref[...]).astype(F32)
    route_rows = dot(spread, routes_ref[...].astype(F32))
    code_rows = dot(spread, code)
    hit = route_rows == me.astype(F32)
    first = jnp.min(jnp.where(hit, code_rows, 1e4), axis=1, keepdims=True)
    last = jnp.max(jnp.where(hit, code_rows, -1.0), axis=1, keepdims=True)
    slot1, step1 = slot[:, :1], step[:, :1]
    chosen = jnp.where(slot1 == 0, first, last).astype(jnp.int32)
    found_first = jnp.where(first < 1e3, 1, 0)
    found_last = jnp.where(last > first, 1, 0)
    found = jnp.where(slot1 == 0, found_first, found_last)
    wanted = jnp.where(found == 1, (chosen & 3) * STEPS + step1, -1)
    sel_ref[...] = jnp.where(lane[:, :8] == wanted, 1.0, 0.0).astype(BF)
    mine = routes_ref[pl.ds(me, 1), :]
    here = mine == group_of_row
    first_link = jnp.min(jnp.where(here, lane, 1000), axis=1, keepdims=True)
    last_link = jnp.max(jnp.where(here, lane, -1), axis=1, keepdims=True)
    first_image = jnp.where(first_link < 1000, first_link >> 3, -1)
    last_image = jnp.where(last_link > first_link, last_link >> 3, -1)
    image_ref[...] = jnp.where(slot1 == 0, first_image, last_image)


def kv_kernel(place_ref, x0, x1, k0, v0, k1, v1, low_ref, high_ref, ahead_ref, behind_ref, own_ref):
    total = dot(x0[...], jnp.concatenate((k0[...], v0[...]), axis=1))
    total = total + dot(x1[...], jnp.concatenate((k1[...], v1[...]), axis=1))
    total = total.astype(BF)
    half = low_ref.shape[0]
    step = pl.program_id(0)

    @pl.when(step == 0)
    def _():
        low_ref[...] = total[:half]
        high_ref[...] = total[half:]

    @pl.when(step == 1)
    def _():
        ahead_ref[...] = total

    @pl.when(step == 2)
    def _():
        behind_ref[...] = total

    @pl.when(step == 3)
    def _():
        own_ref[...] = total


def kv_project(place, vision, k_weight, v_weight):
    rows, depth = vision.shape
    chips = 4

    def head(d, place_ref):
        ahead = jnp.where(d == 0, 2, jnp.where(d == 1, 1, jnp.where(d == 2, 3, 0)))
        return 0, lax.rem(place_ref[0] + ahead, chips) * 2 + place_ref[1]

    states = pl.BlockSpec((rows, depth), lambda d, p: (0, 0))
    weights = pl.BlockSpec((depth, HEAD), head)
    sizes = [rows // 2, rows // 2, rows, rows, rows]
    return pl.pallas_call(
        kv_kernel,
        grid_spec=pltpu.PrefetchScalarGridSpec(
            num_scalar_prefetch=1,
            grid=(chips,),
            in_specs=[states] * 2 + [weights] * 4,
            out_specs=[pl.BlockSpec((n, 2 * HEAD), lambda d, p: (0, 0)) for n in sizes],
        ),
        out_shape=[jax.ShapeDtypeStruct((n, 2 * HEAD), BF) for n in sizes],
        compiler_params=params(LARGE_VMEM_BYTES),
    )(
        place,
        vision,
        shift(vision, "c", 1),
        k_weight,
        v_weight,
        shift(k_weight, "c", 1),
        shift(v_weight, "c", 1),
    )


def kv_merge_kernel(ahead_ref, behind_ref, low_ref, high_ref, forward_ref, backward_ref):
    half = low_ref.shape[0]
    forward_ref[:half] = (ahead_ref[:half].astype(F32) + low_ref[...].astype(F32)).astype(BF)
    forward_ref[half:] = ahead_ref[half:]
    backward_ref[:half] = behind_ref[:half]
    backward_ref[half:] = (behind_ref[half:].astype(F32) + high_ref[...].astype(F32)).astype(BF)


def half_of(shape):
    return (lax.broadcasted_iota(jnp.int32, shape, 0) >> 2) & 1


def query_kernel(parts_ref, sel_ref, gain_ref, out_ref):
    total = jnp.sum(parts_ref[...].astype(F32), axis=0)
    gain = gain_ref[...]
    sel = sel_ref[...]
    heads = total.shape[1] // HEAD // 2
    upper = half_of((sel.shape[0], HEAD)) == 1

    def chosen(h):
        v = total[:, h * HEAD : (h + 1) * HEAD]
        scale = lax.rsqrt(jnp.mean(v * v, axis=1, keepdims=True) + EPS)
        return dot(sel, (v * scale * gain).astype(BF))

    for h in range(heads):
        out_ref[:, h * HEAD : (h + 1) * HEAD] = jnp.where(upper, chosen(heads + h), chosen(h)).astype(BF)


def attention_kernel(me_ref, tiles_ref, own_ref, left_ref, right_ref, gain_ref, q_ref, image_ref, out_ref):
    me = me_ref[0]
    total = own_ref[...].astype(F32) + left_ref[...].astype(F32) + right_ref[...].astype(F32)
    k = total[:, :HEAD]
    scale = lax.rsqrt(jnp.mean(k * k, axis=1, keepdims=True) + EPS)
    k = (k * scale * gain_ref[...]).astype(BF)
    v = total[:, HEAD:].astype(BF)
    rows, keys = q_ref.shape[0], k.shape[0]
    tile = lax.broadcasted_iota(jnp.int32, (1, keys), 1) >> 6
    owner = jnp.zeros((1, keys), jnp.int32)
    end = jnp.int32(0)
    for j in range(4):
        end = end + tiles_ref[me, j]
        owner = owner + (tile >= end).astype(jnp.int32)
    allowed = owner == image_ref[...]
    lane = lax.broadcasted_iota(jnp.int32, (rows, HEAD), 1)
    sums = jnp.zeros((rows, HEAD), F32)
    heads = q_ref.shape[1] // HEAD
    for h in range(heads):
        span = slice(h * HEAD, (h + 1) * HEAD)
        score = lax.dot_general(
            q_ref[:, span], k, (((1,), (1,)), ((), ())), preferred_element_type=F32
        )
        weight = jnp.where(allowed, jnp.exp(score * (1.0 / math.sqrt(HEAD))), 0.0)
        den = jnp.sum(weight, axis=1, keepdims=True)
        high = den.astype(BF).astype(F32)
        sums = sums + jnp.where(lane == h, high, 0.0) + jnp.where(lane == heads + h, den - high, 0.0)
        out_ref[:, span] = dot(weight.astype(BF), v).astype(BF)
    out_ref[:, heads * HEAD :] = sums.astype(BF)


def combine_kernel(parts_ref, sel_ref, out_ref):
    sel = sel_ref[...].astype(F32)
    parts = parts_ref[...]
    heads = out_ref.shape[2] // HEAD // 2
    for part in range(2):
        mine = jnp.where(half_of(sel.shape) == part, sel, 0.0).astype(BF)
        total = lax.dot_general(mine, parts, (((0,), (0,)), ((), ())), preferred_element_type=F32)
        sums = total[:, heads * HEAD :]
        for h in range(heads):
            den = sums[:, h : h + 1] + sums[:, heads + h : heads + h + 1]
            mixed = total[:, h * HEAD : (h + 1) * HEAD] / jnp.where(den > 0.0, den, 1.0)
            mixed = jnp.broadcast_to(mixed.astype(BF)[None], (out_ref.shape[0],) + mixed.shape)
            at = (part * heads + h) * HEAD
            out_ref[:, :, at : at + HEAD] = mixed


def gate_up_kernel(m0, m1, m2, m3, w0, w1, gate2, up2, w3, out_ref):
    units = gate2.shape[1]
    step = pl.program_id(0)

    def product(w2):
        total = dot(m0[...], w0[...]) + dot(m1[...], w1[...])
        return (total + dot(m2[...], w2[...]) + dot(m3[...], w3[...])).astype(BF)

    @pl.when(step == 0)
    def _():
        out_ref[:, :units] = product(gate2)

    @pl.when(step == 1)
    def _():
        out_ref[:, units : 2 * units] = product(up2)
        square = jnp.zeros((m0.shape[0], 1), F32)
        for m in (m0, m1, m2, m3):
            value = m[...].astype(F32)
            square = square + jnp.sum(value * value, axis=1, keepdims=True)
        high = square.astype(BF).astype(F32)
        lane = lax.broadcasted_iota(jnp.int32, (m0.shape[0], HEAD), 1)
        extra = jnp.where(lane == 0, high, jnp.where(lane == 1, square - high, 0.0))
        out_ref[:, 2 * units :] = extra.astype(BF)


def down_kernel(a_ref, d0, d1, low2, high2, d3, own_ref, behind_ref, across_ref, ahead_ref):
    active = a_ref[...]
    half = low2.shape[0]
    total = dot(active[:, :half], low2[...]) + dot(active[:, half:], high2[...])
    across_ref[...] = total.astype(BF)
    behind_ref[...] = dot(active, d1[...]).astype(BF)
    ahead_ref[...] = dot(active, d3[...]).astype(BF)
    own_ref[...] = dot(active, d0[...])


def active_kernel(full_width, parts_ref, out_ref):
    total = jnp.sum(parts_ref[...].astype(F32), axis=0)
    units = out_ref.shape[2]
    square = total[:, 2 * units : 2 * units + 1] + total[:, 2 * units + 1 : 2 * units + 2]
    scale = lax.rsqrt(square * (1.0 / full_width) + EPS)
    gate = total[:, :units] * scale
    up = total[:, units : 2 * units] * scale
    active = (gate / (1.0 + jnp.exp(-gate)) * up).astype(BF)
    out_ref[...] = jnp.broadcast_to(active[None], out_ref.shape)


def shift(value, axis, by):
    n = lax.axis_size(axis)
    return lax.ppermute(value, axis, [(i, (i + by) % n) for i in range(n)])


def after(value, *others):
    return lax.optimization_barrier((value,) + others)[0]


def exchange(value, axis):
    n = lax.axis_size(axis)
    out = lax.all_to_all(value, axis, 0, 0, tiled=True)
    return out.reshape((n, value.shape[0] // n) + value.shape[1:])


def tensor_sum(part):
    part = part.astype(BF)
    pair = (part.astype(F32) + shift(part, "c", 1).astype(F32)).astype(BF)
    ahead, behind, across = shift(pair, "x", 1), shift(pair, "x", -1), shift(pair, "x", 2)
    return (pair.astype(F32) + across.astype(F32)) + (ahead.astype(F32) + behind.astype(F32))


def shards(
    hidden,
    vision,
    attn_gain,
    q_weight,
    k_weight,
    v_weight,
    q_gain,
    k_gain,
    o_weight,
    gate_logits,
    mlp_gain,
    gate_weight,
    up_weight,
    down_weight,
    image_tiles,
    image_groups,
    image_requests,
):
    groups = lax.axis_size("z") * lax.axis_size("y")
    me = (lax.axis_index("z") * lax.axis_size("y") + lax.axis_index("y")).astype(jnp.int32).reshape(1)
    place = jnp.stack((lax.axis_index("x"), lax.axis_index("c"))).astype(jnp.int32)
    all_rows, width_part = hidden.shape
    own_rows = all_rows // groups
    full_width = width_part * groups
    local_heads = q_weight.shape[1]
    hidden_part = gate_weight.shape[1]
    slot_rows = groups * 2 * SLOTS * STEPS
    key_rows = vision.shape[0]

    sel, row_image = pl.pallas_call(
        route_kernel,
        in_specs=[smem(), vmem(), vmem()],
        out_specs=[vmem(), vmem()],
        out_shape=[
            jax.ShapeDtypeStruct((slot_rows, own_rows), BF),
            jax.ShapeDtypeStruct((slot_rows, 1), jnp.int32),
        ],
        compiler_params=params(),
    )(me, image_groups.reshape(groups, -1), image_requests.reshape(groups, -1))

    hidden_f = hidden.astype(F32)
    normed = (hidden_f * attn_gain).astype(BF)
    q_part = dot(normed, q_weight).astype(BF)
    q_parts = exchange(q_part, GROUP)

    low, high, ahead, behind, own = kv_project(place, vision, k_weight, v_weight)
    q_parts = after(q_parts, own)
    forward, backward = pl.pallas_call(
        kv_merge_kernel,
        in_specs=[vmem()] * 4,
        out_specs=[vmem()] * 2,
        out_shape=[jax.ShapeDtypeStruct(ahead.shape, BF)] * 2,
        compiler_params=params(),
    )(ahead, behind, shift(low, "x", 1), shift(high, "x", -1))
    kv_left = shift(forward, "x", 1)
    kv_right = shift(backward, "x", -1)

    chips_y = lax.axis_size("y")
    units = hidden_part // chips_y
    half = units // 2
    gain = mlp_gain[:, None]

    def columns(weight, d):
        at = lax.rem(lax.axis_index("y") + d, chips_y) * units
        return lax.dynamic_slice_in_dim(weight, at, units, 1).astype(F32)

    def wide(*parts):
        return (jnp.concatenate(parts, axis=1) * gain).astype(BF)

    queries = pl.pallas_call(
        query_kernel,
        in_specs=[vmem()] * 3,
        out_specs=vmem(),
        out_shape=jax.ShapeDtypeStruct((slot_rows, local_heads // 2), BF),
        compiler_params=params(),
    )(q_parts, sel, q_gain.reshape(1, HEAD))
    queries = after(queries, forward, backward)
    later_gate, later_up = lax.optimization_barrier((gate_weight, up_weight, queries))[:2]
    wide_0 = wide(columns(later_gate, 0), columns(later_up, 0))
    wide_1 = shift(wide(columns(later_gate, 1), columns(later_up, 1)), "y", 1)
    wide_3 = shift(wide(columns(later_gate, 3), columns(later_up, 3)), "y", -1)
    queries = lax.all_to_all(queries, GROUP, 0, 0, tiled=True)

    mixed = pl.pallas_call(
        attention_kernel,
        in_specs=[smem(), smem()] + [vmem()] * 6,
        out_specs=vmem(),
        out_shape=jax.ShapeDtypeStruct((slot_rows, local_heads // 2 + HEAD), BF),
        compiler_params=params(),
    )(me, image_tiles, own, kv_left, kv_right, k_gain.reshape(1, HEAD), queries, row_image)
    gate_weight, up_weight, down_weight = lax.optimization_barrier((gate_weight, up_weight, down_weight, mixed))[:3]
    gate_2, up_2 = wide(columns(gate_weight, 2)), wide(columns(up_weight, 2))

    def rows(d, start, size):
        at = lax.rem(lax.axis_index("y") + d, chips_y) * units + start
        return lax.dynamic_slice_in_dim(down_weight, at, size, 0)

    down_0, down_1, down_3 = rows(0, 0, units), rows(1, 0, units), rows(3, 0, units)
    down_2 = rows(2, 0, half), rows(2, half, half)
    mixed = lax.all_to_all(mixed, GROUP, 0, 0, tiled=True)
    mixed = after(mixed, gate_2, up_2, down_1, down_3, *down_2)
    gate_2, up_2 = shift(gate_2, "y", 1), shift(up_2, "y", -1)

    attended = pl.pallas_call(
        combine_kernel,
        in_specs=[vmem()] * 2,
        out_specs=vmem(),
        out_shape=jax.ShapeDtypeStruct((groups, own_rows, local_heads), BF),
        compiler_params=params(),
    )(mixed, sel)
    attended = after(attended, wide_1, wide_3)
    attended = lax.all_to_all(attended, GROUP, 0, 0, tiled=True).reshape(all_rows, local_heads)
    attended = after(attended, gate_2, up_2)
    gate_2, up_2 = shift(gate_2, "y", 1), shift(up_2, "y", -1)
    attn_sum = tensor_sum(dot(attended, o_weight))
    middle = (hidden_f + jnp.tanh(gate_logits[0]) * attn_sum).astype(BF)
    middle_f = middle.astype(F32)
    middle = after(middle, gate_2, up_2)
    middles = [middle] + [shift(middle, "y", d) for d in (1, 2, 3)]
    block = pl.BlockSpec((all_rows, width_part), lambda i: (0, 0))
    direct = pl.BlockSpec((width_part, units), lambda i: (0, i))
    passed = pl.BlockSpec((width_part, units), lambda i: (0, 0))
    gate_up = pl.pallas_call(
        gate_up_kernel,
        grid=(2,),
        in_specs=[block] * 4 + [direct] * 2 + [passed] * 2 + [direct],
        out_specs=pl.BlockSpec((all_rows, 2 * units + HEAD), lambda i: (0, 0)),
        out_shape=jax.ShapeDtypeStruct((all_rows, 2 * units + HEAD), BF),
        compiler_params=params(LARGE_VMEM_BYTES),
    )(*middles, wide_0, wide_1, gate_2, up_2, wide_3)
    down_1, down_3, *down_2 = lax.optimization_barrier((down_1, down_3, *down_2, gate_up))[:4]
    down_1, down_3 = shift(down_1, "y", 1), shift(down_3, "y", -1)
    down_2 = shift(down_2[0], "y", 1), shift(down_2[1], "y", -1)
    parts = after(exchange(gate_up, "z"), down_1, down_3, *down_2)
    down_2 = shift(down_2[0], "y", 1), shift(down_2[1], "y", -1)
    active = pl.pallas_call(
        functools.partial(active_kernel, full_width),
        in_specs=[vmem()],
        out_specs=vmem(),
        out_shape=jax.ShapeDtypeStruct(parts.shape[:2] + (units,), BF),
        compiler_params=params(),
    )(parts)
    active = lax.all_to_all(active, "z", 0, 0, tiled=True).reshape(all_rows, units)
    own_down, behind, across, ahead = pl.pallas_call(
        down_kernel,
        in_specs=[vmem()] * 6,
        out_specs=[vmem()] * 4,
        out_shape=[jax.ShapeDtypeStruct((all_rows, width_part), F32)]
        + [jax.ShapeDtypeStruct((all_rows, width_part), BF)] * 3,
        compiler_params=params(LARGE_VMEM_BYTES),
    )(active, down_0, down_1, *down_2, down_3)
    across, behind, ahead = shift(across, "y", 2), shift(behind, "y", -1), shift(ahead, "y", 1)
    down_part = own_down + across.astype(F32) + behind.astype(F32) + ahead.astype(F32)
    down_sum = tensor_sum(down_part)
    row_request = jnp.arange(all_rows, dtype=jnp.int32) // STEPS
    request_ids = (image_groups * (own_rows // STEPS) + image_requests).reshape(-1)
    has_image = jnp.any(row_request[:, None] == request_ids[None, :], axis=1).astype(F32)
    return (middle_f + jnp.tanh(gate_logits[1]) * has_image[:, None] * down_sum).astype(BF)


def solution(mesh):
    fine = Mesh(mesh.devices.reshape(8, 4, 4, 2), GROUP + TENSOR)
    in_specs = (
        P(None, GROUP),
        P(GROUP, TENSOR),
        P(GROUP),
        P(GROUP, TENSOR),
        P(TENSOR, None),
        P(TENSOR, None),
        P(),
        P(),
        P(TENSOR, GROUP),
        P(),
        P(GROUP),
        P(GROUP, TENSOR),
        P(GROUP, TENSOR),
        P(TENSOR, GROUP),
        P(),
        P(),
        P(),
    )
    return jax.shard_map(shards, mesh=fine, in_specs=in_specs, out_specs=P(None, GROUP), check_vma=False)
```

```python
import functools
import math

import jax
import jax.numpy as jnp
from jax import lax
from jax.experimental import pallas as pl
from jax.experimental.pallas import tpu as pltpu
from jax.sharding import Mesh
from jax.sharding import PartitionSpec as P

GROUP = ("z", "y")
TENSOR = ("x", "c")
HEAD = 128
SLOTS = 2
STEPS = 2
EPS = 1e-05
VMEM_BYTES = 16 * 1024 * 1024
LARGE_VMEM_BYTES = 60 * 1024 * 1024
BF = jnp.bfloat16
F32 = jnp.float32


def params(limit=VMEM_BYTES):
    return pltpu.CompilerParams(vmem_limit_bytes=limit)


def dot(a, b):
    return jnp.dot(a, b, preferred_element_type=F32)


def vmem():
    return pl.BlockSpec(memory_space=pltpu.VMEM)


def smem():
    return pl.BlockSpec(memory_space=pltpu.SMEM)


def route_kernel(me_ref, routes_ref, requests_ref, sel_ref, image_ref):
    me = me_ref[0]
    groups, links = routes_ref.shape
    rows = groups * 2 * SLOTS * STEPS
    row = lax.broadcasted_iota(jnp.int32, (rows, links), 0)
    lane = lax.broadcasted_iota(jnp.int32, (rows, links), 1)
    group_of_row = row >> 3
    slot = (row >> 1) & 1
    step = row & 1
    spread = (group_of_row == lane).astype(F32)
    link = lax.broadcasted_iota(jnp.int32, (groups, links), 1)
    code = (link * 4 + requests_ref[...]).astype(F32)
    route_rows = dot(spread, routes_ref[...].astype(F32))
    code_rows = dot(spread, code)
    hit = route_rows == me.astype(F32)
    first = jnp.min(jnp.where(hit, code_rows, 1e4), axis=1, keepdims=True)
    last = jnp.max(jnp.where(hit, code_rows, -1.0), axis=1, keepdims=True)
    slot1, step1 = slot[:, :1], step[:, :1]
    chosen = jnp.where(slot1 == 0, first, last).astype(jnp.int32)
    found_first = jnp.where(first < 1e3, 1, 0)
    found_last = jnp.where(last > first, 1, 0)
    found = jnp.where(slot1 == 0, found_first, found_last)
    wanted = jnp.where(found == 1, (chosen & 3) * STEPS + step1, -1)
    sel_ref[...] = jnp.where(lane[:, :8] == wanted, 1.0, 0.0).astype(BF)
    mine = routes_ref[pl.ds(me, 1), :]
    here = mine == group_of_row
    first_link = jnp.min(jnp.where(here, lane, 1000), axis=1, keepdims=True)
    last_link = jnp.max(jnp.where(here, lane, -1), axis=1, keepdims=True)
    first_image = jnp.where(first_link < 1000, first_link >> 3, -1)
    last_image = jnp.where(last_link > first_link, last_link >> 3, -1)
    image_ref[...] = jnp.where(slot1 == 0, first_image, last_image)


def kv_kernel(place_ref, x0, x1, k0, v0, k1, v1, low_ref, high_ref, ahead_ref, behind_ref, own_ref):
    total = dot(x0[...], jnp.concatenate((k0[...], v0[...]), axis=1))
    total = total + dot(x1[...], jnp.concatenate((k1[...], v1[...]), axis=1))
    total = total.astype(BF)
    half = low_ref.shape[0]
    step = pl.program_id(0)

    @pl.when(step == 0)
    def _():
        low_ref[...] = total[:half]
        high_ref[...] = total[half:]

    @pl.when(step == 1)
    def _():
        ahead_ref[...] = total

    @pl.when(step == 2)
    def _():
        behind_ref[...] = total

    @pl.when(step == 3)
    def _():
        own_ref[...] = total


def kv_project(place, vision, k_weight, v_weight):
    rows, depth = vision.shape
    chips = 4

    def head(d, place_ref):
        ahead = jnp.where(d == 0, 2, jnp.where(d == 1, 1, jnp.where(d == 2, 3, 0)))
        return 0, lax.rem(place_ref[0] + ahead, chips) * 2 + place_ref[1]

    states = pl.BlockSpec((rows, depth), lambda d, p: (0, 0))
    weights = pl.BlockSpec((depth, HEAD), head)
    sizes = [rows // 2, rows // 2, rows, rows, rows]
    return pl.pallas_call(
        kv_kernel,
        grid_spec=pltpu.PrefetchScalarGridSpec(
            num_scalar_prefetch=1,
            grid=(chips,),
            in_specs=[states] * 2 + [weights] * 4,
            out_specs=[pl.BlockSpec((n, 2 * HEAD), lambda d, p: (0, 0)) for n in sizes],
        ),
        out_shape=[jax.ShapeDtypeStruct((n, 2 * HEAD), BF) for n in sizes],
        compiler_params=params(LARGE_VMEM_BYTES),
    )(
        place,
        vision,
        shift(vision, "c", 1),
        k_weight,
        v_weight,
        shift(k_weight, "c", 1),
        shift(v_weight, "c", 1),
    )


def kv_merge_kernel(ahead_ref, behind_ref, low_ref, high_ref, forward_ref, backward_ref):
    half = low_ref.shape[0]
    forward_ref[:half] = (ahead_ref[:half].astype(F32) + low_ref[...].astype(F32)).astype(BF)
    forward_ref[half:] = ahead_ref[half:]
    backward_ref[:half] = behind_ref[:half]
    backward_ref[half:] = (behind_ref[half:].astype(F32) + high_ref[...].astype(F32)).astype(BF)


def half_of(shape):
    return (lax.broadcasted_iota(jnp.int32, shape, 0) >> 2) & 1


def query_kernel(parts_ref, sel_ref, gain_ref, out_ref):
    total = jnp.sum(parts_ref[...].astype(F32), axis=0)
    gain = gain_ref[...]
    sel = sel_ref[...]
    heads = total.shape[1] // HEAD // 2
    upper = half_of((sel.shape[0], HEAD)) == 1

    def chosen(h):
        v = total[:, h * HEAD : (h + 1) * HEAD]
        scale = lax.rsqrt(jnp.mean(v * v, axis=1, keepdims=True) + EPS)
        return dot(sel, (v * scale * gain).astype(BF))

    for h in range(heads):
        out_ref[:, h * HEAD : (h + 1) * HEAD] = jnp.where(upper, chosen(heads + h), chosen(h)).astype(BF)


def attention_kernel(me_ref, tiles_ref, own_ref, left_ref, right_ref, gain_ref, q_ref, image_ref, out_ref):
    me = me_ref[0]
    total = own_ref[...].astype(F32) + left_ref[...].astype(F32) + right_ref[...].astype(F32)
    k = total[:, :HEAD]
    scale = lax.rsqrt(jnp.mean(k * k, axis=1, keepdims=True) + EPS)
    k = (k * scale * gain_ref[...]).astype(BF)
    v = total[:, HEAD:].astype(BF)
    rows, keys = q_ref.shape[0], k.shape[0]
    tile = lax.broadcasted_iota(jnp.int32, (1, keys), 1) >> 6
    owner = jnp.zeros((1, keys), jnp.int32)
    end = jnp.int32(0)
    for j in range(4):
        end = end + tiles_ref[me, j]
        owner = owner + (tile >= end).astype(jnp.int32)
    allowed = owner == image_ref[...]
    lane = lax.broadcasted_iota(jnp.int32, (rows, HEAD), 1)
    sums = jnp.zeros((rows, HEAD), F32)
    heads = q_ref.shape[1] // HEAD
    for h in range(heads):
        span = slice(h * HEAD, (h + 1) * HEAD)
        score = lax.dot_general(
            q_ref[:, span], k, (((1,), (1,)), ((), ())), preferred_element_type=F32
        )
        weight = jnp.where(allowed, jnp.exp(score * (1.0 / math.sqrt(HEAD))), 0.0)
        den = jnp.sum(weight, axis=1, keepdims=True)
        high = den.astype(BF).astype(F32)
        sums = sums + jnp.where(lane == h, high, 0.0) + jnp.where(lane == heads + h, den - high, 0.0)
        out_ref[:, span] = dot(weight.astype(BF), v).astype(BF)
    out_ref[:, heads * HEAD :] = sums.astype(BF)


def combine_kernel(parts_ref, sel_ref, out_ref):
    sel = sel_ref[...].astype(F32)
    parts = parts_ref[...]
    heads = out_ref.shape[2] // HEAD // 2
    for part in range(2):
        mine = jnp.where(half_of(sel.shape) == part, sel, 0.0).astype(BF)
        total = lax.dot_general(mine, parts, (((0,), (0,)), ((), ())), preferred_element_type=F32)
        sums = total[:, heads * HEAD :]
        for h in range(heads):
            den = sums[:, h : h + 1] + sums[:, heads + h : heads + h + 1]
            mixed = total[:, h * HEAD : (h + 1) * HEAD] / jnp.where(den > 0.0, den, 1.0)
            mixed = jnp.broadcast_to(mixed.astype(BF)[None], (out_ref.shape[0],) + mixed.shape)
            at = (part * heads + h) * HEAD
            out_ref[:, :, at : at + HEAD] = mixed


def gate_up_kernel(m0, m1, m2, m3, w0, w1, gate2, up2, w3, out_ref):
    units = gate2.shape[1]
    step = pl.program_id(0)

    def product(w2):
        total = dot(m0[...], w0[...]) + dot(m1[...], w1[...])
        return (total + dot(m2[...], w2[...]) + dot(m3[...], w3[...])).astype(BF)

    @pl.when(step == 0)
    def _():
        out_ref[:, :units] = product(gate2)

    @pl.when(step == 1)
    def _():
        out_ref[:, units : 2 * units] = product(up2)
        square = jnp.zeros((m0.shape[0], 1), F32)
        for m in (m0, m1, m2, m3):
            value = m[...].astype(F32)
            square = square + jnp.sum(value * value, axis=1, keepdims=True)
        high = square.astype(BF).astype(F32)
        lane = lax.broadcasted_iota(jnp.int32, (m0.shape[0], HEAD), 1)
        extra = jnp.where(lane == 0, high, jnp.where(lane == 1, square - high, 0.0))
        out_ref[:, 2 * units :] = extra.astype(BF)


def down_kernel(a_ref, d0, d1, low2, high2, d3, own_ref, behind_ref, across_ref, ahead_ref):
    active = a_ref[...]
    half = low2.shape[0]
    total = dot(active[:, :half], low2[...]) + dot(active[:, half:], high2[...])
    across_ref[...] = total.astype(BF)
    behind_ref[...] = dot(active, d1[...]).astype(BF)
    ahead_ref[...] = dot(active, d3[...]).astype(BF)
    own_ref[...] = dot(active, d0[...])


def active_kernel(full_width, parts_ref, out_ref):
    total = jnp.sum(parts_ref[...].astype(F32), axis=0)
    units = out_ref.shape[2]
    square = total[:, 2 * units : 2 * units + 1] + total[:, 2 * units + 1 : 2 * units + 2]
    scale = lax.rsqrt(square * (1.0 / full_width) + EPS)
    gate = total[:, :units] * scale
    up = total[:, units : 2 * units] * scale
    active = (gate / (1.0 + jnp.exp(-gate)) * up).astype(BF)
    out_ref[...] = jnp.broadcast_to(active[None], out_ref.shape)


def shift(value, axis, by):
    n = lax.axis_size(axis)
    return lax.ppermute(value, axis, [(i, (i + by) % n) for i in range(n)])


def after(value, *others):
    return lax.optimization_barrier((value,) + others)[0]


def exchange(value, axis):
    n = lax.axis_size(axis)
    out = lax.all_to_all(value, axis, 0, 0, tiled=True)
    return out.reshape((n, value.shape[0] // n) + value.shape[1:])


def tensor_sum(part, *others):
    part = part.astype(BF)
    pair = (part.astype(F32) + shift(part, "c", 1).astype(F32)).astype(BF)
    pair = after(pair, *others)
    ahead, behind, across = shift(pair, "x", 1), shift(pair, "x", -1), shift(pair, "x", 2)
    return (pair.astype(F32) + across.astype(F32)) + (ahead.astype(F32) + behind.astype(F32))


def shards(
    hidden,
    vision,
    attn_gain,
    q_weight,
    k_weight,
    v_weight,
    q_gain,
    k_gain,
    o_weight,
    gate_logits,
    mlp_gain,
    gate_weight,
    up_weight,
    down_weight,
    image_tiles,
    image_groups,
    image_requests,
):
    groups = lax.axis_size("z") * lax.axis_size("y")
    me = (lax.axis_index("z") * lax.axis_size("y") + lax.axis_index("y")).astype(jnp.int32).reshape(1)
    place = jnp.stack((lax.axis_index("x"), lax.axis_index("c"))).astype(jnp.int32)
    all_rows, width_part = hidden.shape
    own_rows = all_rows // groups
    full_width = width_part * groups
    local_heads = q_weight.shape[1]
    hidden_part = gate_weight.shape[1]
    slot_rows = groups * 2 * SLOTS * STEPS
    key_rows = vision.shape[0]

    sel, row_image = pl.pallas_call(
        route_kernel,
        in_specs=[smem(), vmem(), vmem()],
        out_specs=[vmem(), vmem()],
        out_shape=[
            jax.ShapeDtypeStruct((slot_rows, own_rows), BF),
            jax.ShapeDtypeStruct((slot_rows, 1), jnp.int32),
        ],
        compiler_params=params(),
    )(me, image_groups.reshape(groups, -1), image_requests.reshape(groups, -1))

    hidden_f = hidden.astype(F32)
    normed = (hidden_f * attn_gain).astype(BF)
    q_part = dot(normed, q_weight).astype(BF)
    q_parts = exchange(q_part, GROUP)

    low, high, ahead, behind, own = kv_project(place, vision, k_weight, v_weight)
    q_parts = after(q_parts, own)
    forward, backward = pl.pallas_call(
        kv_merge_kernel,
        in_specs=[vmem()] * 4,
        out_specs=[vmem()] * 2,
        out_shape=[jax.ShapeDtypeStruct(ahead.shape, BF)] * 2,
        compiler_params=params(),
    )(ahead, behind, shift(low, "x", 1), shift(high, "x", -1))
    kv_left = shift(forward, "x", 1)
    kv_right = shift(backward, "x", -1)

    chips_y = lax.axis_size("y")
    units = hidden_part // chips_y
    half = units // 2
    gain = mlp_gain[:, None]

    def columns(weight, d):
        at = lax.rem(lax.axis_index("y") + d, chips_y) * units
        return lax.dynamic_slice_in_dim(weight, at, units, 1).astype(F32)

    def wide(*parts):
        return (jnp.concatenate(parts, axis=1) * gain).astype(BF)

    queries = pl.pallas_call(
        query_kernel,
        in_specs=[vmem()] * 3,
        out_specs=vmem(),
        out_shape=jax.ShapeDtypeStruct((slot_rows, local_heads // 2), BF),
        compiler_params=params(),
    )(q_parts, sel, q_gain.reshape(1, HEAD))
    queries = after(queries, forward, backward)
    later_gate, later_up = lax.optimization_barrier((gate_weight, up_weight, queries))[:2]
    wide_0 = wide(columns(later_gate, 0), columns(later_up, 0))
    wide_1 = shift(wide(columns(later_gate, 1), columns(later_up, 1)), "y", 1)
    wide_3 = shift(wide(columns(later_gate, 3), columns(later_up, 3)), "y", -1)
    queries = lax.all_to_all(queries, GROUP, 0, 0, tiled=True)

    mixed = pl.pallas_call(
        attention_kernel,
        in_specs=[smem(), smem()] + [vmem()] * 6,
        out_specs=vmem(),
        out_shape=jax.ShapeDtypeStruct((slot_rows, local_heads // 2 + HEAD), BF),
        compiler_params=params(),
    )(me, image_tiles, own, kv_left, kv_right, k_gain.reshape(1, HEAD), queries, row_image)
    gate_weight, up_weight, down_weight = lax.optimization_barrier((gate_weight, up_weight, down_weight, mixed))[:3]
    gate_2, up_2 = wide(columns(gate_weight, 2)), wide(columns(up_weight, 2))

    def rows(d, start, size):
        at = lax.rem(lax.axis_index("y") + d, chips_y) * units + start
        return lax.dynamic_slice_in_dim(down_weight, at, size, 0)

    down_0, down_1, down_3 = rows(0, 0, units), rows(1, 0, units), rows(3, 0, units)
    down_2 = rows(2, 0, half), rows(2, half, half)
    mixed = lax.all_to_all(mixed, GROUP, 0, 0, tiled=True)
    mixed = after(mixed, gate_2, up_2, down_1, down_3, *down_2)
    gate_2, up_2 = shift(gate_2, "y", 1), shift(up_2, "y", -1)

    attended = pl.pallas_call(
        combine_kernel,
        in_specs=[vmem()] * 2,
        out_specs=vmem(),
        out_shape=jax.ShapeDtypeStruct((groups, own_rows, local_heads), BF),
        compiler_params=params(),
    )(mixed, sel)
    attended = after(attended, wide_1, wide_3)
    attended = lax.all_to_all(attended, GROUP, 0, 0, tiled=True).reshape(all_rows, local_heads)
    attn_sum = tensor_sum(dot(attended, o_weight), gate_2, up_2)
    gate_2, up_2 = shift(gate_2, "y", 1), shift(up_2, "y", -1)
    middle = (hidden_f + jnp.tanh(gate_logits[0]) * attn_sum).astype(BF)
    middle_f = middle.astype(F32)
    middles = [middle] + [shift(middle, "y", d) for d in (1, 2, 3)]
    block = pl.BlockSpec((all_rows, width_part), lambda i: (0, 0))
    direct = pl.BlockSpec((width_part, units), lambda i: (0, i))
    passed = pl.BlockSpec((width_part, units), lambda i: (0, 0))
    gate_up = pl.pallas_call(
        gate_up_kernel,
        grid=(2,),
        in_specs=[block] * 4 + [direct] * 2 + [passed] * 2 + [direct],
        out_specs=pl.BlockSpec((all_rows, 2 * units + HEAD), lambda i: (0, 0)),
        out_shape=jax.ShapeDtypeStruct((all_rows, 2 * units + HEAD), BF),
        compiler_params=params(LARGE_VMEM_BYTES),
    )(*middles, wide_0, wide_1, gate_2, up_2, wide_3)
    down_1, down_3, *down_2 = lax.optimization_barrier((down_1, down_3, *down_2, gate_up))[:4]
    down_1, down_3 = shift(down_1, "y", 1), shift(down_3, "y", -1)
    down_2 = shift(down_2[0], "y", 1), shift(down_2[1], "y", -1)
    parts = after(exchange(gate_up, "z"), down_1, down_3, *down_2)
    down_2 = shift(down_2[0], "y", 1), shift(down_2[1], "y", -1)
    active = pl.pallas_call(
        functools.partial(active_kernel, full_width),
        in_specs=[vmem()],
        out_specs=vmem(),
        out_shape=jax.ShapeDtypeStruct(parts.shape[:2] + (units,), BF),
        compiler_params=params(),
    )(parts)
    active = lax.all_to_all(active, "z", 0, 0, tiled=True).reshape(all_rows, units)
    own_down, behind, across, ahead = pl.pallas_call(
        down_kernel,
        in_specs=[vmem()] * 6,
        out_specs=[vmem()] * 4,
        out_shape=[jax.ShapeDtypeStruct((all_rows, width_part), F32)]
        + [jax.ShapeDtypeStruct((all_rows, width_part), BF)] * 3,
        compiler_params=params(LARGE_VMEM_BYTES),
    )(active, down_0, down_1, *down_2, down_3)
    across, behind, ahead = shift(across, "y", 2), shift(behind, "y", -1), shift(ahead, "y", 1)
    down_part = own_down + across.astype(F32) + behind.astype(F32) + ahead.astype(F32)
    down_sum = tensor_sum(down_part)
    row_request = jnp.arange(all_rows, dtype=jnp.int32) // STEPS
    request_ids = (image_groups * (own_rows // STEPS) + image_requests).reshape(-1)
    has_image = jnp.any(row_request[:, None] == request_ids[None, :], axis=1).astype(F32)
    return (middle_f + jnp.tanh(gate_logits[1]) * has_image[:, None] * down_sum).astype(BF)


def solution(mesh):
    fine = Mesh(mesh.devices.reshape(8, 4, 4, 2), GROUP + TENSOR)
    in_specs = (
        P(None, GROUP),
        P(GROUP, TENSOR),
        P(GROUP),
        P(GROUP, TENSOR),
        P(TENSOR, None),
        P(TENSOR, None),
        P(),
        P(),
        P(TENSOR, GROUP),
        P(),
        P(GROUP),
        P(GROUP, TENSOR),
        P(GROUP, TENSOR),
        P(TENSOR, GROUP),
        P(),
        P(),
        P(),
    )
    return jax.shard_map(shards, mesh=fine, in_specs=in_specs, out_specs=P(None, GROUP), check_vma=False)
```

```python
import functools
import math

import jax
import jax.numpy as jnp
from jax import lax
from jax.experimental import pallas as pl
from jax.experimental.pallas import tpu as pltpu
from jax.sharding import Mesh
from jax.sharding import PartitionSpec as P

GROUP = ("z", "y")
TENSOR = ("x", "c")
HEAD = 128
SLOTS = 2
STEPS = 2
EPS = 1e-05
VMEM_BYTES = 16 * 1024 * 1024
LARGE_VMEM_BYTES = 60 * 1024 * 1024
BF = jnp.bfloat16
F32 = jnp.float32


def params(limit=VMEM_BYTES):
    return pltpu.CompilerParams(vmem_limit_bytes=limit)


def dot(a, b):
    return jnp.dot(a, b, preferred_element_type=F32)


def vmem():
    return pl.BlockSpec(memory_space=pltpu.VMEM)


def smem():
    return pl.BlockSpec(memory_space=pltpu.SMEM)


def route_kernel(me_ref, routes_ref, requests_ref, sel_ref, image_ref):
    me = me_ref[0]
    groups, links = routes_ref.shape
    rows = groups * 2 * SLOTS * STEPS
    row = lax.broadcasted_iota(jnp.int32, (rows, links), 0)
    lane = lax.broadcasted_iota(jnp.int32, (rows, links), 1)
    group_of_row = row >> 3
    slot = (row >> 1) & 1
    step = row & 1
    spread = (group_of_row == lane).astype(F32)
    link = lax.broadcasted_iota(jnp.int32, (groups, links), 1)
    code = (link * 4 + requests_ref[...]).astype(F32)
    route_rows = dot(spread, routes_ref[...].astype(F32))
    code_rows = dot(spread, code)
    hit = route_rows == me.astype(F32)
    first = jnp.min(jnp.where(hit, code_rows, 1e4), axis=1, keepdims=True)
    last = jnp.max(jnp.where(hit, code_rows, -1.0), axis=1, keepdims=True)
    slot1, step1 = slot[:, :1], step[:, :1]
    chosen = jnp.where(slot1 == 0, first, last).astype(jnp.int32)
    found_first = jnp.where(first < 1e3, 1, 0)
    found_last = jnp.where(last > first, 1, 0)
    found = jnp.where(slot1 == 0, found_first, found_last)
    wanted = jnp.where(found == 1, (chosen & 3) * STEPS + step1, -1)
    sel_ref[...] = jnp.where(lane[:, :8] == wanted, 1.0, 0.0).astype(BF)
    mine = routes_ref[pl.ds(me, 1), :]
    here = mine == group_of_row
    first_link = jnp.min(jnp.where(here, lane, 1000), axis=1, keepdims=True)
    last_link = jnp.max(jnp.where(here, lane, -1), axis=1, keepdims=True)
    first_image = jnp.where(first_link < 1000, first_link >> 3, -1)
    last_image = jnp.where(last_link > first_link, last_link >> 3, -1)
    image_ref[...] = jnp.where(slot1 == 0, first_image, last_image)


def kv_kernel(place_ref, x0, x1, k0, v0, k1, v1, low_ref, high_ref, ahead_ref, behind_ref, own_ref):
    total = dot(x0[...], jnp.concatenate((k0[...], v0[...]), axis=1))
    total = total + dot(x1[...], jnp.concatenate((k1[...], v1[...]), axis=1))
    total = total.astype(BF)
    half = low_ref.shape[0]
    step = pl.program_id(0)

    @pl.when(step == 0)
    def _():
        low_ref[...] = total[:half]
        high_ref[...] = total[half:]

    @pl.when(step == 1)
    def _():
        ahead_ref[...] = total

    @pl.when(step == 2)
    def _():
        behind_ref[...] = total

    @pl.when(step == 3)
    def _():
        own_ref[...] = total


def kv_project(place, vision, k_weight, v_weight):
    rows, depth = vision.shape
    chips = 4

    def head(d, place_ref):
        ahead = jnp.where(d == 0, 2, jnp.where(d == 1, 1, jnp.where(d == 2, 3, 0)))
        return 0, lax.rem(place_ref[0] + ahead, chips) * 2 + place_ref[1]

    states = pl.BlockSpec((rows, depth), lambda d, p: (0, 0))
    weights = pl.BlockSpec((depth, HEAD), head)
    sizes = [rows // 2, rows // 2, rows, rows, rows]
    return pl.pallas_call(
        kv_kernel,
        grid_spec=pltpu.PrefetchScalarGridSpec(
            num_scalar_prefetch=1,
            grid=(chips,),
            in_specs=[states] * 2 + [weights] * 4,
            out_specs=[pl.BlockSpec((n, 2 * HEAD), lambda d, p: (0, 0)) for n in sizes],
        ),
        out_shape=[jax.ShapeDtypeStruct((n, 2 * HEAD), BF) for n in sizes],
        compiler_params=params(LARGE_VMEM_BYTES),
    )(
        place,
        vision,
        shift(vision, "c", 1),
        k_weight,
        v_weight,
        shift(k_weight, "c", 1),
        shift(v_weight, "c", 1),
    )


def kv_merge_kernel(ahead_ref, behind_ref, low_ref, high_ref, forward_ref, backward_ref):
    half = low_ref.shape[0]
    forward_ref[:half] = (ahead_ref[:half].astype(F32) + low_ref[...].astype(F32)).astype(BF)
    forward_ref[half:] = ahead_ref[half:]
    backward_ref[:half] = behind_ref[:half]
    backward_ref[half:] = (behind_ref[half:].astype(F32) + high_ref[...].astype(F32)).astype(BF)


def half_of(shape):
    return (lax.broadcasted_iota(jnp.int32, shape, 0) >> 2) & 1


def query_kernel(parts_ref, sel_ref, gain_ref, out_ref):
    total = jnp.sum(parts_ref[...].astype(F32), axis=0)
    gain = gain_ref[...]
    sel = sel_ref[...]
    heads = total.shape[1] // HEAD // 2
    upper = half_of((sel.shape[0], HEAD)) == 1

    def chosen(h):
        v = total[:, h * HEAD : (h + 1) * HEAD]
        scale = lax.rsqrt(jnp.mean(v * v, axis=1, keepdims=True) + EPS)
        return dot(sel, (v * scale * gain).astype(BF))

    for h in range(heads):
        out_ref[:, h * HEAD : (h + 1) * HEAD] = jnp.where(upper, chosen(heads + h), chosen(h)).astype(BF)


def attention_kernel(me_ref, tiles_ref, own_ref, left_ref, right_ref, gain_ref, q_ref, image_ref, out_ref):
    me = me_ref[0]
    total = own_ref[...].astype(F32) + left_ref[...].astype(F32) + right_ref[...].astype(F32)
    k = total[:, :HEAD]
    scale = lax.rsqrt(jnp.mean(k * k, axis=1, keepdims=True) + EPS)
    k = (k * scale * gain_ref[...]).astype(BF)
    v = total[:, HEAD:].astype(BF)
    rows, keys = q_ref.shape[0], k.shape[0]
    tile = lax.broadcasted_iota(jnp.int32, (1, keys), 1) >> 6
    owner = jnp.zeros((1, keys), jnp.int32)
    end = jnp.int32(0)
    for j in range(4):
        end = end + tiles_ref[me, j]
        owner = owner + (tile >= end).astype(jnp.int32)
    allowed = owner == image_ref[...]
    lane = lax.broadcasted_iota(jnp.int32, (rows, HEAD), 1)
    sums = jnp.zeros((rows, HEAD), F32)
    heads = q_ref.shape[1] // HEAD
    for h in range(heads):
        span = slice(h * HEAD, (h + 1) * HEAD)
        score = lax.dot_general(
            q_ref[:, span], k, (((1,), (1,)), ((), ())), preferred_element_type=F32
        )
        weight = jnp.where(allowed, jnp.exp(score * (1.0 / math.sqrt(HEAD))), 0.0)
        den = jnp.sum(weight, axis=1, keepdims=True)
        high = den.astype(BF).astype(F32)
        sums = sums + jnp.where(lane == h, high, 0.0) + jnp.where(lane == heads + h, den - high, 0.0)
        out_ref[:, span] = dot(weight.astype(BF), v).astype(BF)
    out_ref[:, heads * HEAD :] = sums.astype(BF)


def combine_kernel(parts_ref, sel_ref, out_ref):
    sel = sel_ref[...].astype(F32)
    parts = parts_ref[...]
    heads = out_ref.shape[2] // HEAD // 2
    for part in range(2):
        mine = jnp.where(half_of(sel.shape) == part, sel, 0.0).astype(BF)
        total = lax.dot_general(mine, parts, (((0,), (0,)), ((), ())), preferred_element_type=F32)
        sums = total[:, heads * HEAD :]
        for h in range(heads):
            den = sums[:, h : h + 1] + sums[:, heads + h : heads + h + 1]
            mixed = total[:, h * HEAD : (h + 1) * HEAD] / jnp.where(den > 0.0, den, 1.0)
            mixed = jnp.broadcast_to(mixed.astype(BF)[None], (out_ref.shape[0],) + mixed.shape)
            at = (part * heads + h) * HEAD
            out_ref[:, :, at : at + HEAD] = mixed


def core_rows(place_ref, rows):
    return (
        pl.ds(pl.multiple_of(place_ref[1] * rows, rows), rows),
        pl.ds(pl.multiple_of((1 - place_ref[1]) * rows, rows), rows),
    )


def out_kernel(place_ref, a_ref, w_ref, mine_ref, theirs_ref):
    mine, theirs = core_rows(place_ref, mine_ref.shape[0])
    theirs_ref[...] = dot(a_ref[theirs, :], w_ref[...]).astype(BF)
    mine_ref[...] = dot(a_ref[mine, :], w_ref[...])


def gate_up_kernel(place_ref, own_ref, other_ref, w0, w1, gate2, up2, w3, out_ref, m_ref):
    units = gate2.shape[1]
    step = pl.program_id(0)

    @pl.when(step == 0)
    def _():
        rows = own_ref.shape[0] // 4
        mine, theirs = core_rows(place_ref, rows)
        for d in range(4):
            m_ref[d, mine, :] = own_ref[d * rows : (d + 1) * rows]
            m_ref[d, theirs, :] = other_ref[d * rows : (d + 1) * rows]

    def product(w2):
        total = dot(m_ref[0], w0[...]) + dot(m_ref[1], w1[...])
        return (total + dot(m_ref[2], w2[...]) + dot(m_ref[3], w3[...])).astype(BF)

    @pl.when(step == 0)
    def _():
        out_ref[:, :units] = product(gate2)

    @pl.when(step == 1)
    def _():
        out_ref[:, units : 2 * units] = product(up2)
        square = jnp.zeros((m_ref.shape[1], 1), F32)
        for d in range(4):
            value = m_ref[d].astype(F32)
            square = square + jnp.sum(value * value, axis=1, keepdims=True)
        high = square.astype(BF).astype(F32)
        lane = lax.broadcasted_iota(jnp.int32, (m_ref.shape[1], HEAD), 1)
        extra = jnp.where(lane == 0, high, jnp.where(lane == 1, square - high, 0.0))
        out_ref[:, 2 * units :] = extra.astype(BF)


def down_kernel(place_ref, a_ref, d0, d1, low2, high2, d3, mine_ref, theirs_ref):
    active = a_ref[...]
    half = low2.shape[0]
    rows = mine_ref.shape[1]

    def store(d, total, keep_ref):
        keep_ref[d] = total
        theirs_ref[d] = keep_ref[d, core_rows(place_ref, rows)[1], :].astype(BF)
        mine_ref[d] = keep_ref[d, core_rows(place_ref, rows)[0], :]

    def run(keep_ref):
        store(0, dot(active, d0[...]), keep_ref)
        store(1, dot(active, d1[...]), keep_ref)
        store(2, dot(active[:, :half], low2[...]) + dot(active[:, half:], high2[...]), keep_ref)
        store(3, dot(active, d3[...]), keep_ref)

    pl.run_scoped(run, pltpu.VMEM((4,) + active.shape[:1] + (d0.shape[1],), F32))


def pair_kernel(mine_ref, theirs_ref, own_ref, behind_ref, across_ref, ahead_ref):
    own_ref[...] = mine_ref[0] + theirs_ref[0].astype(F32)
    behind_ref[...] = (mine_ref[1] + theirs_ref[1].astype(F32)).astype(BF)
    across_ref[...] = (mine_ref[2] + theirs_ref[2].astype(F32)).astype(BF)
    ahead_ref[...] = (mine_ref[3] + theirs_ref[3].astype(F32)).astype(BF)


def active_kernel(full_width, parts_ref, out_ref):
    total = jnp.sum(parts_ref[...].astype(F32), axis=0)
    units = out_ref.shape[2]
    square = total[:, 2 * units : 2 * units + 1] + total[:, 2 * units + 1 : 2 * units + 2]
    scale = lax.rsqrt(square * (1.0 / full_width) + EPS)
    gate = total[:, :units] * scale
    up = total[:, units : 2 * units] * scale
    active = (gate / (1.0 + jnp.exp(-gate)) * up).astype(BF)
    out_ref[...] = jnp.broadcast_to(active[None], out_ref.shape)


def shift(value, axis, by):
    n = lax.axis_size(axis)
    return lax.ppermute(value, axis, [(i, (i + by) % n) for i in range(n)])


def after(value, *others):
    return lax.optimization_barrier((value,) + others)[0]


def exchange(value, axis):
    n = lax.axis_size(axis)
    out = lax.all_to_all(value, axis, 0, 0, tiled=True)
    return out.reshape((n, value.shape[0] // n) + value.shape[1:])


def chip_sum(part):
    part = part.astype(BF)
    ahead, behind, across = shift(part, "x", 1), shift(part, "x", -1), shift(part, "x", 2)
    return (part.astype(F32) + across.astype(F32)) + (ahead.astype(F32) + behind.astype(F32))


def shards(
    hidden,
    vision,
    attn_gain,
    q_weight,
    k_weight,
    v_weight,
    q_gain,
    k_gain,
    o_weight,
    gate_logits,
    mlp_gain,
    gate_weight,
    up_weight,
    down_weight,
    image_tiles,
    image_groups,
    image_requests,
):
    groups = lax.axis_size("z") * lax.axis_size("y")
    me = (lax.axis_index("z") * lax.axis_size("y") + lax.axis_index("y")).astype(jnp.int32).reshape(1)
    place = jnp.stack((lax.axis_index("x"), lax.axis_index("c"))).astype(jnp.int32)
    all_rows, width_part = hidden.shape
    own_rows = all_rows // groups
    full_width = width_part * groups
    local_heads = q_weight.shape[1]
    hidden_part = gate_weight.shape[1]
    slot_rows = groups * 2 * SLOTS * STEPS
    key_rows = vision.shape[0]

    sel, row_image = pl.pallas_call(
        route_kernel,
        in_specs=[smem(), vmem(), vmem()],
        out_specs=[vmem(), vmem()],
        out_shape=[
            jax.ShapeDtypeStruct((slot_rows, own_rows), BF),
            jax.ShapeDtypeStruct((slot_rows, 1), jnp.int32),
        ],
        compiler_params=params(),
    )(me, image_groups.reshape(groups, -1), image_requests.reshape(groups, -1))

    hidden_f = hidden.astype(F32)
    normed = (hidden_f * attn_gain).astype(BF)
    q_part = dot(normed, q_weight).astype(BF)
    q_parts = exchange(q_part, GROUP)

    low, high, ahead, behind, own = kv_project(place, vision, k_weight, v_weight)
    q_parts = after(q_parts, own)
    forward, backward = pl.pallas_call(
        kv_merge_kernel,
        in_specs=[vmem()] * 4,
        out_specs=[vmem()] * 2,
        out_shape=[jax.ShapeDtypeStruct(ahead.shape, BF)] * 2,
        compiler_params=params(),
    )(ahead, behind, shift(low, "x", 1), shift(high, "x", -1))
    kv_left = shift(forward, "x", 1)
    kv_right = shift(backward, "x", -1)

    chips_y = lax.axis_size("y")
    units = hidden_part // chips_y
    half = units // 2
    gain = mlp_gain[:, None]

    def columns(weight, d):
        at = lax.rem(lax.axis_index("y") + d, chips_y) * units
        return lax.dynamic_slice_in_dim(weight, at, units, 1).astype(F32)

    def wide(*parts):
        return (jnp.concatenate(parts, axis=1) * gain).astype(BF)

    queries = pl.pallas_call(
        query_kernel,
        in_specs=[vmem()] * 3,
        out_specs=vmem(),
        out_shape=jax.ShapeDtypeStruct((slot_rows, local_heads // 2), BF),
        compiler_params=params(),
    )(q_parts, sel, q_gain.reshape(1, HEAD))
    queries = after(queries, forward, backward)
    later_gate, later_up = lax.optimization_barrier((gate_weight, up_weight, queries))[:2]
    wide_0 = wide(columns(later_gate, 0), columns(later_up, 0))
    wide_1 = shift(wide(columns(later_gate, 1), columns(later_up, 1)), "y", 1)
    wide_3 = shift(wide(columns(later_gate, 3), columns(later_up, 3)), "y", -1)
    queries = lax.all_to_all(queries, GROUP, 0, 0, tiled=True)

    mixed = pl.pallas_call(
        attention_kernel,
        in_specs=[smem(), smem()] + [vmem()] * 6,
        out_specs=vmem(),
        out_shape=jax.ShapeDtypeStruct((slot_rows, local_heads // 2 + HEAD), BF),
        compiler_params=params(),
    )(me, image_tiles, own, kv_left, kv_right, k_gain.reshape(1, HEAD), queries, row_image)
    gate_weight, up_weight, down_weight = lax.optimization_barrier((gate_weight, up_weight, down_weight, mixed))[:3]
    gate_2, up_2 = wide(columns(gate_weight, 2)), wide(columns(up_weight, 2))

    def rows(d, start, size):
        at = lax.rem(lax.axis_index("y") + d, chips_y) * units + start
        return lax.dynamic_slice_in_dim(down_weight, at, size, 0)

    down_0, down_1, down_3 = rows(0, 0, units), rows(1, 0, units), rows(3, 0, units)
    down_2 = rows(2, 0, half), rows(2, half, half)
    mixed = lax.all_to_all(mixed, GROUP, 0, 0, tiled=True)
    mixed = after(mixed, gate_2, up_2, down_1, down_3, *down_2)
    gate_2, up_2 = shift(gate_2, "y", 1), shift(up_2, "y", -1)

    attended = pl.pallas_call(
        combine_kernel,
        in_specs=[vmem()] * 2,
        out_specs=vmem(),
        out_shape=jax.ShapeDtypeStruct((groups, own_rows, local_heads), BF),
        compiler_params=params(),
    )(mixed, sel)
    attended = after(attended, wide_1, wide_3)
    attended = lax.all_to_all(attended, GROUP, 0, 0, tiled=True).reshape(all_rows, local_heads)
    half_rows = all_rows // 2
    first_row = lax.axis_index("c") * half_rows
    half_f = lax.dynamic_slice_in_dim(hidden, first_row, half_rows, 0).astype(F32)
    mine, theirs = pl.pallas_call(
        out_kernel,
        in_specs=[smem(), vmem(), vmem()],
        out_specs=[vmem()] * 2,
        out_shape=[
            jax.ShapeDtypeStruct((half_rows, width_part), F32),
            jax.ShapeDtypeStruct((half_rows, width_part), BF),
        ],
        compiler_params=params(),
    )(place, attended, o_weight)
    pair = (mine + shift(theirs, "c", 1).astype(F32)).astype(BF)
    attn_sum = chip_sum(after(pair, gate_2, up_2))
    gate_2, up_2 = shift(gate_2, "y", 1), shift(up_2, "y", -1)
    middle = (half_f + jnp.tanh(gate_logits[0]) * attn_sum).astype(BF)
    middle_f = middle.astype(F32)
    own_rows_all = jnp.concatenate([middle] + [shift(middle, "y", d) for d in (1, 2, 3)], axis=0)
    other_rows_all = shift(own_rows_all, "c", 1)
    block = pl.BlockSpec((4 * half_rows, width_part), lambda i: (0, 0))
    direct = pl.BlockSpec((width_part, units), lambda i: (0, i))
    passed = pl.BlockSpec((width_part, units), lambda i: (0, 0))
    gate_up = pl.pallas_call(
        gate_up_kernel,
        grid=(2,),
        in_specs=[smem()] + [block] * 2 + [direct] * 2 + [passed] * 2 + [direct],
        out_specs=pl.BlockSpec((all_rows, 2 * units + HEAD), lambda i: (0, 0)),
        out_shape=jax.ShapeDtypeStruct((all_rows, 2 * units + HEAD), BF),
        scratch_shapes=[pltpu.VMEM((4, all_rows, width_part), BF)],
        compiler_params=params(LARGE_VMEM_BYTES),
    )(place, own_rows_all, other_rows_all, wide_0, wide_1, gate_2, up_2, wide_3)
    down_1, down_3, *down_2 = lax.optimization_barrier((down_1, down_3, *down_2, gate_up))[:4]
    down_1, down_3 = shift(down_1, "y", 1), shift(down_3, "y", -1)
    down_2 = shift(down_2[0], "y", 1), shift(down_2[1], "y", -1)
    parts = after(exchange(gate_up, "z"), down_1, down_3, *down_2)
    down_2 = shift(down_2[0], "y", 1), shift(down_2[1], "y", -1)
    active = pl.pallas_call(
        functools.partial(active_kernel, full_width),
        in_specs=[vmem()],
        out_specs=vmem(),
        out_shape=jax.ShapeDtypeStruct(parts.shape[:2] + (units,), BF),
        compiler_params=params(),
    )(parts)
    active = lax.all_to_all(active, "z", 0, 0, tiled=True).reshape(all_rows, units)
    mine, theirs = pl.pallas_call(
        down_kernel,
        in_specs=[smem()] + [vmem()] * 6,
        out_specs=[vmem()] * 2,
        out_shape=[
            jax.ShapeDtypeStruct((4, half_rows, width_part), F32),
            jax.ShapeDtypeStruct((4, half_rows, width_part), BF),
        ],
        compiler_params=params(LARGE_VMEM_BYTES),
    )(place, active, down_0, down_1, *down_2, down_3)
    own_down, behind, across, ahead = pl.pallas_call(
        pair_kernel,
        in_specs=[vmem()] * 2,
        out_specs=[vmem()] * 4,
        out_shape=[jax.ShapeDtypeStruct((half_rows, width_part), F32)]
        + [jax.ShapeDtypeStruct((half_rows, width_part), BF)] * 3,
        compiler_params=params(),
    )(mine, shift(theirs, "c", 1))
    across, behind, ahead = shift(across, "y", 2), shift(behind, "y", -1), shift(ahead, "y", 1)
    down_sum = chip_sum(own_down + across.astype(F32) + behind.astype(F32) + ahead.astype(F32))
    row_request = (jnp.arange(half_rows, dtype=jnp.int32) + first_row) // STEPS
    request_ids = (image_groups * (own_rows // STEPS) + image_requests).reshape(-1)
    has_image = jnp.any(row_request[:, None] == request_ids[None, :], axis=1).astype(F32)
    output = (middle_f + jnp.tanh(gate_logits[1]) * has_image[:, None] * down_sum).astype(BF)
    swapped = shift(output, "c", 1)
    lower = lax.axis_index("c") == 0
    return jnp.concatenate((jnp.where(lower, output, swapped), jnp.where(lower, swapped, output)), axis=0)


def solution(mesh):
    fine = Mesh(mesh.devices.reshape(8, 4, 4, 2), GROUP + TENSOR)
    in_specs = (
        P(None, GROUP),
        P(GROUP, TENSOR),
        P(GROUP),
        P(GROUP, TENSOR),
        P(TENSOR, None),
        P(TENSOR, None),
        P(),
        P(),
        P(TENSOR, GROUP),
        P(),
        P(GROUP),
        P(GROUP, TENSOR),
        P(GROUP, TENSOR),
        P(TENSOR, GROUP),
        P(),
        P(),
        P(),
    )
    return jax.shard_map(shards, mesh=fine, in_specs=in_specs, out_specs=P(None, GROUP), check_vma=False)
```

```python
import functools
import math

import jax
import jax.numpy as jnp
from jax import lax
from jax.experimental import pallas as pl
from jax.experimental.pallas import tpu as pltpu
from jax.sharding import Mesh
from jax.sharding import PartitionSpec as P

GROUP = ("z", "y")
TENSOR = ("x", "c")
HEAD = 128
SLOTS = 2
STEPS = 2
EPS = 1e-05
QUARTERS_SENT = (1, 3, 2)
VMEM_BYTES = 16 * 1024 * 1024
LARGE_VMEM_BYTES = 60 * 1024 * 1024
BF = jnp.bfloat16
F32 = jnp.float32


def params(limit=VMEM_BYTES):
    return pltpu.CompilerParams(vmem_limit_bytes=limit)


def dot(a, b):
    return jnp.dot(a, b, preferred_element_type=F32)


def vmem():
    return pl.BlockSpec(memory_space=pltpu.VMEM)


def smem():
    return pl.BlockSpec(memory_space=pltpu.SMEM)


def route_kernel(me_ref, routes_ref, requests_ref, sel_ref, image_ref):
    me = me_ref[0]
    groups, links = routes_ref.shape
    rows = groups * 2 * SLOTS * STEPS
    row = lax.broadcasted_iota(jnp.int32, (rows, links), 0)
    lane = lax.broadcasted_iota(jnp.int32, (rows, links), 1)
    group_of_row = row >> 3
    slot = (row >> 1) & 1
    step = row & 1
    spread = (group_of_row == lane).astype(F32)
    link = lax.broadcasted_iota(jnp.int32, (groups, links), 1)
    code = (link * 4 + requests_ref[...]).astype(F32)
    route_rows = dot(spread, routes_ref[...].astype(F32))
    code_rows = dot(spread, code)
    hit = route_rows == me.astype(F32)
    first = jnp.min(jnp.where(hit, code_rows, 1e4), axis=1, keepdims=True)
    last = jnp.max(jnp.where(hit, code_rows, -1.0), axis=1, keepdims=True)
    slot1, step1 = slot[:, :1], step[:, :1]
    chosen = jnp.where(slot1 == 0, first, last).astype(jnp.int32)
    found_first = jnp.where(first < 1e3, 1, 0)
    found_last = jnp.where(last > first, 1, 0)
    found = jnp.where(slot1 == 0, found_first, found_last)
    wanted = jnp.where(found == 1, (chosen & 3) * STEPS + step1, -1)
    sel_ref[...] = jnp.where(lane[:, :8] == wanted, 1.0, 0.0).astype(BF)
    mine = routes_ref[pl.ds(me, 1), :]
    here = mine == group_of_row
    first_link = jnp.min(jnp.where(here, lane, 1000), axis=1, keepdims=True)
    last_link = jnp.max(jnp.where(here, lane, -1), axis=1, keepdims=True)
    first_image = jnp.where(first_link < 1000, first_link >> 3, -1)
    last_image = jnp.where(last_link > first_link, last_link >> 3, -1)
    image_ref[...] = jnp.where(slot1 == 0, first_image, last_image)


def kv_kernel(place_ref, x0, x1, k0, v0, k1, v1, low_ref, high_ref, ahead_ref, behind_ref, own_ref):
    total = dot(x0[...], jnp.concatenate((k0[...], v0[...]), axis=1))
    total = total + dot(x1[...], jnp.concatenate((k1[...], v1[...]), axis=1))
    total = total.astype(BF)
    half = low_ref.shape[0]
    step = pl.program_id(0)

    @pl.when(step == 0)
    def _():
        low_ref[...] = total[:half]
        high_ref[...] = total[half:]

    @pl.when(step == 1)
    def _():
        ahead_ref[...] = total

    @pl.when(step == 2)
    def _():
        behind_ref[...] = total

    @pl.when(step == 3)
    def _():
        own_ref[...] = total


def kv_project(place, vision, k_weight, v_weight):
    rows, depth = vision.shape
    chips = 4

    def head(d, place_ref):
        ahead = jnp.where(d == 0, 2, jnp.where(d == 1, 1, jnp.where(d == 2, 3, 0)))
        return 0, lax.rem(place_ref[0] + ahead, chips) * 2 + place_ref[1]

    states = pl.BlockSpec((rows, depth), lambda d, p: (0, 0))
    weights = pl.BlockSpec((depth, HEAD), head)
    sizes = [rows // 2, rows // 2, rows, rows, rows]
    return pl.pallas_call(
        kv_kernel,
        grid_spec=pltpu.PrefetchScalarGridSpec(
            num_scalar_prefetch=1,
            grid=(chips,),
            in_specs=[states] * 2 + [weights] * 4,
            out_specs=[pl.BlockSpec((n, 2 * HEAD), lambda d, p: (0, 0)) for n in sizes],
        ),
        out_shape=[jax.ShapeDtypeStruct((n, 2 * HEAD), BF) for n in sizes],
        compiler_params=params(LARGE_VMEM_BYTES),
    )(
        place,
        vision,
        shift(vision, "c", 1),
        k_weight,
        v_weight,
        shift(k_weight, "c", 1),
        shift(v_weight, "c", 1),
    )


def kv_merge_kernel(ahead_ref, behind_ref, low_ref, high_ref, forward_ref, backward_ref):
    half = low_ref.shape[0]
    forward_ref[:half] = (ahead_ref[:half].astype(F32) + low_ref[...].astype(F32)).astype(BF)
    forward_ref[half:] = ahead_ref[half:]
    backward_ref[:half] = behind_ref[:half]
    backward_ref[half:] = (behind_ref[half:].astype(F32) + high_ref[...].astype(F32)).astype(BF)


def half_of(shape):
    return (lax.broadcasted_iota(jnp.int32, shape, 0) >> 2) & 1


def query_kernel(parts_ref, sel_ref, gain_ref, out_ref):
    total = jnp.sum(parts_ref[...].astype(F32), axis=0)
    gain = gain_ref[...]
    sel = sel_ref[...]
    heads = total.shape[1] // HEAD // 2
    upper = half_of((sel.shape[0], HEAD)) == 1

    def chosen(h):
        v = total[:, h * HEAD : (h + 1) * HEAD]
        scale = lax.rsqrt(jnp.mean(v * v, axis=1, keepdims=True) + EPS)
        return dot(sel, (v * scale * gain).astype(BF))

    for h in range(heads):
        out_ref[:, h * HEAD : (h + 1) * HEAD] = jnp.where(upper, chosen(heads + h), chosen(h)).astype(BF)


def attention_kernel(me_ref, tiles_ref, own_ref, left_ref, right_ref, gain_ref, q_ref, image_ref, out_ref):
    me = me_ref[0]
    total = own_ref[...].astype(F32) + left_ref[...].astype(F32) + right_ref[...].astype(F32)
    k = total[:, :HEAD]
    scale = lax.rsqrt(jnp.mean(k * k, axis=1, keepdims=True) + EPS)
    k = (k * scale * gain_ref[...]).astype(BF)
    v = total[:, HEAD:].astype(BF)
    rows, keys = q_ref.shape[0], k.shape[0]
    tile = lax.broadcasted_iota(jnp.int32, (1, keys), 1) >> 6
    owner = jnp.zeros((1, keys), jnp.int32)
    end = jnp.int32(0)
    for j in range(4):
        end = end + tiles_ref[me, j]
        owner = owner + (tile >= end).astype(jnp.int32)
    allowed = owner == image_ref[...]
    lane = lax.broadcasted_iota(jnp.int32, (rows, HEAD), 1)
    sums = jnp.zeros((rows, HEAD), F32)
    heads = q_ref.shape[1] // HEAD
    for h in range(heads):
        span = slice(h * HEAD, (h + 1) * HEAD)
        score = lax.dot_general(
            q_ref[:, span], k, (((1,), (1,)), ((), ())), preferred_element_type=F32
        )
        weight = jnp.where(allowed, jnp.exp(score * (1.0 / math.sqrt(HEAD))), 0.0)
        den = jnp.sum(weight, axis=1, keepdims=True)
        high = den.astype(BF).astype(F32)
        sums = sums + jnp.where(lane == h, high, 0.0) + jnp.where(lane == heads + h, den - high, 0.0)
        out_ref[:, span] = dot(weight.astype(BF), v).astype(BF)
    out_ref[:, heads * HEAD :] = sums.astype(BF)


def combine_kernel(parts_ref, sel_ref, out_ref):
    sel = sel_ref[...].astype(F32)
    parts = parts_ref[...]
    heads = out_ref.shape[2] // HEAD // 2
    for part in range(2):
        mine = jnp.where(half_of(sel.shape) == part, sel, 0.0).astype(BF)
        total = lax.dot_general(mine, parts, (((0,), (0,)), ((), ())), preferred_element_type=F32)
        sums = total[:, heads * HEAD :]
        for h in range(heads):
            den = sums[:, h : h + 1] + sums[:, heads + h : heads + h + 1]
            mixed = total[:, h * HEAD : (h + 1) * HEAD] / jnp.where(den > 0.0, den, 1.0)
            mixed = jnp.broadcast_to(mixed.astype(BF)[None], (out_ref.shape[0],) + mixed.shape)
            at = (part * heads + h) * HEAD
            out_ref[:, :, at : at + HEAD] = mixed


def core_rows(place_ref, rows):
    return (
        pl.ds(pl.multiple_of(place_ref[1] * rows, rows), rows),
        pl.ds(pl.multiple_of((1 - place_ref[1]) * rows, rows), rows),
    )


def out_kernel(place_ref, a_ref, w_ref, mine_ref, theirs_ref):
    mine, theirs = core_rows(place_ref, mine_ref.shape[0])
    theirs_ref[...] = dot(a_ref[theirs, :], w_ref[...]).astype(BF)
    mine_ref[...] = dot(a_ref[mine, :], w_ref[...])


def quarters_kernel(place_ref, gain_ref, *refs):
    gain = gain_ref[...]
    count = len(QUARTERS_SENT) * 2 if len(refs) > 4 else 2
    inputs, outputs = refs[:count], refs[count:]
    units = inputs[0].shape[1]
    for pair in range(count // 2):
        gate = (inputs[2 * pair][...].astype(F32) * gain).astype(BF)
        up = (inputs[2 * pair + 1][...].astype(F32) * gain).astype(BF)
        if pair < 2:
            outputs[pair][:, :units] = gate
            outputs[pair][:, units:] = up
        else:
            outputs[pair][...] = gate
            outputs[pair + 1][...] = up


def quarters(place, gain, gate_weight, up_weight, sent):
    depth, width = gate_weight.shape
    units, steps = width // 4, 4
    rows = depth // steps
    offsets = QUARTERS_SENT if sent else (0,)

    def quarter(d):
        return pl.BlockSpec((rows, units), lambda i, p: (i, lax.rem(p[2] + d, 4)))

    widths = [2 * units, 2 * units, units, units] if sent else [2 * units]
    return pl.pallas_call(
        quarters_kernel,
        grid_spec=pltpu.PrefetchScalarGridSpec(
            num_scalar_prefetch=1,
            grid=(steps,),
            in_specs=[pl.BlockSpec((rows, 1), lambda i, p: (i, 0))]
            + [spec for d in offsets for spec in (quarter(d), quarter(d))],
            out_specs=[pl.BlockSpec((rows, n), lambda i, p: (i, 0)) for n in widths],
        ),
        out_shape=[jax.ShapeDtypeStruct((depth, n), BF) for n in widths],
        compiler_params=params(LARGE_VMEM_BYTES),
    )(place, gain, *[w for _ in offsets for w in (gate_weight, up_weight)])


def gate_up_kernel(place_ref, own_ref, other_ref, w0, w1, gate2, up2, w3, out_ref, m_ref):
    units = gate2.shape[1]
    step = pl.program_id(0)

    @pl.when(step == 0)
    def _():
        rows = own_ref.shape[0] // 4
        mine, theirs = core_rows(place_ref, rows)
        for d in range(4):
            m_ref[d, mine, :] = own_ref[d * rows : (d + 1) * rows]
            m_ref[d, theirs, :] = other_ref[d * rows : (d + 1) * rows]

    def product(w2):
        total = dot(m_ref[0], w0[...]) + dot(m_ref[1], w1[...])
        return (total + dot(m_ref[2], w2[...]) + dot(m_ref[3], w3[...])).astype(BF)

    @pl.when(step == 0)
    def _():
        out_ref[:, :units] = product(gate2)

    @pl.when(step == 1)
    def _():
        out_ref[:, units : 2 * units] = product(up2)
        square = jnp.zeros((m_ref.shape[1], 1), F32)
        for d in range(4):
            value = m_ref[d].astype(F32)
            square = square + jnp.sum(value * value, axis=1, keepdims=True)
        high = square.astype(BF).astype(F32)
        lane = lax.broadcasted_iota(jnp.int32, (m_ref.shape[1], HEAD), 1)
        extra = jnp.where(lane == 0, high, jnp.where(lane == 1, square - high, 0.0))
        out_ref[:, 2 * units :] = extra.astype(BF)


def down_kernel(place_ref, a_ref, d0, d1, low2, high2, d3, mine_ref, theirs_ref):
    active = a_ref[...]
    half = low2.shape[0]
    rows = mine_ref.shape[1]

    def store(d, total, keep_ref):
        keep_ref[d] = total
        theirs_ref[d] = keep_ref[d, core_rows(place_ref, rows)[1], :].astype(BF)
        mine_ref[d] = keep_ref[d, core_rows(place_ref, rows)[0], :]

    def run(keep_ref):
        store(0, dot(active, d0[...]), keep_ref)
        store(1, dot(active, d1[...]), keep_ref)
        store(2, dot(active[:, :half], low2[...]) + dot(active[:, half:], high2[...]), keep_ref)
        store(3, dot(active, d3[...]), keep_ref)

    pl.run_scoped(run, pltpu.VMEM((4,) + active.shape[:1] + (d0.shape[1],), F32))


def pair_kernel(mine_ref, theirs_ref, own_ref, behind_ref, across_ref, ahead_ref):
    own_ref[...] = mine_ref[0] + theirs_ref[0].astype(F32)
    behind_ref[...] = (mine_ref[1] + theirs_ref[1].astype(F32)).astype(BF)
    across_ref[...] = (mine_ref[2] + theirs_ref[2].astype(F32)).astype(BF)
    ahead_ref[...] = (mine_ref[3] + theirs_ref[3].astype(F32)).astype(BF)


def active_kernel(full_width, parts_ref, out_ref):
    total = jnp.sum(parts_ref[...].astype(F32), axis=0)
    units = out_ref.shape[2]
    square = total[:, 2 * units : 2 * units + 1] + total[:, 2 * units + 1 : 2 * units + 2]
    scale = lax.rsqrt(square * (1.0 / full_width) + EPS)
    gate = total[:, :units] * scale
    up = total[:, units : 2 * units] * scale
    active = (gate / (1.0 + jnp.exp(-gate)) * up).astype(BF)
    out_ref[...] = jnp.broadcast_to(active[None], out_ref.shape)


def shift(value, axis, by):
    n = lax.axis_size(axis)
    return lax.ppermute(value, axis, [(i, (i + by) % n) for i in range(n)])


def after(value, *others):
    return lax.optimization_barrier((value,) + others)[0]


def exchange(value, axis):
    n = lax.axis_size(axis)
    out = lax.all_to_all(value, axis, 0, 0, tiled=True)
    return out.reshape((n, value.shape[0] // n) + value.shape[1:])


def chip_sum(part):
    part = part.astype(BF)
    ahead, behind, across = shift(part, "x", 1), shift(part, "x", -1), shift(part, "x", 2)
    return (part.astype(F32) + across.astype(F32)) + (ahead.astype(F32) + behind.astype(F32))


def shards(
    hidden,
    vision,
    attn_gain,
    q_weight,
    k_weight,
    v_weight,
    q_gain,
    k_gain,
    o_weight,
    gate_logits,
    mlp_gain,
    gate_weight,
    up_weight,
    down_weight,
    image_tiles,
    image_groups,
    image_requests,
):
    groups = lax.axis_size("z") * lax.axis_size("y")
    me = (lax.axis_index("z") * lax.axis_size("y") + lax.axis_index("y")).astype(jnp.int32).reshape(1)
    place = jnp.stack((lax.axis_index("x"), lax.axis_index("c"), lax.axis_index("y"))).astype(jnp.int32)
    all_rows, width_part = hidden.shape
    own_rows = all_rows // groups
    full_width = width_part * groups
    local_heads = q_weight.shape[1]
    hidden_part = gate_weight.shape[1]
    slot_rows = groups * 2 * SLOTS * STEPS
    key_rows = vision.shape[0]

    sel, row_image = pl.pallas_call(
        route_kernel,
        in_specs=[smem(), vmem(), vmem()],
        out_specs=[vmem(), vmem()],
        out_shape=[
            jax.ShapeDtypeStruct((slot_rows, own_rows), BF),
            jax.ShapeDtypeStruct((slot_rows, 1), jnp.int32),
        ],
        compiler_params=params(),
    )(me, image_groups.reshape(groups, -1), image_requests.reshape(groups, -1))

    hidden_f = hidden.astype(F32)
    normed = (hidden_f * attn_gain).astype(BF)
    q_part = dot(normed, q_weight).astype(BF)
    q_parts = exchange(q_part, GROUP)

    low, high, ahead, behind, own = kv_project(place, vision, k_weight, v_weight)
    q_parts = after(q_parts, own)
    forward, backward = pl.pallas_call(
        kv_merge_kernel,
        in_specs=[vmem()] * 4,
        out_specs=[vmem()] * 2,
        out_shape=[jax.ShapeDtypeStruct(ahead.shape, BF)] * 2,
        compiler_params=params(),
    )(ahead, behind, shift(low, "x", 1), shift(high, "x", -1))
    kv_left = shift(forward, "x", 1)
    kv_right = shift(backward, "x", -1)

    chips_y = lax.axis_size("y")
    units = hidden_part // chips_y
    half = units // 2
    gain = mlp_gain[:, None]

    queries = pl.pallas_call(
        query_kernel,
        in_specs=[vmem()] * 3,
        out_specs=vmem(),
        out_shape=jax.ShapeDtypeStruct((slot_rows, local_heads // 2), BF),
        compiler_params=params(),
    )(q_parts, sel, q_gain.reshape(1, HEAD))
    queries = after(queries, forward, backward)
    first_gate, first_up = lax.optimization_barrier((gate_weight, up_weight, queries))[:2]
    wide_1, wide_3, gate_2, up_2 = quarters(place, gain, first_gate, first_up, True)
    gate_2, up_2 = shift(gate_2, "y", 1), shift(up_2, "y", -1)
    wide_1, wide_3 = shift(wide_1, "y", 1), shift(wide_3, "y", -1)
    queries = lax.all_to_all(queries, GROUP, 0, 0, tiled=True)

    mixed = pl.pallas_call(
        attention_kernel,
        in_specs=[smem(), smem()] + [vmem()] * 6,
        out_specs=vmem(),
        out_shape=jax.ShapeDtypeStruct((slot_rows, local_heads // 2 + HEAD), BF),
        compiler_params=params(),
    )(me, image_tiles, own, kv_left, kv_right, k_gain.reshape(1, HEAD), queries, row_image)
    gate_weight, up_weight, down_weight = lax.optimization_barrier((gate_weight, up_weight, down_weight, mixed))[:3]
    (wide_0,) = quarters(place, gain, gate_weight, up_weight, False)

    def rows(d, start, size):
        at = lax.rem(lax.axis_index("y") + d, chips_y) * units + start
        return lax.dynamic_slice_in_dim(down_weight, at, size, 0)

    down_0, down_1, down_3 = rows(0, 0, units), rows(1, 0, units), rows(3, 0, units)
    down_2 = rows(2, 0, half), rows(2, half, half)
    mixed = lax.all_to_all(mixed, GROUP, 0, 0, tiled=True)
    mixed = after(mixed, wide_0, down_1, down_3, *down_2)
    gate_2, up_2 = shift(gate_2, "y", 1), shift(up_2, "y", -1)

    attended = pl.pallas_call(
        combine_kernel,
        in_specs=[vmem()] * 2,
        out_specs=vmem(),
        out_shape=jax.ShapeDtypeStruct((groups, own_rows, local_heads), BF),
        compiler_params=params(),
    )(mixed, sel)
    attended = after(attended, wide_1, wide_3)
    attended = lax.all_to_all(attended, GROUP, 0, 0, tiled=True).reshape(all_rows, local_heads)
    half_rows = all_rows // 2
    first_row = lax.axis_index("c") * half_rows
    half_f = lax.dynamic_slice_in_dim(hidden, first_row, half_rows, 0).astype(F32)
    mine, theirs = pl.pallas_call(
        out_kernel,
        in_specs=[smem(), vmem(), vmem()],
        out_specs=[vmem()] * 2,
        out_shape=[
            jax.ShapeDtypeStruct((half_rows, width_part), F32),
            jax.ShapeDtypeStruct((half_rows, width_part), BF),
        ],
        compiler_params=params(),
    )(place, attended, o_weight)
    pair = (mine + shift(theirs, "c", 1).astype(F32)).astype(BF)
    attn_sum = chip_sum(pair)
    middle = (half_f + jnp.tanh(gate_logits[0]) * attn_sum).astype(BF)
    middle = after(middle, gate_2, up_2)
    middle_f = middle.astype(F32)
    own_rows_all = jnp.concatenate([middle] + [shift(middle, "y", d) for d in (1, 2, 3)], axis=0)
    other_rows_all = shift(own_rows_all, "c", 1)
    block = pl.BlockSpec((4 * half_rows, width_part), lambda i: (0, 0))
    direct = pl.BlockSpec((width_part, units), lambda i: (0, i))
    passed = pl.BlockSpec((width_part, units), lambda i: (0, 0))
    gate_up = pl.pallas_call(
        gate_up_kernel,
        grid=(2,),
        in_specs=[smem()] + [block] * 2 + [direct] * 2 + [passed] * 2 + [direct],
        out_specs=pl.BlockSpec((all_rows, 2 * units + HEAD), lambda i: (0, 0)),
        out_shape=jax.ShapeDtypeStruct((all_rows, 2 * units + HEAD), BF),
        scratch_shapes=[pltpu.VMEM((4, all_rows, width_part), BF)],
        compiler_params=params(LARGE_VMEM_BYTES),
    )(place, own_rows_all, other_rows_all, wide_0, wide_1, gate_2, up_2, wide_3)
    down_1, down_3, *down_2 = lax.optimization_barrier((down_1, down_3, *down_2, gate_up))[:4]
    down_1, down_3 = shift(down_1, "y", 1), shift(down_3, "y", -1)
    down_2 = shift(down_2[0], "y", 1), shift(down_2[1], "y", -1)
    parts = after(exchange(gate_up, "z"), down_1, down_3, *down_2)
    down_2 = shift(down_2[0], "y", 1), shift(down_2[1], "y", -1)
    active = pl.pallas_call(
        functools.partial(active_kernel, full_width),
        in_specs=[vmem()],
        out_specs=vmem(),
        out_shape=jax.ShapeDtypeStruct(parts.shape[:2] + (units,), BF),
        compiler_params=params(),
    )(parts)
    active = lax.all_to_all(active, "z", 0, 0, tiled=True).reshape(all_rows, units)
    mine, theirs = pl.pallas_call(
        down_kernel,
        in_specs=[smem()] + [vmem()] * 6,
        out_specs=[vmem()] * 2,
        out_shape=[
            jax.ShapeDtypeStruct((4, half_rows, width_part), F32),
            jax.ShapeDtypeStruct((4, half_rows, width_part), BF),
        ],
        compiler_params=params(),
    )(place, active, down_0, down_1, *down_2, down_3)
    own_down, behind, across, ahead = pl.pallas_call(
        pair_kernel,
        in_specs=[vmem()] * 2,
        out_specs=[vmem()] * 4,
        out_shape=[jax.ShapeDtypeStruct((half_rows, width_part), F32)]
        + [jax.ShapeDtypeStruct((half_rows, width_part), BF)] * 3,
        compiler_params=params(),
    )(mine, shift(theirs, "c", 1))
    across, behind, ahead = shift(across, "y", 2), shift(behind, "y", -1), shift(ahead, "y", 1)
    down_sum = chip_sum(own_down + across.astype(F32) + behind.astype(F32) + ahead.astype(F32))
    row_request = (jnp.arange(half_rows, dtype=jnp.int32) + first_row) // STEPS
    request_ids = (image_groups * (own_rows // STEPS) + image_requests).reshape(-1)
    has_image = jnp.any(row_request[:, None] == request_ids[None, :], axis=1).astype(F32)
    output = (middle_f + jnp.tanh(gate_logits[1]) * has_image[:, None] * down_sum).astype(BF)
    swapped = shift(output, "c", 1)
    lower = lax.axis_index("c") == 0
    return jnp.concatenate((jnp.where(lower, output, swapped), jnp.where(lower, swapped, output)), axis=0)


def solution(mesh):
    fine = Mesh(mesh.devices.reshape(8, 4, 4, 2), GROUP + TENSOR)
    in_specs = (
        P(None, GROUP),
        P(GROUP, TENSOR),
        P(GROUP),
        P(GROUP, TENSOR),
        P(TENSOR, None),
        P(TENSOR, None),
        P(),
        P(),
        P(TENSOR, GROUP),
        P(),
        P(GROUP),
        P(GROUP, TENSOR),
        P(GROUP, TENSOR),
        P(TENSOR, GROUP),
        P(),
        P(),
        P(),
    )
    return jax.shard_map(shards, mesh=fine, in_specs=in_specs, out_specs=P(None, GROUP), check_vma=False)
```

```python
import functools
import math

import jax
import jax.numpy as jnp
from jax import lax
from jax.experimental import pallas as pl
from jax.experimental.pallas import tpu as pltpu
from jax.sharding import Mesh
from jax.sharding import PartitionSpec as P

GROUP = ("z", "y")
TENSOR = ("x", "c")
HEAD = 128
SLOTS = 2
STEPS = 2
EPS = 1e-05
VMEM_BYTES = 16 * 1024 * 1024
LARGE_VMEM_BYTES = 60 * 1024 * 1024
BF = jnp.bfloat16
F32 = jnp.float32


def params(limit=VMEM_BYTES):
    return pltpu.CompilerParams(vmem_limit_bytes=limit)


def dot(a, b):
    return jnp.dot(a, b, preferred_element_type=F32)


def vmem():
    return pl.BlockSpec(memory_space=pltpu.VMEM)


def smem():
    return pl.BlockSpec(memory_space=pltpu.SMEM)


def route_kernel(me_ref, routes_ref, requests_ref, sel_ref, image_ref):
    me = me_ref[0]
    groups, links = routes_ref.shape
    rows = groups * 2 * SLOTS * STEPS
    row = lax.broadcasted_iota(jnp.int32, (rows, links), 0)
    lane = lax.broadcasted_iota(jnp.int32, (rows, links), 1)
    group_of_row = row >> 3
    slot = (row >> 1) & 1
    step = row & 1
    spread = (group_of_row == lane).astype(F32)
    link = lax.broadcasted_iota(jnp.int32, (groups, links), 1)
    code = (link * 4 + requests_ref[...]).astype(F32)
    route_rows = dot(spread, routes_ref[...].astype(F32))
    code_rows = dot(spread, code)
    hit = route_rows == me.astype(F32)
    first = jnp.min(jnp.where(hit, code_rows, 1e4), axis=1, keepdims=True)
    last = jnp.max(jnp.where(hit, code_rows, -1.0), axis=1, keepdims=True)
    slot1, step1 = slot[:, :1], step[:, :1]
    chosen = jnp.where(slot1 == 0, first, last).astype(jnp.int32)
    found_first = jnp.where(first < 1e3, 1, 0)
    found_last = jnp.where(last > first, 1, 0)
    found = jnp.where(slot1 == 0, found_first, found_last)
    wanted = jnp.where(found == 1, (chosen & 3) * STEPS + step1, -1)
    sel_ref[...] = jnp.where(lane[:, :8] == wanted, 1.0, 0.0).astype(BF)
    mine = routes_ref[pl.ds(me, 1), :]
    here = mine == group_of_row
    first_link = jnp.min(jnp.where(here, lane, 1000), axis=1, keepdims=True)
    last_link = jnp.max(jnp.where(here, lane, -1), axis=1, keepdims=True)
    first_image = jnp.where(first_link < 1000, first_link >> 3, -1)
    last_image = jnp.where(last_link > first_link, last_link >> 3, -1)
    image_ref[...] = jnp.where(slot1 == 0, first_image, last_image)


def kv_kernel(place_ref, x0, x1, k0, v0, k1, v1, low_ref, high_ref, ahead_ref, behind_ref, own_ref):
    total = dot(x0[...], jnp.concatenate((k0[...], v0[...]), axis=1))
    total = total + dot(x1[...], jnp.concatenate((k1[...], v1[...]), axis=1))
    total = total.astype(BF)
    half = low_ref.shape[0]
    step = pl.program_id(0)

    @pl.when(step == 0)
    def _():
        low_ref[...] = total[:half]
        high_ref[...] = total[half:]

    @pl.when(step == 1)
    def _():
        ahead_ref[...] = total

    @pl.when(step == 2)
    def _():
        behind_ref[...] = total

    @pl.when(step == 3)
    def _():
        own_ref[...] = total


def kv_project(place, vision, k_weight, v_weight):
    rows, depth = vision.shape
    chips = 4

    def head(d, place_ref):
        ahead = jnp.where(d == 0, 2, jnp.where(d == 1, 1, jnp.where(d == 2, 3, 0)))
        return 0, lax.rem(place_ref[0] + ahead, chips) * 2 + place_ref[1]

    states = pl.BlockSpec((rows, depth), lambda d, p: (0, 0))
    weights = pl.BlockSpec((depth, HEAD), head)
    sizes = [rows // 2, rows // 2, rows, rows, rows]
    return pl.pallas_call(
        kv_kernel,
        grid_spec=pltpu.PrefetchScalarGridSpec(
            num_scalar_prefetch=1,
            grid=(chips,),
            in_specs=[states] * 2 + [weights] * 4,
            out_specs=[pl.BlockSpec((n, 2 * HEAD), lambda d, p: (0, 0)) for n in sizes],
        ),
        out_shape=[jax.ShapeDtypeStruct((n, 2 * HEAD), BF) for n in sizes],
        compiler_params=params(LARGE_VMEM_BYTES),
    )(
        place,
        vision,
        shift(vision, "c", 1),
        k_weight,
        v_weight,
        shift(k_weight, "c", 1),
        shift(v_weight, "c", 1),
    )


def kv_merge_kernel(ahead_ref, behind_ref, low_ref, high_ref, forward_ref, backward_ref):
    half = low_ref.shape[0]
    forward_ref[:half] = (ahead_ref[:half].astype(F32) + low_ref[...].astype(F32)).astype(BF)
    forward_ref[half:] = ahead_ref[half:]
    backward_ref[:half] = behind_ref[:half]
    backward_ref[half:] = (behind_ref[half:].astype(F32) + high_ref[...].astype(F32)).astype(BF)


def half_of(shape):
    return (lax.broadcasted_iota(jnp.int32, shape, 0) >> 2) & 1


def query_kernel(parts_ref, sel_ref, gain_ref, out_ref):
    total = jnp.sum(parts_ref[...].astype(F32), axis=0)
    gain = gain_ref[...]
    sel = sel_ref[...]
    heads = total.shape[1] // HEAD // 2
    upper = half_of((sel.shape[0], HEAD)) == 1

    def chosen(h):
        v = total[:, h * HEAD : (h + 1) * HEAD]
        scale = lax.rsqrt(jnp.mean(v * v, axis=1, keepdims=True) + EPS)
        return dot(sel, (v * scale * gain).astype(BF))

    for h in range(heads):
        out_ref[:, h * HEAD : (h + 1) * HEAD] = jnp.where(upper, chosen(heads + h), chosen(h)).astype(BF)


def attention_kernel(me_ref, tiles_ref, own_ref, left_ref, right_ref, gain_ref, q_ref, image_ref, out_ref):
    me = me_ref[0]
    total = own_ref[...].astype(F32) + left_ref[...].astype(F32) + right_ref[...].astype(F32)
    k = total[:, :HEAD]
    scale = lax.rsqrt(jnp.mean(k * k, axis=1, keepdims=True) + EPS)
    k = (k * scale * gain_ref[...]).astype(BF)
    v = total[:, HEAD:].astype(BF)
    rows, keys = q_ref.shape[0], k.shape[0]
    tile = lax.broadcasted_iota(jnp.int32, (1, keys), 1) >> 6
    owner = jnp.zeros((1, keys), jnp.int32)
    end = jnp.int32(0)
    for j in range(4):
        end = end + tiles_ref[me, j]
        owner = owner + (tile >= end).astype(jnp.int32)
    allowed = owner == image_ref[...]
    lane = lax.broadcasted_iota(jnp.int32, (rows, HEAD), 1)
    sums = jnp.zeros((rows, HEAD), F32)
    heads = q_ref.shape[1] // HEAD
    for h in range(heads):
        span = slice(h * HEAD, (h + 1) * HEAD)
        score = lax.dot_general(
            q_ref[:, span], k, (((1,), (1,)), ((), ())), preferred_element_type=F32
        )
        weight = jnp.where(allowed, jnp.exp(score * (1.0 / math.sqrt(HEAD))), 0.0)
        den = jnp.sum(weight, axis=1, keepdims=True)
        high = den.astype(BF).astype(F32)
        sums = sums + jnp.where(lane == h, high, 0.0) + jnp.where(lane == heads + h, den - high, 0.0)
        out_ref[:, span] = dot(weight.astype(BF), v).astype(BF)
    out_ref[:, heads * HEAD :] = sums.astype(BF)


def combine_kernel(parts_ref, sel_ref, out_ref):
    sel = sel_ref[...].astype(F32)
    parts = parts_ref[...]
    heads = out_ref.shape[2] // HEAD // 2
    for part in range(2):
        mine = jnp.where(half_of(sel.shape) == part, sel, 0.0).astype(BF)
        total = lax.dot_general(mine, parts, (((0,), (0,)), ((), ())), preferred_element_type=F32)
        sums = total[:, heads * HEAD :]
        for h in range(heads):
            den = sums[:, h : h + 1] + sums[:, heads + h : heads + h + 1]
            mixed = total[:, h * HEAD : (h + 1) * HEAD] / jnp.where(den > 0.0, den, 1.0)
            mixed = jnp.broadcast_to(mixed.astype(BF)[None], (out_ref.shape[0],) + mixed.shape)
            at = (part * heads + h) * HEAD
            out_ref[:, :, at : at + HEAD] = mixed


def core_rows(place_ref, rows):
    return (
        pl.ds(pl.multiple_of(place_ref[1] * rows, rows), rows),
        pl.ds(pl.multiple_of((1 - place_ref[1]) * rows, rows), rows),
    )


def out_kernel(place_ref, a_ref, w_ref, mine_ref, theirs_ref):
    mine, theirs = core_rows(place_ref, mine_ref.shape[0])
    theirs_ref[...] = dot(a_ref[theirs, :], w_ref[...]).astype(BF)
    mine_ref[...] = dot(a_ref[mine, :], w_ref[...])


def gate_up_kernel(place_ref, own_ref, other_ref, w0, w1, gate2, up2, w3, out_ref, m_ref):
    units = gate2.shape[1]
    step = pl.program_id(0)

    @pl.when(step == 0)
    def _():
        rows = own_ref.shape[0] // 4
        mine, theirs = core_rows(place_ref, rows)
        for d in range(4):
            m_ref[d, mine, :] = own_ref[d * rows : (d + 1) * rows]
            m_ref[d, theirs, :] = other_ref[d * rows : (d + 1) * rows]

    def product(w2):
        total = dot(m_ref[0], w0[...]) + dot(m_ref[1], w1[...])
        return (total + dot(m_ref[2], w2[...]) + dot(m_ref[3], w3[...])).astype(BF)

    @pl.when(step == 0)
    def _():
        out_ref[:, :units] = product(gate2)

    @pl.when(step == 1)
    def _():
        out_ref[:, units : 2 * units] = product(up2)
        square = jnp.zeros((m_ref.shape[1], 1), F32)
        for d in range(4):
            value = m_ref[d].astype(F32)
            square = square + jnp.sum(value * value, axis=1, keepdims=True)
        high = square.astype(BF).astype(F32)
        lane = lax.broadcasted_iota(jnp.int32, (m_ref.shape[1], HEAD), 1)
        extra = jnp.where(lane == 0, high, jnp.where(lane == 1, square - high, 0.0))
        out_ref[:, 2 * units :] = extra.astype(BF)


def down_kernel(place_ref, a_ref, d0, d1, low2, high2, d3, mine_ref, theirs_ref):
    active = a_ref[...]
    half = low2.shape[0]
    rows = mine_ref.shape[1]

    def store(d, total, keep_ref):
        keep_ref[d] = total
        theirs_ref[d] = keep_ref[d, core_rows(place_ref, rows)[1], :].astype(BF)
        mine_ref[d] = keep_ref[d, core_rows(place_ref, rows)[0], :]

    def run(keep_ref):
        store(0, dot(active, d0[...]), keep_ref)
        store(1, dot(active, d1[...]), keep_ref)
        store(2, dot(active[:, :half], low2[...]) + dot(active[:, half:], high2[...]), keep_ref)
        store(3, dot(active, d3[...]), keep_ref)

    pl.run_scoped(run, pltpu.VMEM((4,) + active.shape[:1] + (d0.shape[1],), F32))


def pair_kernel(mine_ref, theirs_ref, own_ref, behind_ref, across_ref, ahead_ref):
    own_ref[...] = mine_ref[0] + theirs_ref[0].astype(F32)
    behind_ref[...] = (mine_ref[1] + theirs_ref[1].astype(F32)).astype(BF)
    across_ref[...] = (mine_ref[2] + theirs_ref[2].astype(F32)).astype(BF)
    ahead_ref[...] = (mine_ref[3] + theirs_ref[3].astype(F32)).astype(BF)


def active_kernel(full_width, parts_ref, out_ref):
    total = jnp.sum(parts_ref[...].astype(F32), axis=0)
    units = out_ref.shape[2]
    square = total[:, 2 * units : 2 * units + 1] + total[:, 2 * units + 1 : 2 * units + 2]
    scale = lax.rsqrt(square * (1.0 / full_width) + EPS)
    gate = total[:, :units] * scale
    up = total[:, units : 2 * units] * scale
    active = (gate / (1.0 + jnp.exp(-gate)) * up).astype(BF)
    out_ref[...] = jnp.broadcast_to(active[None], out_ref.shape)


def shift(value, axis, by):
    n = lax.axis_size(axis)
    return lax.ppermute(value, axis, [(i, (i + by) % n) for i in range(n)])


def after(value, *others):
    return lax.optimization_barrier((value,) + others)[0]


def exchange(value, axis):
    n = lax.axis_size(axis)
    out = lax.all_to_all(value, axis, 0, 0, tiled=True)
    return out.reshape((n, value.shape[0] // n) + value.shape[1:])


def chip_sum(part):
    part = part.astype(BF)
    ahead, behind, across = shift(part, "x", 1), shift(part, "x", -1), shift(part, "x", 2)
    return (part.astype(F32) + across.astype(F32)) + (ahead.astype(F32) + behind.astype(F32))


def shards(
    hidden,
    vision,
    attn_gain,
    q_weight,
    k_weight,
    v_weight,
    q_gain,
    k_gain,
    o_weight,
    gate_logits,
    mlp_gain,
    gate_weight,
    up_weight,
    down_weight,
    image_tiles,
    image_groups,
    image_requests,
):
    groups = lax.axis_size("z") * lax.axis_size("y")
    me = (lax.axis_index("z") * lax.axis_size("y") + lax.axis_index("y")).astype(jnp.int32).reshape(1)
    place = jnp.stack((lax.axis_index("x"), lax.axis_index("c"))).astype(jnp.int32)
    all_rows, width_part = hidden.shape
    own_rows = all_rows // groups
    full_width = width_part * groups
    local_heads = q_weight.shape[1]
    hidden_part = gate_weight.shape[1]
    slot_rows = groups * 2 * SLOTS * STEPS
    key_rows = vision.shape[0]

    sel, row_image = pl.pallas_call(
        route_kernel,
        in_specs=[smem(), vmem(), vmem()],
        out_specs=[vmem(), vmem()],
        out_shape=[
            jax.ShapeDtypeStruct((slot_rows, own_rows), BF),
            jax.ShapeDtypeStruct((slot_rows, 1), jnp.int32),
        ],
        compiler_params=params(),
    )(me, image_groups.reshape(groups, -1), image_requests.reshape(groups, -1))

    hidden = after(hidden, place)
    hidden_f = hidden.astype(F32)
    normed = (hidden_f * attn_gain).astype(BF)
    q_part = dot(normed, q_weight).astype(BF)
    q_parts = exchange(q_part, GROUP)

    low, high, ahead, behind, own = kv_project(place, vision, k_weight, v_weight)
    q_parts = after(q_parts, own)
    forward, backward = pl.pallas_call(
        kv_merge_kernel,
        in_specs=[vmem()] * 4,
        out_specs=[vmem()] * 2,
        out_shape=[jax.ShapeDtypeStruct(ahead.shape, BF)] * 2,
        compiler_params=params(LARGE_VMEM_BYTES),
    )(ahead, behind, shift(low, "x", 1), shift(high, "x", -1))
    kv_left = shift(forward, "x", 1)
    kv_right = shift(backward, "x", -1)

    chips_y = lax.axis_size("y")
    units = hidden_part // chips_y
    half = units // 2
    gain = mlp_gain[:, None]

    def columns(weight, d):
        at = lax.rem(lax.axis_index("y") + d, chips_y) * units
        return lax.dynamic_slice_in_dim(weight, at, units, 1).astype(F32)

    def wide(*parts):
        return (jnp.concatenate(parts, axis=1) * gain).astype(BF)

    queries = pl.pallas_call(
        query_kernel,
        in_specs=[vmem()] * 3,
        out_specs=vmem(),
        out_shape=jax.ShapeDtypeStruct((slot_rows, local_heads // 2), BF),
        compiler_params=params(),
    )(q_parts, sel, q_gain.reshape(1, HEAD))
    queries = after(queries, forward, backward)
    later_gate, later_up = lax.optimization_barrier((gate_weight, up_weight, queries))[:2]
    wide_0 = wide(columns(later_gate, 0), columns(later_up, 0))
    wide_1 = shift(wide(columns(later_gate, 1), columns(later_up, 1)), "y", 1)
    wide_3 = shift(wide(columns(later_gate, 3), columns(later_up, 3)), "y", -1)
    queries = lax.all_to_all(queries, GROUP, 0, 0, tiled=True)

    mixed = pl.pallas_call(
        attention_kernel,
        in_specs=[smem(), smem()] + [vmem()] * 6,
        out_specs=vmem(),
        out_shape=jax.ShapeDtypeStruct((slot_rows, local_heads // 2 + HEAD), BF),
        compiler_params=params(),
    )(me, image_tiles, own, kv_left, kv_right, k_gain.reshape(1, HEAD), queries, row_image)
    gate_weight, up_weight, down_weight = lax.optimization_barrier((gate_weight, up_weight, down_weight, mixed))[:3]
    gate_2, up_2 = wide(columns(gate_weight, 2)), wide(columns(up_weight, 2))

    def rows(d, start, size):
        at = lax.rem(lax.axis_index("y") + d, chips_y) * units + start
        return lax.dynamic_slice_in_dim(down_weight, at, size, 0)

    down_0, down_1, down_3 = rows(0, 0, units), rows(1, 0, units), rows(3, 0, units)
    down_2 = rows(2, 0, half), rows(2, half, half)
    mixed = lax.all_to_all(mixed, GROUP, 0, 0, tiled=True)
    mixed = after(mixed, gate_2, up_2, down_1, down_3, *down_2)
    gate_2, up_2 = shift(gate_2, "y", 1), shift(up_2, "y", -1)

    attended = pl.pallas_call(
        combine_kernel,
        in_specs=[vmem()] * 2,
        out_specs=vmem(),
        out_shape=jax.ShapeDtypeStruct((groups, own_rows, local_heads), BF),
        compiler_params=params(),
    )(mixed, sel)
    attended = after(attended, wide_1, wide_3)
    attended = lax.all_to_all(attended, GROUP, 0, 0, tiled=True).reshape(all_rows, local_heads)
    half_rows = all_rows // 2
    first_row = lax.axis_index("c") * half_rows
    half_f = lax.dynamic_slice_in_dim(hidden, first_row, half_rows, 0).astype(F32)
    mine, theirs = pl.pallas_call(
        out_kernel,
        in_specs=[smem(), vmem(), vmem()],
        out_specs=[vmem()] * 2,
        out_shape=[
            jax.ShapeDtypeStruct((half_rows, width_part), F32),
            jax.ShapeDtypeStruct((half_rows, width_part), BF),
        ],
        compiler_params=params(),
    )(place, attended, o_weight)
    pair = (mine + shift(theirs, "c", 1).astype(F32)).astype(BF)
    attn_sum = chip_sum(pair)
    gate_2, up_2 = shift(gate_2, "y", 1), shift(up_2, "y", -1)
    middle = (half_f + jnp.tanh(gate_logits[0]) * attn_sum).astype(BF)
    middle = after(middle, gate_2, up_2)
    middle_f = middle.astype(F32)
    own_rows_all = jnp.concatenate([middle] + [shift(middle, "y", d) for d in (1, 2, 3)], axis=0)
    other_rows_all = shift(own_rows_all, "c", 1)
    block = pl.BlockSpec((4 * half_rows, width_part), lambda i: (0, 0))
    direct = pl.BlockSpec((width_part, units), lambda i: (0, i))
    passed = pl.BlockSpec((width_part, units), lambda i: (0, 0))
    gate_up = pl.pallas_call(
        gate_up_kernel,
        grid=(2,),
        in_specs=[smem()] + [block] * 2 + [direct] * 2 + [passed] * 2 + [direct],
        out_specs=pl.BlockSpec((all_rows, 2 * units + HEAD), lambda i: (0, 0)),
        out_shape=jax.ShapeDtypeStruct((all_rows, 2 * units + HEAD), BF),
        scratch_shapes=[pltpu.VMEM((4, all_rows, width_part), BF)],
        compiler_params=params(LARGE_VMEM_BYTES),
    )(place, own_rows_all, other_rows_all, wide_0, wide_1, gate_2, up_2, wide_3)
    down_1, down_3, *down_2 = lax.optimization_barrier((down_1, down_3, *down_2, gate_up))[:4]
    down_1, down_3 = shift(down_1, "y", 1), shift(down_3, "y", -1)
    down_2 = shift(down_2[0], "y", 1), shift(down_2[1], "y", -1)
    parts = after(exchange(gate_up, "z"), down_1, down_3, *down_2)
    down_2 = shift(down_2[0], "y", 1), shift(down_2[1], "y", -1)
    active = pl.pallas_call(
        functools.partial(active_kernel, full_width),
        in_specs=[vmem()],
        out_specs=vmem(),
        out_shape=jax.ShapeDtypeStruct(parts.shape[:2] + (units,), BF),
        compiler_params=params(),
    )(parts)
    active = lax.all_to_all(active, "z", 0, 0, tiled=True).reshape(all_rows, units)
    mine, theirs = pl.pallas_call(
        down_kernel,
        in_specs=[smem()] + [vmem()] * 6,
        out_specs=[vmem()] * 2,
        out_shape=[
            jax.ShapeDtypeStruct((4, half_rows, width_part), F32),
            jax.ShapeDtypeStruct((4, half_rows, width_part), BF),
        ],
        compiler_params=params(),
    )(place, active, down_0, down_1, *down_2, down_3)
    own_down, behind, across, ahead = pl.pallas_call(
        pair_kernel,
        in_specs=[vmem()] * 2,
        out_specs=[vmem()] * 4,
        out_shape=[jax.ShapeDtypeStruct((half_rows, width_part), F32)]
        + [jax.ShapeDtypeStruct((half_rows, width_part), BF)] * 3,
        compiler_params=params(),
    )(mine, shift(theirs, "c", 1))
    across, behind, ahead = shift(across, "y", 2), shift(behind, "y", -1), shift(ahead, "y", 1)
    down_sum = chip_sum(own_down + across.astype(F32) + behind.astype(F32) + ahead.astype(F32))
    row_request = (jnp.arange(half_rows, dtype=jnp.int32) + first_row) // STEPS
    request_ids = (image_groups * (own_rows // STEPS) + image_requests).reshape(-1)
    has_image = jnp.any(row_request[:, None] == request_ids[None, :], axis=1).astype(F32)
    output = (middle_f + jnp.tanh(gate_logits[1]) * has_image[:, None] * down_sum).astype(BF)
    swapped = shift(output, "c", 1)
    lower = lax.axis_index("c") == 0
    return jnp.concatenate((jnp.where(lower, output, swapped), jnp.where(lower, swapped, output)), axis=0)


def solution(mesh):
    fine = Mesh(mesh.devices.reshape(8, 4, 4, 2), GROUP + TENSOR)
    in_specs = (
        P(None, GROUP),
        P(GROUP, TENSOR),
        P(GROUP),
        P(GROUP, TENSOR),
        P(TENSOR, None),
        P(TENSOR, None),
        P(),
        P(),
        P(TENSOR, GROUP),
        P(),
        P(GROUP),
        P(GROUP, TENSOR),
        P(GROUP, TENSOR),
        P(TENSOR, GROUP),
        P(),
        P(),
        P(),
    )
    return jax.shard_map(shards, mesh=fine, in_specs=in_specs, out_specs=P(None, GROUP), check_vma=False)
```

```python
import functools
import math

import jax
import jax.numpy as jnp
from jax import lax
from jax.experimental import pallas as pl
from jax.experimental.pallas import tpu as pltpu
from jax.sharding import Mesh
from jax.sharding import PartitionSpec as P

GROUP = ("z", "y")
TENSOR = ("x", "c")
HEAD = 128
SLOTS = 2
STEPS = 2
EPS = 1e-05
VMEM_BYTES = 16 * 1024 * 1024
LARGE_VMEM_BYTES = 60 * 1024 * 1024
BF = jnp.bfloat16
F32 = jnp.float32


def params(limit=VMEM_BYTES):
    return pltpu.CompilerParams(vmem_limit_bytes=limit)


def dot(a, b):
    return jnp.dot(a, b, preferred_element_type=F32)


def vmem():
    return pl.BlockSpec(memory_space=pltpu.VMEM)


def smem():
    return pl.BlockSpec(memory_space=pltpu.SMEM)


def route_kernel(me_ref, routes_ref, requests_ref, sel_ref, image_ref):
    me = me_ref[0]
    groups, links = routes_ref.shape
    rows = groups * 2 * SLOTS * STEPS
    row = lax.broadcasted_iota(jnp.int32, (rows, links), 0)
    lane = lax.broadcasted_iota(jnp.int32, (rows, links), 1)
    group_of_row = row >> 3
    slot = (row >> 1) & 1
    step = row & 1
    spread = (group_of_row == lane).astype(F32)
    link = lax.broadcasted_iota(jnp.int32, (groups, links), 1)
    code = (link * 4 + requests_ref[...]).astype(F32)
    route_rows = dot(spread, routes_ref[...].astype(F32))
    code_rows = dot(spread, code)
    hit = route_rows == me.astype(F32)
    first = jnp.min(jnp.where(hit, code_rows, 1e4), axis=1, keepdims=True)
    last = jnp.max(jnp.where(hit, code_rows, -1.0), axis=1, keepdims=True)
    slot1, step1 = slot[:, :1], step[:, :1]
    chosen = jnp.where(slot1 == 0, first, last).astype(jnp.int32)
    found_first = jnp.where(first < 1e3, 1, 0)
    found_last = jnp.where(last > first, 1, 0)
    found = jnp.where(slot1 == 0, found_first, found_last)
    wanted = jnp.where(found == 1, (chosen & 3) * STEPS + step1, -1)
    sel_ref[...] = jnp.where(lane[:, :8] == wanted, 1.0, 0.0).astype(BF)
    mine = routes_ref[pl.ds(me, 1), :]
    here = mine == group_of_row
    first_link = jnp.min(jnp.where(here, lane, 1000), axis=1, keepdims=True)
    last_link = jnp.max(jnp.where(here, lane, -1), axis=1, keepdims=True)
    first_image = jnp.where(first_link < 1000, first_link >> 3, -1)
    last_image = jnp.where(last_link > first_link, last_link >> 3, -1)
    image_ref[...] = jnp.where(slot1 == 0, first_image, last_image)


def kv_kernel(place_ref, x0, x1, k0, v0, k1, v1, low_ref, high_ref, ahead_ref, behind_ref, own_ref):
    total = dot(x0[...], jnp.concatenate((k0[...], v0[...]), axis=1))
    total = total + dot(x1[...], jnp.concatenate((k1[...], v1[...]), axis=1))
    total = total.astype(BF)
    half = low_ref.shape[0]
    step = pl.program_id(0)

    @pl.when(step == 0)
    def _():
        low_ref[...] = total[:half]
        high_ref[...] = total[half:]

    @pl.when(step == 1)
    def _():
        ahead_ref[...] = total

    @pl.when(step == 2)
    def _():
        behind_ref[...] = total

    @pl.when(step == 3)
    def _():
        own_ref[...] = total


def kv_project(place, vision, k_weight, v_weight):
    rows, depth = vision.shape
    chips = 4

    def head(d, place_ref):
        ahead = jnp.where(d == 0, 2, jnp.where(d == 1, 1, jnp.where(d == 2, 3, 0)))
        return 0, lax.rem(place_ref[0] + ahead, chips) * 2 + place_ref[1]

    states = pl.BlockSpec((rows, depth), lambda d, p: (0, 0))
    weights = pl.BlockSpec((depth, HEAD), head)
    sizes = [rows // 2, rows // 2, rows, rows, rows]
    return pl.pallas_call(
        kv_kernel,
        grid_spec=pltpu.PrefetchScalarGridSpec(
            num_scalar_prefetch=1,
            grid=(chips,),
            in_specs=[states] * 2 + [weights] * 4,
            out_specs=[pl.BlockSpec((n, 2 * HEAD), lambda d, p: (0, 0)) for n in sizes],
        ),
        out_shape=[jax.ShapeDtypeStruct((n, 2 * HEAD), BF) for n in sizes],
        compiler_params=params(LARGE_VMEM_BYTES),
    )(
        place,
        vision,
        shift(vision, "c", 1),
        k_weight,
        v_weight,
        shift(k_weight, "c", 1),
        shift(v_weight, "c", 1),
    )


def kv_merge_kernel(ahead_ref, behind_ref, low_ref, high_ref, forward_ref, backward_ref):
    half = low_ref.shape[0]
    forward_ref[:half] = (ahead_ref[:half].astype(F32) + low_ref[...].astype(F32)).astype(BF)
    forward_ref[half:] = ahead_ref[half:]
    backward_ref[:half] = behind_ref[:half]
    backward_ref[half:] = (behind_ref[half:].astype(F32) + high_ref[...].astype(F32)).astype(BF)


def half_of(shape):
    return (lax.broadcasted_iota(jnp.int32, shape, 0) >> 2) & 1


def query_kernel(parts_ref, sel_ref, gain_ref, out_ref):
    total = jnp.sum(parts_ref[...].astype(F32), axis=0)
    gain = gain_ref[...]
    sel = sel_ref[...]
    heads = total.shape[1] // HEAD // 2
    upper = half_of((sel.shape[0], HEAD)) == 1

    def chosen(h):
        v = total[:, h * HEAD : (h + 1) * HEAD]
        scale = lax.rsqrt(jnp.mean(v * v, axis=1, keepdims=True) + EPS)
        return dot(sel, (v * scale * gain).astype(BF))

    for h in range(heads):
        out_ref[:, h * HEAD : (h + 1) * HEAD] = jnp.where(upper, chosen(heads + h), chosen(h)).astype(BF)


def attention_kernel(me_ref, tiles_ref, own_ref, left_ref, right_ref, gain_ref, q_ref, image_ref, out_ref):
    me = me_ref[0]
    total = own_ref[...].astype(F32) + left_ref[...].astype(F32) + right_ref[...].astype(F32)
    k = total[:, :HEAD]
    scale = lax.rsqrt(jnp.mean(k * k, axis=1, keepdims=True) + EPS)
    k = (k * scale * gain_ref[...]).astype(BF)
    v = total[:, HEAD:].astype(BF)
    rows, keys = q_ref.shape[0], k.shape[0]
    tile = lax.broadcasted_iota(jnp.int32, (1, keys), 1) >> 6
    owner = jnp.zeros((1, keys), jnp.int32)
    end = jnp.int32(0)
    for j in range(4):
        end = end + tiles_ref[me, j]
        owner = owner + (tile >= end).astype(jnp.int32)
    allowed = owner == image_ref[...]
    lane = lax.broadcasted_iota(jnp.int32, (rows, HEAD), 1)
    sums = jnp.zeros((rows, HEAD), F32)
    heads = q_ref.shape[1] // HEAD
    for h in range(heads):
        span = slice(h * HEAD, (h + 1) * HEAD)
        score = lax.dot_general(
            q_ref[:, span], k, (((1,), (1,)), ((), ())), preferred_element_type=F32
        )
        weight = jnp.where(allowed, jnp.exp(score * (1.0 / math.sqrt(HEAD))), 0.0)
        den = jnp.sum(weight, axis=1, keepdims=True)
        high = den.astype(BF).astype(F32)
        sums = sums + jnp.where(lane == h, high, 0.0) + jnp.where(lane == heads + h, den - high, 0.0)
        out_ref[:, span] = dot(weight.astype(BF), v).astype(BF)
    out_ref[:, heads * HEAD :] = sums.astype(BF)


def combine_kernel(parts_ref, sel_ref, out_ref):
    sel = sel_ref[...].astype(F32)
    parts = parts_ref[...]
    heads = out_ref.shape[2] // HEAD // 2
    for part in range(2):
        mine = jnp.where(half_of(sel.shape) == part, sel, 0.0).astype(BF)
        total = lax.dot_general(mine, parts, (((0,), (0,)), ((), ())), preferred_element_type=F32)
        sums = total[:, heads * HEAD :]
        for h in range(heads):
            den = sums[:, h : h + 1] + sums[:, heads + h : heads + h + 1]
            mixed = total[:, h * HEAD : (h + 1) * HEAD] / jnp.where(den > 0.0, den, 1.0)
            mixed = jnp.broadcast_to(mixed.astype(BF)[None], (out_ref.shape[0],) + mixed.shape)
            at = (part * heads + h) * HEAD
            out_ref[:, :, at : at + HEAD] = mixed


def core_rows(place_ref, rows):
    return (
        pl.ds(pl.multiple_of(place_ref[1] * rows, rows), rows),
        pl.ds(pl.multiple_of((1 - place_ref[1]) * rows, rows), rows),
    )


def out_kernel(place_ref, a_ref, w_ref, mine_ref, theirs_ref):
    mine, theirs = core_rows(place_ref, mine_ref.shape[0])
    theirs_ref[...] = dot(a_ref[theirs, :], w_ref[...]).astype(BF)
    mine_ref[...] = dot(a_ref[mine, :], w_ref[...])


def gate_up_kernel(place_ref, own_ref, other_ref, w0, w1, w2, w3, out_ref, m_ref):
    units = w0.shape[1]
    step = pl.program_id(0)

    @pl.when(step == 0)
    def _():
        rows = own_ref.shape[0] // 4
        mine, theirs = core_rows(place_ref, rows)
        for d in range(4):
            m_ref[d, mine, :] = own_ref[d * rows : (d + 1) * rows]
            m_ref[d, theirs, :] = other_ref[d * rows : (d + 1) * rows]

    def product():
        total = dot(m_ref[0], w0[...]) + dot(m_ref[1], w1[...])
        return (total + dot(m_ref[2], w2[...]) + dot(m_ref[3], w3[...])).astype(BF)

    @pl.when(step == 0)
    def _():
        out_ref[:, :units] = product()

    @pl.when(step == 1)
    def _():
        out_ref[:, units : 2 * units] = product()
        square = jnp.zeros((m_ref.shape[1], 1), F32)
        for d in range(4):
            value = m_ref[d].astype(F32)
            square = square + jnp.sum(value * value, axis=1, keepdims=True)
        high = square.astype(BF).astype(F32)
        lane = lax.broadcasted_iota(jnp.int32, (m_ref.shape[1], HEAD), 1)
        extra = jnp.where(lane == 0, high, jnp.where(lane == 1, square - high, 0.0))
        out_ref[:, 2 * units :] = extra.astype(BF)


def down_kernel(place_ref, a_ref, d0, d1, d2, d3, mine_ref, theirs_ref):
    active = a_ref[...]
    rows = mine_ref.shape[1]

    def store(d, total, keep_ref):
        keep_ref[d] = total
        theirs_ref[d] = keep_ref[d, core_rows(place_ref, rows)[1], :].astype(BF)
        mine_ref[d] = keep_ref[d, core_rows(place_ref, rows)[0], :]

    def run(keep_ref):
        store(0, dot(active, d0[...]), keep_ref)
        store(1, dot(active, d1[...]), keep_ref)
        store(2, dot(active, d2[...]), keep_ref)
        store(3, dot(active, d3[...]), keep_ref)

    pl.run_scoped(run, pltpu.VMEM((4,) + active.shape[:1] + (d0.shape[1],), F32))


def pair_kernel(mine_ref, theirs_ref, own_ref, behind_ref, across_ref, ahead_ref):
    own_ref[...] = mine_ref[0] + theirs_ref[0].astype(F32)
    behind_ref[...] = (mine_ref[1] + theirs_ref[1].astype(F32)).astype(BF)
    across_ref[...] = (mine_ref[2] + theirs_ref[2].astype(F32)).astype(BF)
    ahead_ref[...] = (mine_ref[3] + theirs_ref[3].astype(F32)).astype(BF)


def active_kernel(full_width, parts_ref, out_ref):
    total = jnp.sum(parts_ref[...].astype(F32), axis=0)
    units = out_ref.shape[2]
    square = total[:, 2 * units : 2 * units + 1] + total[:, 2 * units + 1 : 2 * units + 2]
    scale = lax.rsqrt(square * (1.0 / full_width) + EPS)
    gate = total[:, :units] * scale
    up = total[:, units : 2 * units] * scale
    active = (gate / (1.0 + jnp.exp(-gate)) * up).astype(BF)
    out_ref[...] = jnp.broadcast_to(active[None], out_ref.shape)


def shift(value, axis, by):
    n = lax.axis_size(axis)
    return lax.ppermute(value, axis, [(i, (i + by) % n) for i in range(n)])


def after(value, *others):
    return lax.optimization_barrier((value,) + others)[0]


def exchange(value, axis):
    n = lax.axis_size(axis)
    out = lax.all_to_all(value, axis, 0, 0, tiled=True)
    return out.reshape((n, value.shape[0] // n) + value.shape[1:])


def chip_sum(part):
    part = part.astype(BF)
    ahead, behind, across = shift(part, "x", 1), shift(part, "x", -1), shift(part, "x", 2)
    return (part.astype(F32) + across.astype(F32)) + (ahead.astype(F32) + behind.astype(F32))


def shards(
    hidden,
    vision,
    attn_gain,
    q_weight,
    k_weight,
    v_weight,
    q_gain,
    k_gain,
    o_weight,
    gate_logits,
    mlp_gain,
    gate_weight,
    up_weight,
    down_weight,
    image_tiles,
    image_groups,
    image_requests,
):
    groups = lax.axis_size("z") * lax.axis_size("y")
    me = (lax.axis_index("z") * lax.axis_size("y") + lax.axis_index("y")).astype(jnp.int32).reshape(1)
    place = jnp.stack((lax.axis_index("x"), lax.axis_index("c"))).astype(jnp.int32)
    all_rows, width_part = hidden.shape
    own_rows = all_rows // groups
    full_width = width_part * groups
    local_heads = q_weight.shape[1]
    hidden_part = gate_weight.shape[1]
    slot_rows = groups * 2 * SLOTS * STEPS
    key_rows = vision.shape[0]

    sel, row_image = pl.pallas_call(
        route_kernel,
        in_specs=[smem(), vmem(), vmem()],
        out_specs=[vmem(), vmem()],
        out_shape=[
            jax.ShapeDtypeStruct((slot_rows, own_rows), BF),
            jax.ShapeDtypeStruct((slot_rows, 1), jnp.int32),
        ],
        compiler_params=params(),
    )(me, image_groups.reshape(groups, -1), image_requests.reshape(groups, -1))

    hidden = after(hidden, place)
    hidden_f = hidden.astype(F32)
    normed = (hidden_f * attn_gain).astype(BF)
    q_part = dot(normed, q_weight).astype(BF)
    q_parts = exchange(q_part, GROUP)

    low, high, ahead, behind, own = kv_project(place, vision, k_weight, v_weight)
    q_parts = after(q_parts, own)
    forward, backward = pl.pallas_call(
        kv_merge_kernel,
        in_specs=[vmem()] * 4,
        out_specs=[vmem()] * 2,
        out_shape=[jax.ShapeDtypeStruct(ahead.shape, BF)] * 2,
        compiler_params=params(LARGE_VMEM_BYTES),
    )(ahead, behind, shift(low, "x", 1), shift(high, "x", -1))
    kv_left = shift(forward, "x", 1)
    kv_right = shift(backward, "x", -1)

    chips_y = lax.axis_size("y")
    units = hidden_part // chips_y
    gain = mlp_gain[:, None]

    def columns(weight, d):
        at = lax.rem(lax.axis_index("y") + d, chips_y) * units
        return lax.dynamic_slice_in_dim(weight, at, units, 1).astype(F32)

    def wide(*parts):
        return (jnp.concatenate(parts, axis=1) * gain).astype(BF)

    queries = pl.pallas_call(
        query_kernel,
        in_specs=[vmem()] * 3,
        out_specs=vmem(),
        out_shape=jax.ShapeDtypeStruct((slot_rows, local_heads // 2), BF),
        compiler_params=params(),
    )(q_parts, sel, q_gain.reshape(1, HEAD))
    queries = after(queries, forward, backward)
    later_gate, later_up = lax.optimization_barrier((gate_weight, up_weight, queries))[:2]
    wide_0 = wide(columns(later_gate, 0), columns(later_up, 0))
    wide_1 = shift(wide(columns(later_gate, 1), columns(later_up, 1)), "y", 1)
    wide_3 = shift(wide(columns(later_gate, 3), columns(later_up, 3)), "y", -1)
    queries = lax.all_to_all(queries, GROUP, 0, 0, tiled=True)

    mixed = pl.pallas_call(
        attention_kernel,
        in_specs=[smem(), smem()] + [vmem()] * 6,
        out_specs=vmem(),
        out_shape=jax.ShapeDtypeStruct((slot_rows, local_heads // 2 + HEAD), BF),
        compiler_params=params(),
    )(me, image_tiles, own, kv_left, kv_right, k_gain.reshape(1, HEAD), queries, row_image)
    gate_weight, up_weight, down_weight = lax.optimization_barrier((gate_weight, up_weight, down_weight, mixed))[:3]
    wide_2 = wide(columns(gate_weight, 2), columns(up_weight, 2))

    def rows(d):
        at = lax.rem(lax.axis_index("y") + d, chips_y) * units
        return lax.dynamic_slice_in_dim(down_weight, at, units, 0)

    down_0, down_1, down_2, down_3 = rows(0), rows(1), rows(2), rows(3)
    mixed = lax.all_to_all(mixed, GROUP, 0, 0, tiled=True)
    mixed = after(mixed, wide_2, down_1, down_2, down_3)
    wide_2 = shift(wide_2, "y", 2)

    attended = pl.pallas_call(
        combine_kernel,
        in_specs=[vmem()] * 2,
        out_specs=vmem(),
        out_shape=jax.ShapeDtypeStruct((groups, own_rows, local_heads), BF),
        compiler_params=params(),
    )(mixed, sel)
    attended = after(attended, wide_1, wide_3)
    attended = lax.all_to_all(attended, GROUP, 0, 0, tiled=True).reshape(all_rows, local_heads)
    half_rows = all_rows // 2
    first_row = lax.axis_index("c") * half_rows
    half_f = lax.dynamic_slice_in_dim(hidden, first_row, half_rows, 0).astype(F32)
    mine, theirs = pl.pallas_call(
        out_kernel,
        in_specs=[smem(), vmem(), vmem()],
        out_specs=[vmem()] * 2,
        out_shape=[
            jax.ShapeDtypeStruct((half_rows, width_part), F32),
            jax.ShapeDtypeStruct((half_rows, width_part), BF),
        ],
        compiler_params=params(),
    )(place, attended, o_weight)
    pair = (mine + shift(theirs, "c", 1).astype(F32)).astype(BF)
    attn_sum = chip_sum(pair)
    middle = (half_f + jnp.tanh(gate_logits[0]) * attn_sum).astype(BF)
    middle = after(middle, wide_2)
    middle_f = middle.astype(F32)
    own_rows_all = jnp.concatenate([middle] + [shift(middle, "y", d) for d in (1, 2, 3)], axis=0)
    other_rows_all = shift(own_rows_all, "c", 1)
    block = pl.BlockSpec((4 * half_rows, width_part), lambda i: (0, 0))
    direct = pl.BlockSpec((width_part, units), lambda i: (0, i))
    gate_up = pl.pallas_call(
        gate_up_kernel,
        grid=(2,),
        in_specs=[smem()] + [block] * 2 + [direct] * 4,
        out_specs=pl.BlockSpec((all_rows, 2 * units + HEAD), lambda i: (0, 0)),
        out_shape=jax.ShapeDtypeStruct((all_rows, 2 * units + HEAD), BF),
        scratch_shapes=[pltpu.VMEM((4, all_rows, width_part), BF)],
        compiler_params=params(LARGE_VMEM_BYTES),
    )(place, own_rows_all, other_rows_all, wide_0, wide_1, wide_2, wide_3)
    down_1, down_2, down_3 = lax.optimization_barrier((down_1, down_2, down_3, gate_up))[:3]
    down_1, down_2, down_3 = shift(down_1, "y", 1), shift(down_2, "y", 2), shift(down_3, "y", -1)
    parts = after(exchange(gate_up, "z"), down_1, down_2, down_3)
    active = pl.pallas_call(
        functools.partial(active_kernel, full_width),
        in_specs=[vmem()],
        out_specs=vmem(),
        out_shape=jax.ShapeDtypeStruct(parts.shape[:2] + (units,), BF),
        compiler_params=params(),
    )(parts)
    active = lax.all_to_all(active, "z", 0, 0, tiled=True).reshape(all_rows, units)
    mine, theirs = pl.pallas_call(
        down_kernel,
        in_specs=[smem()] + [vmem()] * 5,
        out_specs=[vmem()] * 2,
        out_shape=[
            jax.ShapeDtypeStruct((4, half_rows, width_part), F32),
            jax.ShapeDtypeStruct((4, half_rows, width_part), BF),
        ],
        compiler_params=params(),
    )(place, active, down_0, down_1, down_2, down_3)
    own_down, behind, across, ahead = pl.pallas_call(
        pair_kernel,
        in_specs=[vmem()] * 2,
        out_specs=[vmem()] * 4,
        out_shape=[jax.ShapeDtypeStruct((half_rows, width_part), F32)]
        + [jax.ShapeDtypeStruct((half_rows, width_part), BF)] * 3,
        compiler_params=params(),
    )(mine, shift(theirs, "c", 1))
    across, behind, ahead = shift(across, "y", 2), shift(behind, "y", -1), shift(ahead, "y", 1)
    down_sum = chip_sum(own_down + across.astype(F32) + behind.astype(F32) + ahead.astype(F32))
    row_request = (jnp.arange(half_rows, dtype=jnp.int32) + first_row) // STEPS
    request_ids = (image_groups * (own_rows // STEPS) + image_requests).reshape(-1)
    has_image = jnp.any(row_request[:, None] == request_ids[None, :], axis=1).astype(F32)
    output = (middle_f + jnp.tanh(gate_logits[1]) * has_image[:, None] * down_sum).astype(BF)
    swapped = shift(output, "c", 1)
    lower = lax.axis_index("c") == 0
    return jnp.concatenate((jnp.where(lower, output, swapped), jnp.where(lower, swapped, output)), axis=0)


def solution(mesh):
    fine = Mesh(mesh.devices.reshape(8, 4, 4, 2), GROUP + TENSOR)
    in_specs = (
        P(None, GROUP),
        P(GROUP, TENSOR),
        P(GROUP),
        P(GROUP, TENSOR),
        P(TENSOR, None),
        P(TENSOR, None),
        P(),
        P(),
        P(TENSOR, GROUP),
        P(),
        P(GROUP),
        P(GROUP, TENSOR),
        P(GROUP, TENSOR),
        P(TENSOR, GROUP),
        P(),
        P(),
        P(),
    )
    return jax.shard_map(shards, mesh=fine, in_specs=in_specs, out_specs=P(None, GROUP), check_vma=False)
```

```python
import functools
import math

import jax
import jax.numpy as jnp
from jax import lax
from jax.experimental import pallas as pl
from jax.experimental.pallas import tpu as pltpu
from jax.sharding import Mesh
from jax.sharding import PartitionSpec as P

GROUP = ("z", "y")
TENSOR = ("x", "c")
HEAD = 128
SLOTS = 2
STEPS = 2
EPS = 1e-05
VMEM_BYTES = 16 * 1024 * 1024
LARGE_VMEM_BYTES = 60 * 1024 * 1024
BF = jnp.bfloat16
F32 = jnp.float32


def params(limit=VMEM_BYTES):
    return pltpu.CompilerParams(vmem_limit_bytes=limit)


def dot(a, b):
    return jnp.dot(a, b, preferred_element_type=F32)


def vmem():
    return pl.BlockSpec(memory_space=pltpu.VMEM)


def smem():
    return pl.BlockSpec(memory_space=pltpu.SMEM)


def route_kernel(me_ref, routes_ref, requests_ref, sel_ref, image_ref):
    me = me_ref[0]
    groups, links = routes_ref.shape
    rows = groups * 2 * SLOTS * STEPS
    row = lax.broadcasted_iota(jnp.int32, (rows, links), 0)
    lane = lax.broadcasted_iota(jnp.int32, (rows, links), 1)
    group_of_row = row >> 3
    slot = (row >> 1) & 1
    step = row & 1
    spread = (group_of_row == lane).astype(F32)
    link = lax.broadcasted_iota(jnp.int32, (groups, links), 1)
    code = (link * 4 + requests_ref[...]).astype(F32)
    route_rows = dot(spread, routes_ref[...].astype(F32))
    code_rows = dot(spread, code)
    hit = route_rows == me.astype(F32)
    first = jnp.min(jnp.where(hit, code_rows, 1e4), axis=1, keepdims=True)
    last = jnp.max(jnp.where(hit, code_rows, -1.0), axis=1, keepdims=True)
    slot1, step1 = slot[:, :1], step[:, :1]
    chosen = jnp.where(slot1 == 0, first, last).astype(jnp.int32)
    found_first = jnp.where(first < 1e3, 1, 0)
    found_last = jnp.where(last > first, 1, 0)
    found = jnp.where(slot1 == 0, found_first, found_last)
    wanted = jnp.where(found == 1, (chosen & 3) * STEPS + step1, -1)
    sel_ref[...] = jnp.where(lane[:, :8] == wanted, 1.0, 0.0).astype(BF)
    mine = routes_ref[pl.ds(me, 1), :]
    here = mine == group_of_row
    first_link = jnp.min(jnp.where(here, lane, 1000), axis=1, keepdims=True)
    last_link = jnp.max(jnp.where(here, lane, -1), axis=1, keepdims=True)
    first_image = jnp.where(first_link < 1000, first_link >> 3, -1)
    last_image = jnp.where(last_link > first_link, last_link >> 3, -1)
    image_ref[...] = jnp.where(slot1 == 0, first_image, last_image)


def kv_kernel(place_ref, x0, x1, k0, v0, k1, v1, low_ref, high_ref, ahead_ref, behind_ref, own_ref):
    total = dot(x0[...], jnp.concatenate((k0[...], v0[...]), axis=1))
    total = total + dot(x1[...], jnp.concatenate((k1[...], v1[...]), axis=1))
    total = total.astype(BF)
    half = low_ref.shape[0]
    step = pl.program_id(0)

    @pl.when(step == 0)
    def _():
        low_ref[...] = total[:half]
        high_ref[...] = total[half:]

    @pl.when(step == 1)
    def _():
        ahead_ref[...] = total

    @pl.when(step == 2)
    def _():
        behind_ref[...] = total

    @pl.when(step == 3)
    def _():
        own_ref[...] = total


def kv_project(place, vision, k_weight, v_weight):
    rows, depth = vision.shape
    chips = 4

    def head(d, place_ref):
        ahead = jnp.where(d == 0, 2, jnp.where(d == 1, 1, jnp.where(d == 2, 3, 0)))
        return 0, lax.rem(place_ref[0] + ahead, chips) * 2 + place_ref[1]

    states = pl.BlockSpec((rows, depth), lambda d, p: (0, 0))
    weights = pl.BlockSpec((depth, HEAD), head)
    sizes = [rows // 2, rows // 2, rows, rows, rows]
    return pl.pallas_call(
        kv_kernel,
        grid_spec=pltpu.PrefetchScalarGridSpec(
            num_scalar_prefetch=1,
            grid=(chips,),
            in_specs=[states] * 2 + [weights] * 4,
            out_specs=[pl.BlockSpec((n, 2 * HEAD), lambda d, p: (0, 0)) for n in sizes],
        ),
        out_shape=[jax.ShapeDtypeStruct((n, 2 * HEAD), BF) for n in sizes],
        compiler_params=params(LARGE_VMEM_BYTES),
    )(
        place,
        vision,
        shift(vision, "c", 1),
        k_weight,
        v_weight,
        shift(k_weight, "c", 1),
        shift(v_weight, "c", 1),
    )


def kv_merge_kernel(ahead_ref, behind_ref, low_ref, high_ref, forward_ref, backward_ref):
    half = low_ref.shape[0]
    forward_ref[:half] = (ahead_ref[:half].astype(F32) + low_ref[...].astype(F32)).astype(BF)
    forward_ref[half:] = ahead_ref[half:]
    backward_ref[:half] = behind_ref[:half]
    backward_ref[half:] = (behind_ref[half:].astype(F32) + high_ref[...].astype(F32)).astype(BF)


def half_of(shape):
    return (lax.broadcasted_iota(jnp.int32, shape, 0) >> 2) & 1


def query_kernel(parts_ref, sel_ref, gain_ref, out_ref):
    total = jnp.sum(parts_ref[...].astype(F32), axis=0)
    gain = gain_ref[...]
    sel = sel_ref[...]
    heads = total.shape[1] // HEAD // 2
    upper = half_of((sel.shape[0], HEAD)) == 1

    def chosen(h):
        v = total[:, h * HEAD : (h + 1) * HEAD]
        scale = lax.rsqrt(jnp.mean(v * v, axis=1, keepdims=True) + EPS)
        return dot(sel, (v * scale * gain).astype(BF))

    for h in range(heads):
        out_ref[:, h * HEAD : (h + 1) * HEAD] = jnp.where(upper, chosen(heads + h), chosen(h)).astype(BF)


def attention_kernel(me_ref, tiles_ref, own_ref, left_ref, right_ref, gain_ref, q_ref, image_ref, out_ref):
    me = me_ref[0]
    total = own_ref[...].astype(F32) + left_ref[...].astype(F32) + right_ref[...].astype(F32)
    k = total[:, :HEAD]
    scale = lax.rsqrt(jnp.mean(k * k, axis=1, keepdims=True) + EPS)
    k = (k * scale * gain_ref[...]).astype(BF)
    v = total[:, HEAD:].astype(BF)
    rows, keys = q_ref.shape[0], k.shape[0]
    tile = lax.broadcasted_iota(jnp.int32, (1, keys), 1) >> 6
    owner = jnp.zeros((1, keys), jnp.int32)
    end = jnp.int32(0)
    for j in range(4):
        end = end + tiles_ref[me, j]
        owner = owner + (tile >= end).astype(jnp.int32)
    allowed = owner == image_ref[...]
    lane = lax.broadcasted_iota(jnp.int32, (rows, HEAD), 1)
    sums = jnp.zeros((rows, HEAD), F32)
    heads = q_ref.shape[1] // HEAD
    for h in range(heads):
        span = slice(h * HEAD, (h + 1) * HEAD)
        score = lax.dot_general(
            q_ref[:, span], k, (((1,), (1,)), ((), ())), preferred_element_type=F32
        )
        weight = jnp.where(allowed, jnp.exp(score * (1.0 / math.sqrt(HEAD))), 0.0)
        den = jnp.sum(weight, axis=1, keepdims=True)
        high = den.astype(BF).astype(F32)
        sums = sums + jnp.where(lane == h, high, 0.0) + jnp.where(lane == heads + h, den - high, 0.0)
        out_ref[:, span] = dot(weight.astype(BF), v).astype(BF)
    out_ref[:, heads * HEAD :] = sums.astype(BF)


def combine_kernel(parts_ref, sel_ref, out_ref):
    sel = sel_ref[...].astype(F32)
    parts = parts_ref[...]
    heads = out_ref.shape[2] // HEAD // 2
    for part in range(2):
        mine = jnp.where(half_of(sel.shape) == part, sel, 0.0).astype(BF)
        total = lax.dot_general(mine, parts, (((0,), (0,)), ((), ())), preferred_element_type=F32)
        sums = total[:, heads * HEAD :]
        for h in range(heads):
            den = sums[:, h : h + 1] + sums[:, heads + h : heads + h + 1]
            mixed = total[:, h * HEAD : (h + 1) * HEAD] / jnp.where(den > 0.0, den, 1.0)
            mixed = jnp.broadcast_to(mixed.astype(BF)[None], (out_ref.shape[0],) + mixed.shape)
            at = (part * heads + h) * HEAD
            out_ref[:, :, at : at + HEAD] = mixed


def core_rows(place_ref, rows):
    return (
        pl.ds(pl.multiple_of(place_ref[1] * rows, rows), rows),
        pl.ds(pl.multiple_of((1 - place_ref[1]) * rows, rows), rows),
    )


def out_kernel(place_ref, a_ref, w_ref, mine_ref, theirs_ref):
    mine, theirs = core_rows(place_ref, mine_ref.shape[0])
    theirs_ref[...] = dot(a_ref[theirs, :], w_ref[...]).astype(BF)
    mine_ref[...] = dot(a_ref[mine, :], w_ref[...])


def gate_up_kernel(place_ref, own_ref, other_ref, w0, w1, w2, w3, out_ref, m_ref):
    units = w0.shape[1]
    step = pl.program_id(0)

    @pl.when(step == 0)
    def _():
        rows = own_ref.shape[0] // 4
        mine, theirs = core_rows(place_ref, rows)
        for d in range(4):
            m_ref[d, mine, :] = own_ref[d * rows : (d + 1) * rows]
            m_ref[d, theirs, :] = other_ref[d * rows : (d + 1) * rows]

    def product():
        total = dot(m_ref[0], w0[...]) + dot(m_ref[1], w1[...])
        return (total + dot(m_ref[2], w2[...]) + dot(m_ref[3], w3[...])).astype(BF)

    @pl.when(step == 0)
    def _():
        out_ref[:, :units] = product()

    @pl.when(step == 1)
    def _():
        out_ref[:, units : 2 * units] = product()
        square = jnp.zeros((m_ref.shape[1], 1), F32)
        for d in range(4):
            value = m_ref[d].astype(F32)
            square = square + jnp.sum(value * value, axis=1, keepdims=True)
        high = square.astype(BF).astype(F32)
        lane = lax.broadcasted_iota(jnp.int32, (m_ref.shape[1], HEAD), 1)
        extra = jnp.where(lane == 0, high, jnp.where(lane == 1, square - high, 0.0))
        out_ref[:, 2 * units :] = extra.astype(BF)


def down_kernel(place_ref, a_ref, d0, d1, low2, high2, d3, mine_ref, theirs_ref):
    active = a_ref[...]
    half = low2.shape[0]
    rows = mine_ref.shape[1]

    def store(d, total, keep_ref):
        keep_ref[d] = total
        theirs_ref[d] = keep_ref[d, core_rows(place_ref, rows)[1], :].astype(BF)
        mine_ref[d] = keep_ref[d, core_rows(place_ref, rows)[0], :]

    def run(keep_ref):
        store(0, dot(active, d0[...]), keep_ref)
        store(1, dot(active, d1[...]), keep_ref)
        store(2, dot(active[:, :half], low2[...]) + dot(active[:, half:], high2[...]), keep_ref)
        store(3, dot(active, d3[...]), keep_ref)

    pl.run_scoped(run, pltpu.VMEM((4,) + active.shape[:1] + (d0.shape[1],), F32))


def pair_kernel(mine_ref, theirs_ref, own_ref, behind_ref, across_ref, ahead_ref):
    own_ref[...] = mine_ref[0] + theirs_ref[0].astype(F32)
    behind_ref[...] = (mine_ref[1] + theirs_ref[1].astype(F32)).astype(BF)
    across_ref[...] = (mine_ref[2] + theirs_ref[2].astype(F32)).astype(BF)
    ahead_ref[...] = (mine_ref[3] + theirs_ref[3].astype(F32)).astype(BF)


def active_kernel(full_width, parts_ref, out_ref):
    total = jnp.sum(parts_ref[...].astype(F32), axis=0)
    units = out_ref.shape[2]
    square = total[:, 2 * units : 2 * units + 1] + total[:, 2 * units + 1 : 2 * units + 2]
    scale = lax.rsqrt(square * (1.0 / full_width) + EPS)
    gate = total[:, :units] * scale
    up = total[:, units : 2 * units] * scale
    active = (gate / (1.0 + jnp.exp(-gate)) * up).astype(BF)
    out_ref[...] = jnp.broadcast_to(active[None], out_ref.shape)


def shift(value, axis, by):
    n = lax.axis_size(axis)
    return lax.ppermute(value, axis, [(i, (i + by) % n) for i in range(n)])


def after(value, *others):
    return lax.optimization_barrier((value,) + others)[0]


def exchange(value, axis):
    n = lax.axis_size(axis)
    out = lax.all_to_all(value, axis, 0, 0, tiled=True)
    return out.reshape((n, value.shape[0] // n) + value.shape[1:])


def chip_sum(part):
    part = part.astype(BF)
    ahead, behind, across = shift(part, "x", 1), shift(part, "x", -1), shift(part, "x", 2)
    return (part.astype(F32) + across.astype(F32)) + (ahead.astype(F32) + behind.astype(F32))


def shards(
    hidden,
    vision,
    attn_gain,
    q_weight,
    k_weight,
    v_weight,
    q_gain,
    k_gain,
    o_weight,
    gate_logits,
    mlp_gain,
    gate_weight,
    up_weight,
    down_weight,
    image_tiles,
    image_groups,
    image_requests,
):
    groups = lax.axis_size("z") * lax.axis_size("y")
    me = (lax.axis_index("z") * lax.axis_size("y") + lax.axis_index("y")).astype(jnp.int32).reshape(1)
    place = jnp.stack((lax.axis_index("x"), lax.axis_index("c"))).astype(jnp.int32)
    all_rows, width_part = hidden.shape
    own_rows = all_rows // groups
    full_width = width_part * groups
    local_heads = q_weight.shape[1]
    hidden_part = gate_weight.shape[1]
    slot_rows = groups * 2 * SLOTS * STEPS
    key_rows = vision.shape[0]

    sel, row_image = pl.pallas_call(
        route_kernel,
        in_specs=[smem(), vmem(), vmem()],
        out_specs=[vmem(), vmem()],
        out_shape=[
            jax.ShapeDtypeStruct((slot_rows, own_rows), BF),
            jax.ShapeDtypeStruct((slot_rows, 1), jnp.int32),
        ],
        compiler_params=params(),
    )(me, image_groups.reshape(groups, -1), image_requests.reshape(groups, -1))

    hidden = after(hidden, place)
    hidden_f = hidden.astype(F32)
    normed = (hidden_f * attn_gain).astype(BF)
    q_part = dot(normed, q_weight).astype(BF)
    q_parts = exchange(q_part, GROUP)

    low, high, ahead, behind, own = kv_project(place, vision, k_weight, v_weight)
    q_parts = after(q_parts, own)
    forward, backward = pl.pallas_call(
        kv_merge_kernel,
        in_specs=[vmem()] * 4,
        out_specs=[vmem()] * 2,
        out_shape=[jax.ShapeDtypeStruct(ahead.shape, BF)] * 2,
        compiler_params=params(LARGE_VMEM_BYTES),
    )(ahead, behind, shift(low, "x", 1), shift(high, "x", -1))
    kv_left = shift(forward, "x", 1)
    kv_right = shift(backward, "x", -1)

    chips_y = lax.axis_size("y")
    units = hidden_part // chips_y
    half = units // 2
    gain = mlp_gain[:, None]

    def columns(weight, d):
        at = lax.rem(lax.axis_index("y") + d, chips_y) * units
        return lax.dynamic_slice_in_dim(weight, at, units, 1).astype(F32)

    def wide(*parts):
        return (jnp.concatenate(parts, axis=1) * gain).astype(BF)

    queries = pl.pallas_call(
        query_kernel,
        in_specs=[vmem()] * 3,
        out_specs=vmem(),
        out_shape=jax.ShapeDtypeStruct((slot_rows, local_heads // 2), BF),
        compiler_params=params(),
    )(q_parts, sel, q_gain.reshape(1, HEAD))
    queries = after(queries, forward, backward)
    later_gate, later_up = lax.optimization_barrier((gate_weight, up_weight, queries))[:2]
    wide_0 = wide(columns(later_gate, 0), columns(later_up, 0))
    wide_1 = shift(wide(columns(later_gate, 1), columns(later_up, 1)), "y", 1)
    wide_2 = wide(columns(later_gate, 2), columns(later_up, 2))
    wide_3 = shift(wide(columns(later_gate, 3), columns(later_up, 3)), "y", -1)
    queries = lax.all_to_all(queries, GROUP, 0, 0, tiled=True)

    mixed = pl.pallas_call(
        attention_kernel,
        in_specs=[smem(), smem()] + [vmem()] * 6,
        out_specs=vmem(),
        out_shape=jax.ShapeDtypeStruct((slot_rows, local_heads // 2 + HEAD), BF),
        compiler_params=params(),
    )(me, image_tiles, own, kv_left, kv_right, k_gain.reshape(1, HEAD), queries, row_image)
    down_weight = after(down_weight, mixed)

    def rows(d, start, size):
        at = lax.rem(lax.axis_index("y") + d, chips_y) * units + start
        return lax.dynamic_slice_in_dim(down_weight, at, size, 0)

    down_0, down_1, down_3 = rows(0, 0, units), rows(1, 0, units), rows(3, 0, units)
    down_2 = rows(2, 0, half), rows(2, half, half)
    mixed = lax.all_to_all(mixed, GROUP, 0, 0, tiled=True)
    mixed = after(mixed, down_1, down_3, *down_2)
    wide_2 = shift(wide_2, "y", 2)

    attended = pl.pallas_call(
        combine_kernel,
        in_specs=[vmem()] * 2,
        out_specs=vmem(),
        out_shape=jax.ShapeDtypeStruct((groups, own_rows, local_heads), BF),
        compiler_params=params(),
    )(mixed, sel)
    attended = after(attended, wide_1, wide_3)
    attended = lax.all_to_all(attended, GROUP, 0, 0, tiled=True).reshape(all_rows, local_heads)
    half_rows = all_rows // 2
    first_row = lax.axis_index("c") * half_rows
    half_f = lax.dynamic_slice_in_dim(hidden, first_row, half_rows, 0).astype(F32)
    mine, theirs = pl.pallas_call(
        out_kernel,
        in_specs=[smem(), vmem(), vmem()],
        out_specs=[vmem()] * 2,
        out_shape=[
            jax.ShapeDtypeStruct((half_rows, width_part), F32),
            jax.ShapeDtypeStruct((half_rows, width_part), BF),
        ],
        compiler_params=params(),
    )(place, attended, o_weight)
    pair = (mine + shift(theirs, "c", 1).astype(F32)).astype(BF)
    attn_sum = chip_sum(pair)
    middle = (half_f + jnp.tanh(gate_logits[0]) * attn_sum).astype(BF)
    middle = after(middle, wide_2)
    middle_f = middle.astype(F32)
    own_rows_all = jnp.concatenate([middle] + [shift(middle, "y", d) for d in (1, 2, 3)], axis=0)
    other_rows_all = shift(own_rows_all, "c", 1)
    block = pl.BlockSpec((4 * half_rows, width_part), lambda i: (0, 0))
    direct = pl.BlockSpec((width_part, units), lambda i: (0, i))
    gate_up = pl.pallas_call(
        gate_up_kernel,
        grid=(2,),
        in_specs=[smem()] + [block] * 2 + [direct] * 4,
        out_specs=pl.BlockSpec((all_rows, 2 * units + HEAD), lambda i: (0, 0)),
        out_shape=jax.ShapeDtypeStruct((all_rows, 2 * units + HEAD), BF),
        scratch_shapes=[pltpu.VMEM((4, all_rows, width_part), BF)],
        compiler_params=params(LARGE_VMEM_BYTES),
    )(place, own_rows_all, other_rows_all, wide_0, wide_1, wide_2, wide_3)
    down_1, down_3, *down_2 = lax.optimization_barrier((down_1, down_3, *down_2, gate_up))[:4]
    down_1, down_3 = shift(down_1, "y", 1), shift(down_3, "y", -1)
    down_2 = shift(down_2[0], "y", 1), shift(down_2[1], "y", -1)
    parts = after(exchange(gate_up, "z"), down_1, down_3, *down_2)
    down_2 = shift(down_2[0], "y", 1), shift(down_2[1], "y", -1)
    active = pl.pallas_call(
        functools.partial(active_kernel, full_width),
        in_specs=[vmem()],
        out_specs=vmem(),
        out_shape=jax.ShapeDtypeStruct(parts.shape[:2] + (units,), BF),
        compiler_params=params(),
    )(parts)
    active = lax.all_to_all(active, "z", 0, 0, tiled=True).reshape(all_rows, units)
    mine, theirs = pl.pallas_call(
        down_kernel,
        in_specs=[smem()] + [vmem()] * 6,
        out_specs=[vmem()] * 2,
        out_shape=[
            jax.ShapeDtypeStruct((4, half_rows, width_part), F32),
            jax.ShapeDtypeStruct((4, half_rows, width_part), BF),
        ],
        compiler_params=params(),
    )(place, active, down_0, down_1, *down_2, down_3)
    own_down, behind, across, ahead = pl.pallas_call(
        pair_kernel,
        in_specs=[vmem()] * 2,
        out_specs=[vmem()] * 4,
        out_shape=[jax.ShapeDtypeStruct((half_rows, width_part), F32)]
        + [jax.ShapeDtypeStruct((half_rows, width_part), BF)] * 3,
        compiler_params=params(),
    )(mine, shift(theirs, "c", 1))
    across, behind, ahead = shift(across, "y", 2), shift(behind, "y", -1), shift(ahead, "y", 1)
    down_sum = chip_sum(own_down + across.astype(F32) + behind.astype(F32) + ahead.astype(F32))
    row_request = (jnp.arange(half_rows, dtype=jnp.int32) + first_row) // STEPS
    request_ids = (image_groups * (own_rows // STEPS) + image_requests).reshape(-1)
    has_image = jnp.any(row_request[:, None] == request_ids[None, :], axis=1).astype(F32)
    output = (middle_f + jnp.tanh(gate_logits[1]) * has_image[:, None] * down_sum).astype(BF)
    swapped = shift(output, "c", 1)
    lower = lax.axis_index("c") == 0
    return jnp.concatenate((jnp.where(lower, output, swapped), jnp.where(lower, swapped, output)), axis=0)


def solution(mesh):
    fine = Mesh(mesh.devices.reshape(8, 4, 4, 2), GROUP + TENSOR)
    in_specs = (
        P(None, GROUP),
        P(GROUP, TENSOR),
        P(GROUP),
        P(GROUP, TENSOR),
        P(TENSOR, None),
        P(TENSOR, None),
        P(),
        P(),
        P(TENSOR, GROUP),
        P(),
        P(GROUP),
        P(GROUP, TENSOR),
        P(GROUP, TENSOR),
        P(TENSOR, GROUP),
        P(),
        P(),
        P(),
    )
    return jax.shard_map(shards, mesh=fine, in_specs=in_specs, out_specs=P(None, GROUP), check_vma=False)
```

```python
import functools
import math

import jax
import jax.numpy as jnp
from jax import lax
from jax.experimental import pallas as pl
from jax.experimental.pallas import tpu as pltpu
from jax.sharding import Mesh
from jax.sharding import PartitionSpec as P

GROUP = ("z", "y")
TENSOR = ("x", "c")
HEAD = 128
SLOTS = 2
STEPS = 2
EPS = 1e-05
VMEM_BYTES = 16 * 1024 * 1024
LARGE_VMEM_BYTES = 60 * 1024 * 1024
BF = jnp.bfloat16
F32 = jnp.float32


def params(limit=VMEM_BYTES):
    return pltpu.CompilerParams(vmem_limit_bytes=limit)


def dot(a, b):
    return jnp.dot(a, b, preferred_element_type=F32)


def vmem():
    return pl.BlockSpec(memory_space=pltpu.VMEM)


def smem():
    return pl.BlockSpec(memory_space=pltpu.SMEM)


def route_kernel(me_ref, routes_ref, requests_ref, sel_ref, image_ref):
    me = me_ref[0]
    groups, links = routes_ref.shape
    rows = groups * 2 * SLOTS * STEPS
    row = lax.broadcasted_iota(jnp.int32, (rows, links), 0)
    lane = lax.broadcasted_iota(jnp.int32, (rows, links), 1)
    group_of_row = row >> 3
    slot = (row >> 1) & 1
    step = row & 1
    spread = (group_of_row == lane).astype(F32)
    link = lax.broadcasted_iota(jnp.int32, (groups, links), 1)
    code = (link * 4 + requests_ref[...]).astype(F32)
    route_rows = dot(spread, routes_ref[...].astype(F32))
    code_rows = dot(spread, code)
    hit = route_rows == me.astype(F32)
    first = jnp.min(jnp.where(hit, code_rows, 1e4), axis=1, keepdims=True)
    last = jnp.max(jnp.where(hit, code_rows, -1.0), axis=1, keepdims=True)
    slot1, step1 = slot[:, :1], step[:, :1]
    chosen = jnp.where(slot1 == 0, first, last).astype(jnp.int32)
    found_first = jnp.where(first < 1e3, 1, 0)
    found_last = jnp.where(last > first, 1, 0)
    found = jnp.where(slot1 == 0, found_first, found_last)
    wanted = jnp.where(found == 1, (chosen & 3) * STEPS + step1, -1)
    sel_ref[...] = jnp.where(lane[:, :8] == wanted, 1.0, 0.0).astype(BF)
    mine = routes_ref[pl.ds(me, 1), :]
    here = mine == group_of_row
    first_link = jnp.min(jnp.where(here, lane, 1000), axis=1, keepdims=True)
    last_link = jnp.max(jnp.where(here, lane, -1), axis=1, keepdims=True)
    first_image = jnp.where(first_link < 1000, first_link >> 3, -1)
    last_image = jnp.where(last_link > first_link, last_link >> 3, -1)
    image_ref[...] = jnp.where(slot1 == 0, first_image, last_image)


def kv_kernel(place_ref, x0, x1, k0, v0, k1, v1, low_ref, high_ref, ahead_ref, behind_ref, own_ref):
    total = dot(x0[...], jnp.concatenate((k0[...], v0[...]), axis=1))
    total = total + dot(x1[...], jnp.concatenate((k1[...], v1[...]), axis=1))
    total = total.astype(BF)
    half = low_ref.shape[0]
    step = pl.program_id(0)

    @pl.when(step == 0)
    def _():
        low_ref[...] = total[:half]
        high_ref[...] = total[half:]

    @pl.when(step == 1)
    def _():
        ahead_ref[...] = total

    @pl.when(step == 2)
    def _():
        behind_ref[...] = total

    @pl.when(step == 3)
    def _():
        own_ref[...] = total


def kv_project(place, vision, k_weight, v_weight):
    rows, depth = vision.shape
    chips = 4

    def head(d, place_ref):
        ahead = jnp.where(d == 0, 2, jnp.where(d == 1, 1, jnp.where(d == 2, 3, 0)))
        return 0, lax.rem(place_ref[0] + ahead, chips) * 2 + place_ref[1]

    states = pl.BlockSpec((rows, depth), lambda d, p: (0, 0))
    weights = pl.BlockSpec((depth, HEAD), head)
    sizes = [rows // 2, rows // 2, rows, rows, rows]
    return pl.pallas_call(
        kv_kernel,
        grid_spec=pltpu.PrefetchScalarGridSpec(
            num_scalar_prefetch=1,
            grid=(chips,),
            in_specs=[states] * 2 + [weights] * 4,
            out_specs=[pl.BlockSpec((n, 2 * HEAD), lambda d, p: (0, 0)) for n in sizes],
        ),
        out_shape=[jax.ShapeDtypeStruct((n, 2 * HEAD), BF) for n in sizes],
        compiler_params=params(LARGE_VMEM_BYTES),
    )(
        place,
        vision,
        shift(vision, "c", 1),
        k_weight,
        v_weight,
        shift(k_weight, "c", 1),
        shift(v_weight, "c", 1),
    )


def kv_merge_kernel(ahead_ref, behind_ref, low_ref, high_ref, forward_ref, backward_ref):
    half = low_ref.shape[0]
    forward_ref[:half] = (ahead_ref[:half].astype(F32) + low_ref[...].astype(F32)).astype(BF)
    forward_ref[half:] = ahead_ref[half:]
    backward_ref[:half] = behind_ref[:half]
    backward_ref[half:] = (behind_ref[half:].astype(F32) + high_ref[...].astype(F32)).astype(BF)


def half_of(shape):
    return (lax.broadcasted_iota(jnp.int32, shape, 0) >> 2) & 1


def query_kernel(parts_ref, sel_ref, gain_ref, out_ref):
    total = jnp.sum(parts_ref[...].astype(F32), axis=0)
    gain = gain_ref[...]
    sel = sel_ref[...]
    heads = total.shape[1] // HEAD // 2
    upper = half_of((sel.shape[0], HEAD)) == 1

    def chosen(h):
        v = total[:, h * HEAD : (h + 1) * HEAD]
        scale = lax.rsqrt(jnp.mean(v * v, axis=1, keepdims=True) + EPS)
        return dot(sel, (v * scale * gain).astype(BF))

    for h in range(heads):
        out_ref[:, h * HEAD : (h + 1) * HEAD] = jnp.where(upper, chosen(heads + h), chosen(h)).astype(BF)


def attention_kernel(me_ref, tiles_ref, own_ref, left_ref, right_ref, gain_ref, q_ref, image_ref, out_ref):
    me = me_ref[0]
    total = own_ref[...].astype(F32) + left_ref[...].astype(F32) + right_ref[...].astype(F32)
    k = total[:, :HEAD]
    scale = lax.rsqrt(jnp.mean(k * k, axis=1, keepdims=True) + EPS)
    k = (k * scale * gain_ref[...]).astype(BF)
    v = total[:, HEAD:].astype(BF)
    rows, keys = q_ref.shape[0], k.shape[0]
    tile = lax.broadcasted_iota(jnp.int32, (1, keys), 1) >> 6
    owner = jnp.zeros((1, keys), jnp.int32)
    end = jnp.int32(0)
    for j in range(4):
        end = end + tiles_ref[me, j]
        owner = owner + (tile >= end).astype(jnp.int32)
    allowed = owner == image_ref[...]
    lane = lax.broadcasted_iota(jnp.int32, (rows, HEAD), 1)
    sums = jnp.zeros((rows, HEAD), F32)
    heads = q_ref.shape[1] // HEAD
    for h in range(heads):
        span = slice(h * HEAD, (h + 1) * HEAD)
        score = lax.dot_general(
            q_ref[:, span], k, (((1,), (1,)), ((), ())), preferred_element_type=F32
        )
        weight = jnp.where(allowed, jnp.exp(score * (1.0 / math.sqrt(HEAD))), 0.0)
        den = jnp.sum(weight, axis=1, keepdims=True)
        high = den.astype(BF).astype(F32)
        sums = sums + jnp.where(lane == h, high, 0.0) + jnp.where(lane == heads + h, den - high, 0.0)
        out_ref[:, span] = dot(weight.astype(BF), v).astype(BF)
    out_ref[:, heads * HEAD :] = sums.astype(BF)


def combine_kernel(parts_ref, sel_ref, out_ref):
    sel = sel_ref[...].astype(F32)
    parts = parts_ref[...]
    heads = out_ref.shape[2] // HEAD // 2
    for part in range(2):
        mine = jnp.where(half_of(sel.shape) == part, sel, 0.0).astype(BF)
        total = lax.dot_general(mine, parts, (((0,), (0,)), ((), ())), preferred_element_type=F32)
        sums = total[:, heads * HEAD :]
        for h in range(heads):
            den = sums[:, h : h + 1] + sums[:, heads + h : heads + h + 1]
            mixed = total[:, h * HEAD : (h + 1) * HEAD] / jnp.where(den > 0.0, den, 1.0)
            mixed = jnp.broadcast_to(mixed.astype(BF)[None], (out_ref.shape[0],) + mixed.shape)
            at = (part * heads + h) * HEAD
            out_ref[:, :, at : at + HEAD] = mixed


def core_rows(place_ref, rows):
    return (
        pl.ds(pl.multiple_of(place_ref[1] * rows, rows), rows),
        pl.ds(pl.multiple_of((1 - place_ref[1]) * rows, rows), rows),
    )


def gate_up_kernel(m0, m1, m2, m3, w0, w1, gate2, up2, w3, out_ref):
    units = gate2.shape[1]
    step = pl.program_id(0)

    def product(w2):
        total = dot(m0[...], w0[...]) + dot(m1[...], w1[...])
        return (total + dot(m2[...], w2[...]) + dot(m3[...], w3[...])).astype(BF)

    @pl.when(step == 0)
    def _():
        out_ref[:, :units] = product(gate2)

    @pl.when(step == 1)
    def _():
        out_ref[:, units : 2 * units] = product(up2)
        square = jnp.zeros((m0.shape[0], 1), F32)
        for m in (m0, m1, m2, m3):
            value = m[...].astype(F32)
            square = square + jnp.sum(value * value, axis=1, keepdims=True)
        high = square.astype(BF).astype(F32)
        lane = lax.broadcasted_iota(jnp.int32, (m0.shape[0], HEAD), 1)
        extra = jnp.where(lane == 0, high, jnp.where(lane == 1, square - high, 0.0))
        out_ref[:, 2 * units :] = extra.astype(BF)


def down_kernel(place_ref, a_ref, d0, d1, low2, high2, d3, mine_ref, theirs_ref):
    active = a_ref[...]
    half = low2.shape[0]
    rows = mine_ref.shape[1]

    def store(d, total, keep_ref):
        keep_ref[d] = total
        theirs_ref[d] = keep_ref[d, core_rows(place_ref, rows)[1], :].astype(BF)
        mine_ref[d] = keep_ref[d, core_rows(place_ref, rows)[0], :]

    def run(keep_ref):
        store(0, dot(active, d0[...]), keep_ref)
        store(1, dot(active, d1[...]), keep_ref)
        store(2, dot(active[:, :half], low2[...]) + dot(active[:, half:], high2[...]), keep_ref)
        store(3, dot(active, d3[...]), keep_ref)

    pl.run_scoped(run, pltpu.VMEM((4,) + active.shape[:1] + (d0.shape[1],), F32))


def pair_kernel(mine_ref, theirs_ref, own_ref, behind_ref, across_ref, ahead_ref):
    own_ref[...] = mine_ref[0] + theirs_ref[0].astype(F32)
    behind_ref[...] = (mine_ref[1] + theirs_ref[1].astype(F32)).astype(BF)
    across_ref[...] = (mine_ref[2] + theirs_ref[2].astype(F32)).astype(BF)
    ahead_ref[...] = (mine_ref[3] + theirs_ref[3].astype(F32)).astype(BF)


def active_kernel(full_width, parts_ref, out_ref):
    total = jnp.sum(parts_ref[...].astype(F32), axis=0)
    units = out_ref.shape[2]
    square = total[:, 2 * units : 2 * units + 1] + total[:, 2 * units + 1 : 2 * units + 2]
    scale = lax.rsqrt(square * (1.0 / full_width) + EPS)
    gate = total[:, :units] * scale
    up = total[:, units : 2 * units] * scale
    active = (gate / (1.0 + jnp.exp(-gate)) * up).astype(BF)
    out_ref[...] = jnp.broadcast_to(active[None], out_ref.shape)


def shift(value, axis, by):
    n = lax.axis_size(axis)
    return lax.ppermute(value, axis, [(i, (i + by) % n) for i in range(n)])


def after(value, *others):
    return lax.optimization_barrier((value,) + others)[0]


def exchange(value, axis):
    n = lax.axis_size(axis)
    out = lax.all_to_all(value, axis, 0, 0, tiled=True)
    return out.reshape((n, value.shape[0] // n) + value.shape[1:])


def chip_sum(part):
    part = part.astype(BF)
    ahead, behind, across = shift(part, "x", 1), shift(part, "x", -1), shift(part, "x", 2)
    return (part.astype(F32) + across.astype(F32)) + (ahead.astype(F32) + behind.astype(F32))


def shards(
    hidden,
    vision,
    attn_gain,
    q_weight,
    k_weight,
    v_weight,
    q_gain,
    k_gain,
    o_weight,
    gate_logits,
    mlp_gain,
    gate_weight,
    up_weight,
    down_weight,
    image_tiles,
    image_groups,
    image_requests,
):
    groups = lax.axis_size("z") * lax.axis_size("y")
    me = (lax.axis_index("z") * lax.axis_size("y") + lax.axis_index("y")).astype(jnp.int32).reshape(1)
    place = jnp.stack((lax.axis_index("x"), lax.axis_index("c"))).astype(jnp.int32)
    all_rows, width_part = hidden.shape
    own_rows = all_rows // groups
    full_width = width_part * groups
    local_heads = q_weight.shape[1]
    hidden_part = gate_weight.shape[1]
    slot_rows = groups * 2 * SLOTS * STEPS
    key_rows = vision.shape[0]

    sel, row_image = pl.pallas_call(
        route_kernel,
        in_specs=[smem(), vmem(), vmem()],
        out_specs=[vmem(), vmem()],
        out_shape=[
            jax.ShapeDtypeStruct((slot_rows, own_rows), BF),
            jax.ShapeDtypeStruct((slot_rows, 1), jnp.int32),
        ],
        compiler_params=params(),
    )(me, image_groups.reshape(groups, -1), image_requests.reshape(groups, -1))

    hidden = after(hidden, place)
    hidden_f = hidden.astype(F32)
    normed = (hidden_f * attn_gain).astype(BF)
    q_part = dot(normed, q_weight).astype(BF)
    q_parts = exchange(q_part, GROUP)

    low, high, ahead, behind, own = kv_project(place, vision, k_weight, v_weight)
    q_parts = after(q_parts, own)
    forward, backward = pl.pallas_call(
        kv_merge_kernel,
        in_specs=[vmem()] * 4,
        out_specs=[vmem()] * 2,
        out_shape=[jax.ShapeDtypeStruct(ahead.shape, BF)] * 2,
        compiler_params=params(LARGE_VMEM_BYTES),
    )(ahead, behind, shift(low, "x", 1), shift(high, "x", -1))
    kv_left = shift(forward, "x", 1)
    kv_right = shift(backward, "x", -1)

    chips_y = lax.axis_size("y")
    units = hidden_part // chips_y
    half = units // 2
    gain = mlp_gain[:, None]

    def columns(weight, d):
        at = lax.rem(lax.axis_index("y") + d, chips_y) * units
        return lax.dynamic_slice_in_dim(weight, at, units, 1).astype(F32)

    def wide(*parts):
        return (jnp.concatenate(parts, axis=1) * gain).astype(BF)

    queries = pl.pallas_call(
        query_kernel,
        in_specs=[vmem()] * 3,
        out_specs=vmem(),
        out_shape=jax.ShapeDtypeStruct((slot_rows, local_heads // 2), BF),
        compiler_params=params(),
    )(q_parts, sel, q_gain.reshape(1, HEAD))
    queries = after(queries, forward, backward)
    later_gate, later_up = lax.optimization_barrier((gate_weight, up_weight, queries))[:2]
    wide_0 = wide(columns(later_gate, 0), columns(later_up, 0))
    wide_1 = shift(wide(columns(later_gate, 1), columns(later_up, 1)), "y", 1)
    wide_3 = shift(wide(columns(later_gate, 3), columns(later_up, 3)), "y", -1)
    queries = lax.all_to_all(queries, GROUP, 0, 0, tiled=True)

    mixed = pl.pallas_call(
        attention_kernel,
        in_specs=[smem(), smem()] + [vmem()] * 6,
        out_specs=vmem(),
        out_shape=jax.ShapeDtypeStruct((slot_rows, local_heads // 2 + HEAD), BF),
        compiler_params=params(),
    )(me, image_tiles, own, kv_left, kv_right, k_gain.reshape(1, HEAD), queries, row_image)
    gate_weight, up_weight, down_weight = lax.optimization_barrier((gate_weight, up_weight, down_weight, mixed))[:3]
    gate_2, up_2 = wide(columns(gate_weight, 2)), wide(columns(up_weight, 2))

    def rows(d, start, size):
        at = lax.rem(lax.axis_index("y") + d, chips_y) * units + start
        return lax.dynamic_slice_in_dim(down_weight, at, size, 0)

    down_0, down_1, down_3 = rows(0, 0, units), rows(1, 0, units), rows(3, 0, units)
    down_2 = rows(2, 0, half), rows(2, half, half)
    mixed = lax.all_to_all(mixed, GROUP, 0, 0, tiled=True)
    mixed = after(mixed, gate_2, up_2, down_1, down_3, *down_2)
    gate_2, up_2 = shift(gate_2, "y", 1), shift(up_2, "y", -1)

    attended = pl.pallas_call(
        combine_kernel,
        in_specs=[vmem()] * 2,
        out_specs=vmem(),
        out_shape=jax.ShapeDtypeStruct((groups, own_rows, local_heads), BF),
        compiler_params=params(),
    )(mixed, sel)
    attended = after(attended, wide_1, wide_3)
    attended = lax.all_to_all(attended, GROUP, 0, 0, tiled=True).reshape(all_rows, local_heads)
    half_rows = all_rows // 2
    first_row = lax.axis_index("c") * half_rows
    part = dot(attended, o_weight).astype(BF)
    pair = (part.astype(F32) + shift(part, "c", 1).astype(F32)).astype(BF)
    attn_sum = chip_sum(after(pair, gate_2, up_2))
    gate_2, up_2 = shift(gate_2, "y", 1), shift(up_2, "y", -1)
    middle = (hidden_f + jnp.tanh(gate_logits[0]) * attn_sum).astype(BF)
    middles = [middle] + [shift(middle, "y", d) for d in (1, 2, 3)]
    middle_f = lax.dynamic_slice_in_dim(middle, first_row, half_rows, 0).astype(F32)
    block = pl.BlockSpec((all_rows, width_part), lambda i: (0, 0))
    direct = pl.BlockSpec((width_part, units), lambda i: (0, i))
    passed = pl.BlockSpec((width_part, units), lambda i: (0, 0))
    gate_up = pl.pallas_call(
        gate_up_kernel,
        grid=(2,),
        in_specs=[block] * 4 + [direct] * 2 + [passed] * 2 + [direct],
        out_specs=pl.BlockSpec((all_rows, 2 * units + HEAD), lambda i: (0, 0)),
        out_shape=jax.ShapeDtypeStruct((all_rows, 2 * units + HEAD), BF),
        compiler_params=params(LARGE_VMEM_BYTES),
    )(*middles, wide_0, wide_1, gate_2, up_2, wide_3)
    down_1, down_3, *down_2 = lax.optimization_barrier((down_1, down_3, *down_2, gate_up))[:4]
    down_1, down_3 = shift(down_1, "y", 1), shift(down_3, "y", -1)
    down_2 = shift(down_2[0], "y", 1), shift(down_2[1], "y", -1)
    parts = after(exchange(gate_up, "z"), down_1, down_3, *down_2)
    down_2 = shift(down_2[0], "y", 1), shift(down_2[1], "y", -1)
    active = pl.pallas_call(
        functools.partial(active_kernel, full_width),
        in_specs=[vmem()],
        out_specs=vmem(),
        out_shape=jax.ShapeDtypeStruct(parts.shape[:2] + (units,), BF),
        compiler_params=params(),
    )(parts)
    active = lax.all_to_all(active, "z", 0, 0, tiled=True).reshape(all_rows, units)
    mine, theirs = pl.pallas_call(
        down_kernel,
        in_specs=[smem()] + [vmem()] * 6,
        out_specs=[vmem()] * 2,
        out_shape=[
            jax.ShapeDtypeStruct((4, half_rows, width_part), F32),
            jax.ShapeDtypeStruct((4, half_rows, width_part), BF),
        ],
        compiler_params=params(),
    )(place, active, down_0, down_1, *down_2, down_3)
    own_down, behind, across, ahead = pl.pallas_call(
        pair_kernel,
        in_specs=[vmem()] * 2,
        out_specs=[vmem()] * 4,
        out_shape=[jax.ShapeDtypeStruct((half_rows, width_part), F32)]
        + [jax.ShapeDtypeStruct((half_rows, width_part), BF)] * 3,
        compiler_params=params(),
    )(mine, shift(theirs, "c", 1))
    across, behind, ahead = shift(across, "y", 2), shift(behind, "y", -1), shift(ahead, "y", 1)
    down_sum = chip_sum(own_down + across.astype(F32) + behind.astype(F32) + ahead.astype(F32))
    row_request = (jnp.arange(half_rows, dtype=jnp.int32) + first_row) // STEPS
    request_ids = (image_groups * (own_rows // STEPS) + image_requests).reshape(-1)
    has_image = jnp.any(row_request[:, None] == request_ids[None, :], axis=1).astype(F32)
    output = (middle_f + jnp.tanh(gate_logits[1]) * has_image[:, None] * down_sum).astype(BF)
    swapped = shift(output, "c", 1)
    lower = lax.axis_index("c") == 0
    return jnp.concatenate((jnp.where(lower, output, swapped), jnp.where(lower, swapped, output)), axis=0)


def solution(mesh):
    fine = Mesh(mesh.devices.reshape(8, 4, 4, 2), GROUP + TENSOR)
    in_specs = (
        P(None, GROUP),
        P(GROUP, TENSOR),
        P(GROUP),
        P(GROUP, TENSOR),
        P(TENSOR, None),
        P(TENSOR, None),
        P(),
        P(),
        P(TENSOR, GROUP),
        P(),
        P(GROUP),
        P(GROUP, TENSOR),
        P(GROUP, TENSOR),
        P(TENSOR, GROUP),
        P(),
        P(),
        P(),
    )
    return jax.shard_map(shards, mesh=fine, in_specs=in_specs, out_specs=P(None, GROUP), check_vma=False)
```
